32 devices in a mesh: ep: 16 (over z, y, core), kv: 2 (over x).
Axes of the slice: x: 2, y: 2, z: 4, core: 2. Of those that a mesh axis runs over, the one named last changes fastest.
Arguments:
- queries: bfloat16 [32, 2048], P('ep'), may hold values from -10 to 10
- key_pool: bfloat16 [192, 128, 2048], P(('ep', 'kv')), may hold values from -4 to 4
- value_pool: bfloat16 [192, 128, 2048], P(('ep', 'kv')), may hold values from -15 to 15
- page_table: int32 [32, 2, 3], P('ep', 'kv'), may hold values from 0 to 5, as said below
- lengths: int32 [32], P('ep'), may hold values from 2 to 768, as said below
- prefill_attn: bfloat16 [2016, 2048], P('ep'), may hold values from -3 to 3
- residual: bfloat16 [2048, 2048], P('ep', 'kv'), may hold values from -64 to 64
- w_out: bfloat16 [2048, 2048], P(None, 'kv'), may hold values from -0.125 to 0.125
- norm_gain: float32 [2048], P('kv'), may hold values from 0.1 to 1.9
- router: bfloat16 [2048, 16], P('kv'), may hold values from -0.125 to 0.125
- w_gate: bfloat16 [16, 2048, 1024], P('ep', None, 'kv'), may hold values from -0.125 to 0.125
- w_up: bfloat16 [16, 2048, 1024], P('ep', None, 'kv'), may hold values from -0.125 to 0.125
- w_down: bfloat16 [16, 1024, 2048], P('ep', 'kv'), may hold values from -0.375 to 0.375
- final_gain: float32 [2048], P('kv'), may hold values from 0.1 to 1.9
- routes: int32 [2048, 8], P('ep'), may hold values from 0 to 15, all different within a row; in each aligned block of 128 rows (0 to 127, 128 to 255, ...) at most 128 rows name the same one
Outputs:
- output: bfloat16 [2048, 2048], P('ep', 'kv')
The draws below stay inside these ranges and needn't reach their ends.
Inputs may be any that keep to these rules, and one draw needn't show every extreme that they name: `page_table`: the 2 x 3 entries of one group of requests at one holder are a permutation of 0 to 5. `lengths`: some request has length exactly 768. `routes`: each row names 8 different experts; in the rows of one index of ep (aligned blocks of 128 rows) no expert is named more than 128 times, a bound that some block reaches.
All inputs are finite; a program needn't handle non-finite values.
Results may differ from the reference program's by a relative error of at most 0.009.
Values may be sent and summed in bfloat16 or wider, within the bound.
No kernel may reach another device: no remote copies, remote signals or barrier semaphores. Data moves between devices by JAX's collectives and lax.ppermute only.
A program may use at most 128 MiB of HBM per device.

```python
import math
import jax
import jax.numpy as jnp
import numpy as np
from jax import lax

D = 2048
HEADS = 16
HEAD_DIM = 128
FF = 1024
TOP = 8
PAGE = 128
DEC_DEV = 2
PPR = 3
PRE_DEV = 126
EXPERTS = 16
ROWS = 128
CAP = 128
POOL = 6
MAXLEN = 768
REQUESTS = 32
PREFILL = 2016
TOKENS = 2048
PAGES = 192
N_EP = 16
N_KV = 2


def draw_queries(key, part):
    result = jax.random.truncated_normal(jax.random.fold_in(key, 1), -4.0, 4.0, (REQUESTS, HEADS, HEAD_DIM), jnp.float32)
    return result.reshape(REQUESTS, D).astype(jnp.bfloat16)


def draw_key_pool(key, part):
    result = jax.random.truncated_normal(jax.random.fold_in(key, 3), -4.0, 4.0, (PAGES, PAGE, HEADS, HEAD_DIM), jnp.float32)
    return result.reshape(PAGES, PAGE, D).astype(jnp.bfloat16)


def draw_residual(key, part):
    column_pos = jnp.arange(D, dtype=jnp.float32) / (D - 1)
    spread = jnp.exp(math.log(10.0) * jax.random.uniform(jax.random.fold_in(key, 3), (D,), jnp.float32))
    noise = jax.random.truncated_normal(jax.random.fold_in(key, 4), -4.0, 4.0, (TOKENS, D), jnp.float32)
    rising = 0.1 * jnp.exp(math.log(3.0) * column_pos)
    row_scale = jnp.exp(jax.random.uniform(jax.random.fold_in(key, 5), (TOKENS, 1), jnp.float32, math.log(0.5), math.log(2.0)))
    return (noise * rising[None, :] * spread[None, :] * row_scale).astype(jnp.bfloat16)


def draw_page_table(key, part):
    device_keys = jax.random.split(jax.random.fold_in(key, 7), N_EP * N_KV)
    orders = jax.vmap(lambda device_key: jax.random.permutation(device_key, POOL))(device_keys)
    orders = orders.reshape(N_EP, N_KV, DEC_DEV, PPR).transpose(0, 2, 1, 3)
    return orders.reshape(REQUESTS, N_KV, PPR).astype(jnp.int32)


def draw_lengths(key, part):
    trials = jax.random.randint(jax.random.fold_in(key, 8), (3, REQUESTS), 2, MAXLEN + 1, jnp.int32)
    shortest = jnp.min(trials, axis=0)
    longest_at = jax.random.randint(jax.random.fold_in(key, 9), (), 0, REQUESTS, jnp.int32)
    return shortest.at[longest_at].set(MAXLEN).astype(jnp.int32)


def levels(rng, shape, shards, least, high):
    factor_of = 1.0
    for dim, shards_of in shards:
        heights = jax.random.uniform(jax.random.fold_in(jax.random.fold_in(rng, 6), dim), (shards_of,), jnp.float32, least / len(shards), high / len(shards))
        factor_of = factor_of * jnp.repeat(jnp.exp(heights), shape[dim] // shards_of).reshape((-1,) + (1,) * (len(shape) - 1 - dim))
    return factor_of


def assign_block(own_key, own, number, rows, count, top, most, skew):
    order = jax.random.permutation(own_key, count)
    heavy_load, common = portions_of(count, rows * top, most, skew, True), portions_of(count, rows * top, most, skew, False)
    places = jnp.arange(count)

    def named(tallies, rotation):
        used = int((tallies > 0).sum())
        fixed = max(1, used // 4)
        passed = fixed + (places - fixed + rotation * (used - fixed)) % max(1, count - fixed)
        return jnp.zeros((count,), jnp.int32).at[order[jnp.where(places < fixed, places, passed)]].set(jnp.asarray(tallies, jnp.int32))

    tallies = jnp.where(number % 4 == 0, named(heavy_load, number // 4), named(common, number - number // 4 - 1))
    mixed = jax.random.permutation(jax.random.fold_in(own, 3), count)
    source_of, sink = mixed[0:count // 2 * 2:2], mixed[1:count // 2 * 2:2]
    slack = jnp.minimum(tallies[source_of] - 1, most - tallies[sink]) // 2
    slack = jnp.where((source_of == order[0]) | (sink == order[0]) | (tallies[sink] == 0), 0, jnp.maximum(slack, 0))
    passed = jax.random.randint(jax.random.fold_in(own, 4), (count // 2,), 0, 1 << 20) % (slack + 1)
    tallies = tallies.at[source_of].add(-passed).at[sink].add(passed)
    labels = jnp.searchsorted(jnp.cumsum(tallies), jnp.arange(rows * top), side="right").astype(jnp.int32)
    grid = labels.reshape(top, rows).T
    grid = grid[jax.random.permutation(jax.random.fold_in(own, 1), rows)]
    rotation = jax.random.randint(jax.random.fold_in(own, 2), (rows, 1), 0, top)
    return jnp.take_along_axis(grid, (jnp.arange(top)[None, :] + rotation) % top, axis=1)


def portions_of(count, total, limit, lean, full):
    loads = [(1 << 20) // math.isqrt(grade ** lean) + 1 for grade in range(1, count + 1)]
    largest = limit if full else min(limit, max(-(-total // count), total * loads[0] // sum(loads)))
    least = 1 if total - largest >= count - 1 else 0
    holding, surplus = [largest] + [least] * (count - 1), total - largest - least * (count - 1)
    while surplus > 0:
        candidates = [i for i in range(1, count) if holding[i] < largest] or [i for i in range(1, count) if holding[i] < limit]
        mass, budget = sum([loads[i] for i in candidates]), surplus
        for i in candidates:
            addition = min(limit - holding[i], max(1, budget * loads[i] // mass), surplus)
            holding[i] = holding[i] + addition
            surplus = surplus - addition
    return np.array(holding)


def gaussian(rng, dims, width, limit, shards=(), kind=jnp.bfloat16):
    entries = width * jax.random.normal(rng, dims, jnp.float32)
    if shards:
        entries = entries * levels(rng, dims, shards, -0.22, 0.18)
    return jnp.clip(entries, -limit, limit).astype(kind)


def setup_inputs(seed: int = 0) -> dict:
    key_of = jax.random.split(jax.random.key(seed), 16)
    queries = draw_queries(jax.random.fold_in(key_of[15], 71), 0)
    key_pool = draw_key_pool(jax.random.fold_in(key_of[15], 71), 0)
    value_pool = gaussian(key_of[2], (PAGES, PAGE, D), 3.0, 15.0, ((0, 32),))
    page_table = draw_page_table(jax.random.fold_in(key_of[15], 71), 0)
    lengths = draw_lengths(jax.random.fold_in(key_of[15], 71), 0)
    prefill_attn = gaussian(key_of[5], (PREFILL, D), 0.5, 3.0, ((0, 16),))
    residual = draw_residual(jax.random.fold_in(key_of[15], 71), 0)
    w_out = gaussian(key_of[7], (D, D), D ** -0.5, 0.125, ((1, 2),))
    norm_gain = jnp.clip(1.0 + 0.18 * jax.random.normal(key_of[8], (D,), jnp.float32), 0.1, 1.9)
    router = gaussian(key_of[9], (D, EXPERTS), D ** -0.5, 0.125, ((0, 2),))
    w_gate = gaussian(key_of[10], (EXPERTS, D, FF), D ** -0.5, 0.125, ((0, 16), (2, 2)))
    w_up = gaussian(key_of[11], (EXPERTS, D, FF), D ** -0.5, 0.125, ((0, 16), (2, 2)))
    w_down = gaussian(key_of[12], (EXPERTS, FF, D), (FF // 4) ** -0.5, 0.375, ((0, 16), (1, 2)))
    final_gain = jnp.clip(1.0 + 0.18 * jax.random.normal(key_of[13], (D,), jnp.float32), 0.1, 1.9)
    routes_keys = jax.random.split(jax.random.fold_in(key_of[14], 1), TOKENS // ROWS)
    routes_turns = jax.random.permutation(jax.random.fold_in(key_of[14], 3), TOKENS // ROWS)
    routes = jax.vmap(lambda own, number: assign_block(jax.random.fold_in(key_of[14], 2), own, number, ROWS, EXPERTS, TOP, CAP, 2))(routes_keys, routes_turns).reshape((TOKENS, TOP))
    return dict(queries=queries, key_pool=key_pool, value_pool=value_pool, page_table=page_table, lengths=lengths, prefill_attn=prefill_attn, residual=residual, w_out=w_out, norm_gain=norm_gain, router=router, w_gate=w_gate, w_up=w_up, w_down=w_down, final_gain=final_gain, routes=routes)


epsilon = 1e-06

def decode_attention(queries, key_pool, value_pool, page_table, lengths):
    total_pages = PPR * N_KV
    page_ids = jnp.arange(total_pages, dtype=jnp.int32)
    holder_of = page_ids % N_KV
    column = page_ids // N_KV

    def one_request(request):
        group_index = request // DEC_DEV
        local_page = page_table[request][holder_of, column]
        pool_index = (group_index * N_KV + holder_of) * POOL + local_page
        key_rows = key_pool[pool_index].reshape(total_pages * PAGE, HEADS, HEAD_DIM).astype(jnp.float32)
        value_rows = value_pool[pool_index].reshape(total_pages * PAGE, HEADS, HEAD_DIM).astype(jnp.float32)
        query_heads = queries[request].reshape(HEADS, HEAD_DIM).astype(jnp.float32)
        scores = jnp.einsum('hd,thd->ht', query_heads, key_rows, precision=lax.Precision.HIGHEST) / math.sqrt(HEAD_DIM)
        visible = jnp.arange(total_pages * PAGE, dtype=jnp.int32) < lengths[request]
        masked = jnp.where(visible[None, :], scores, -jnp.inf)
        top_score = lax.optimization_barrier(jnp.max(masked, axis=1, keepdims=True))
        weights = jnp.where(visible[None, :], jnp.exp(masked - top_score), 0.0)
        weights = weights / lax.optimization_barrier(jnp.sum(weights, axis=1, keepdims=True))
        result = jnp.einsum('ht,thd->hd', weights, value_rows, precision=lax.Precision.HIGHEST)
        return result.reshape(D).astype(jnp.bfloat16)
    return lax.map(one_request, jnp.arange(REQUESTS, dtype=jnp.int32))

def reference(queries, key_pool, value_pool, page_table, lengths, prefill_attn, residual, w_out, norm_gain, router, w_gate, w_up, w_down, final_gain, routes):
    decode_attn = decode_attention(queries, key_pool, value_pool, page_table, lengths)
    attn_rows = jnp.concatenate([prefill_attn.reshape(N_EP, PRE_DEV, D), decode_attn.reshape(N_EP, DEC_DEV, D)], axis=1).reshape(TOKENS, D)
    hidden_state = residual.astype(jnp.float32) + jnp.dot(attn_rows, w_out, preferred_element_type=jnp.float32)
    inv_first = lax.rsqrt(lax.optimization_barrier(jnp.mean(hidden_state * hidden_state, axis=1)) + epsilon)
    scaled = (hidden_state * norm_gain).astype(jnp.bfloat16)
    logits = jnp.dot(scaled, router, preferred_element_type=jnp.float32) * inv_first[:, None]
    normed = (hidden_state * norm_gain * inv_first[:, None]).astype(jnp.bfloat16)
    chosen = jnp.take_along_axis(logits, routes, axis=1)
    raised = jnp.exp(chosen)
    gate_weights = raised / lax.optimization_barrier(jnp.sum(raised, axis=1, keepdims=True))
    pair_count = ROWS * TOP
    grouped = routes.reshape(N_EP, pair_count)
    one_hot = (grouped[:, :, None] == jnp.arange(EXPERTS, dtype=jnp.int32)[None, None, :]).astype(jnp.int32)
    earlier = jnp.cumsum(one_hot, axis=1) - one_hot
    slot_index = lax.optimization_barrier(jnp.sum(earlier * one_hot, axis=2))
    group_ids = jnp.arange(N_EP, dtype=jnp.int32)[:, None]
    position = group_ids * CAP + slot_index
    row_ids = group_ids * ROWS + jnp.arange(pair_count, dtype=jnp.int32)[None, :] // TOP
    sources = jnp.zeros((EXPERTS, N_EP * CAP), jnp.int32).at[grouped, position].set(row_ids)
    shares = jnp.zeros((EXPERTS, N_EP * CAP), jnp.float32).at[grouped, position].set(gate_weights.reshape(N_EP, pair_count))
    group_width = FF // N_KV

    def expert_step(running, inputs):
        gate_e, up_e, down_e, rows_from, share_e = inputs
        rows_in = normed[rows_from]
        gate_proj = jnp.dot(rows_in, gate_e, preferred_element_type=jnp.float32)
        up_proj = jnp.dot(rows_in, up_e, preferred_element_type=jnp.float32)
        activation = (jax.nn.silu(gate_proj) * up_proj).astype(jnp.bfloat16)
        summed = jnp.zeros((N_EP * CAP, D), jnp.float32)
        for kv_block in range(N_KV):
            partial_value = jnp.dot(activation[:, kv_block * group_width:(kv_block + 1) * group_width], down_e[kv_block * group_width:(kv_block + 1) * group_width], preferred_element_type=jnp.float32)
            rounded = lax.optimization_barrier(partial_value.astype(jnp.bfloat16))
            summed = summed + rounded.astype(jnp.float32)
        expert_out = summed.astype(jnp.bfloat16)
        return (running.at[rows_from].add(share_e[:, None] * expert_out.astype(jnp.float32)), None)
    mixture, _ = lax.scan(expert_step, jnp.zeros((TOKENS, D), jnp.float32), (w_gate, w_up, w_down, sources, shares))
    combined = hidden_state + mixture
    inv_second = lax.rsqrt(lax.optimization_barrier(jnp.mean(combined * combined, axis=1)) + epsilon)
    return (combined * inv_second[:, None] * final_gain).astype(jnp.bfloat16)
```

```python
import math

import jax
import jax.numpy as jnp
from jax import lax
from jax.sharding import PartitionSpec as P

D = 2048
HEADS = 16
HEAD_DIM = 128
TOP = 8


epsilon = 1e-06
floor_score = -1e30


def per_device(
    queries,
    key_pool,
    value_pool,
    page_table,
    lengths,
    prefill_attn,
    residual,
    w_out,
    norm_gain,
    router,
    w_gate,
    w_up,
    w_down,
    final_gain,
    routes,
):
    holders = lax.axis_size("kv")
    holder = lax.axis_index("kv")
    request_count = queries.shape[0]
    pool_pages = key_pool.shape[0]
    page_rows = key_pool.shape[1]
    pages_each = page_table.shape[2]
    query_heads = queries.reshape(request_count, HEADS, HEAD_DIM)
    page_slots = page_table[:, 0, :]
    picked_keys = key_pool.reshape(pool_pages, page_rows, HEADS, HEAD_DIM)[page_slots]
    picked_values = value_pool.reshape(pool_pages, page_rows, HEADS, HEAD_DIM)[page_slots]
    scores = jnp.einsum(
        "rhd,rjphd->rhjp", query_heads, picked_keys, preferred_element_type=jnp.float32
    ) / math.sqrt(HEAD_DIM)
    page_number = jnp.arange(pages_each, dtype=jnp.int32) * holders + holder
    position = page_number[:, None] * page_rows + jnp.arange(page_rows, dtype=jnp.int32)[None, :]
    visible = position[None, None, :, :] < lengths[:, None, None, None]
    masked = jnp.where(visible, scores, floor_score)
    local_peak = jnp.max(masked, axis=(2, 3))
    weights = jnp.where(visible, jnp.exp(masked - local_peak[:, :, None, None]), 0.0)
    local_mass = jnp.sum(weights, axis=(2, 3))
    local_sum = jnp.einsum(
        "rhjp,rjphd->rhd",
        weights,
        picked_values.astype(jnp.float32),
        precision=lax.Precision.HIGHEST,
    )
    peak_rows, masses, gathered_sums = (
        lax.all_gather(local_peak[None], "kv", axis=0, tiled=True),
        lax.all_gather(local_mass[None], "kv", axis=0, tiled=True),
        lax.all_gather(local_sum[None], "kv", axis=0, tiled=True),
    )
    all_peak = jnp.max(peak_rows, axis=0)
    factors = jnp.exp(peak_rows - all_peak[None])
    all_mass = jnp.sum(masses * factors, axis=0)
    all_sum = jnp.sum(gathered_sums * factors[..., None], axis=0)
    decode_attn = (all_sum / all_mass[..., None]).reshape(request_count, D).astype(jnp.bfloat16)
    attn_rows = jnp.concatenate([prefill_attn, decode_attn], axis=0)
    hidden_state = residual.astype(jnp.float32) + jnp.dot(
        attn_rows, w_out, preferred_element_type=jnp.float32
    )
    scaled = (hidden_state * norm_gain).astype(jnp.bfloat16)
    row_count = residual.shape[0]
    feature_cols = residual.shape[1]
    expert_count = router.shape[1]
    ep_size = lax.axis_size("ep")
    every = lax.all_gather(scaled, ("ep", "kv"), axis=0, tiled=False)
    every = every.reshape(ep_size, holders, row_count, feature_cols)
    square_sum, logit_parts = lax.psum(
        (
            jnp.sum(hidden_state * hidden_state, axis=1),
            jnp.dot(scaled, router, preferred_element_type=jnp.float32),
        ),
        "kv",
    )
    inv_first = lax.rsqrt(square_sum / D + epsilon)
    logits = logit_parts * inv_first[:, None]
    matches = routes[:, :, None] == jnp.arange(expert_count, dtype=jnp.int32)[None, None, :]
    chosen = jnp.sum(jnp.where(matches, logits[:, None, :], 0.0), axis=2)
    raised = jnp.exp(chosen)
    gate_weights = raised / jnp.sum(raised, axis=1, keepdims=True)
    by_expert = jnp.sum(jnp.where(matches, gate_weights[:, :, None], 0.0), axis=1)
    side = jnp.concatenate([by_expert, inv_first[:, None]], axis=1).T
    sides = lax.all_gather(side, "ep", axis=0, tiled=False)
    own = lax.axis_index("ep")
    share = lax.dynamic_index_in_dim(sides, own, axis=1, keepdims=False).reshape(-1, 1)
    scale = sides[:, expert_count].reshape(-1, 1)
    gate_local = w_gate[0].reshape(holders, feature_cols, -1)
    up_local = w_up[0].reshape(holders, feature_cols, -1)
    down_local = w_down[0]
    gate_proj = jnp.einsum("ehrf,hfu->eru", every, gate_local, preferred_element_type=jnp.float32)
    up_proj = jnp.einsum("ehrf,hfu->eru", every, up_local, preferred_element_type=jnp.float32)
    hidden_units = gate_local.shape[2]
    gate_proj = gate_proj.reshape(-1, hidden_units) * scale
    up_proj = up_proj.reshape(-1, hidden_units) * scale
    activation = (jax.nn.silu(gate_proj) * up_proj).astype(jnp.bfloat16)
    partial = jnp.dot(activation, down_local, preferred_element_type=jnp.float32) * share
    partial = partial.astype(jnp.bfloat16).reshape(ep_size, row_count, holders, feature_cols)
    partial = partial.transpose(0, 2, 1, 3).reshape(ep_size * holders, row_count, feature_cols)
    mixture = lax.psum_scatter(partial, ("ep", "kv"), scatter_dimension=0, tiled=True)
    combined = hidden_state + mixture[0].astype(jnp.float32)
    square_two = lax.psum(jnp.sum(combined * combined, axis=1), "kv")
    return (combined * lax.rsqrt(square_two / D + epsilon)[:, None] * final_gain).astype(
        jnp.bfloat16
    )


def solution(mesh):
    placed = (
        P("ep", None),
        P(("ep", "kv"), None, None),
        P(("ep", "kv"), None, None),
        P("ep", "kv", None),
        P("ep"),
        P("ep", None),
        P("ep", "kv"),
        P(None, "kv"),
        P("kv"),
        P("kv", None),
        P("ep", None, "kv"),
        P("ep", None, "kv"),
        P("ep", "kv", None),
        P("kv"),
        P("ep", None),
    )
    return jax.shard_map(
        per_device, mesh=mesh, in_specs=placed, out_specs=P("ep", "kv"), check_vma=False
    )
```

```python
import math

import jax
import jax.numpy as jnp
from jax import lax
from jax.experimental import pallas as pl
from jax.experimental.pallas import tpu as pltpu
from jax.sharding import PartitionSpec as P

D = 2048
HEADS = 16
HEAD_DIM = 128
TOP = 8


epsilon = 1e-06
floor_score = -1e30


def routed(
    queries,
    key_pool,
    value_pool,
    page_table,
    lengths,
    prefill_attn,
    residual,
    w_out,
    norm_gain,
    router,
    w_gate,
    w_up,
    w_down,
    final_gain,
    routes,
):
    holders = lax.axis_size("kv")
    holder = lax.axis_index("kv")
    request_count = queries.shape[0]
    pool_pages = key_pool.shape[0]
    page_rows = key_pool.shape[1]
    pages_each = page_table.shape[2]
    query_heads = queries.reshape(request_count, HEADS, HEAD_DIM)
    page_slots = page_table[:, 0, :]
    picked_keys = key_pool.reshape(pool_pages, page_rows, HEADS, HEAD_DIM)[page_slots]
    picked_values = value_pool.reshape(pool_pages, page_rows, HEADS, HEAD_DIM)[page_slots]
    scores = jnp.einsum(
        "rhd,rjphd->rhjp", query_heads, picked_keys, preferred_element_type=jnp.float32
    ) / math.sqrt(HEAD_DIM)
    page_number = jnp.arange(pages_each, dtype=jnp.int32) * holders + holder
    position = page_number[:, None] * page_rows + jnp.arange(page_rows, dtype=jnp.int32)[None, :]
    visible = position[None, None, :, :] < lengths[:, None, None, None]
    masked = jnp.where(visible, scores, floor_score)
    local_peak = jnp.max(masked, axis=(2, 3))
    weights = jnp.where(visible, jnp.exp(masked - local_peak[:, :, None, None]), 0.0)
    local_mass = jnp.sum(weights, axis=(2, 3))
    local_sum = jnp.einsum(
        "rhjp,rjphd->rhd",
        weights,
        picked_values.astype(jnp.float32),
        precision=lax.Precision.HIGHEST,
    )
    peak_rows, masses, gathered_sums = (
        lax.all_gather(local_peak[None], "kv", axis=0, tiled=True),
        lax.all_gather(local_mass[None], "kv", axis=0, tiled=True),
        lax.all_gather(local_sum[None], "kv", axis=0, tiled=True),
    )
    all_peak = jnp.max(peak_rows, axis=0)
    factors = jnp.exp(peak_rows - all_peak[None])
    all_mass = jnp.sum(masses * factors, axis=0)
    all_sum = jnp.sum(gathered_sums * factors[..., None], axis=0)
    decode_attn = (all_sum / all_mass[..., None]).reshape(request_count, D).astype(jnp.bfloat16)
    attn_rows = jnp.concatenate([prefill_attn, decode_attn], axis=0)
    hidden_state = residual.astype(jnp.float32) + jnp.dot(
        attn_rows, w_out, preferred_element_type=jnp.float32
    )
    scaled = (hidden_state * norm_gain).astype(jnp.bfloat16)
    square_sum, logit_parts = lax.psum(
        (
            jnp.sum(hidden_state * hidden_state, axis=1),
            jnp.dot(scaled, router, preferred_element_type=jnp.float32),
        ),
        "kv",
    )
    inv_first = lax.rsqrt(square_sum / D + epsilon)
    logits = logit_parts * inv_first[:, None]
    normed = (hidden_state * norm_gain * inv_first[:, None]).astype(jnp.bfloat16)
    row_count = residual.shape[0]
    expert_count = router.shape[1]
    capacity = min(row_count, 2 * row_count * TOP // expert_count)
    matches = routes[:, :, None] == jnp.arange(expert_count, dtype=jnp.int32)[None, None, :]
    chosen = jnp.sum(jnp.where(matches, logits[:, None, :], 0.0), axis=2)
    raised = jnp.exp(chosen)
    gate_weights = raised / jnp.sum(raised, axis=1, keepdims=True)
    one_hot = matches.reshape(row_count * TOP, expert_count).astype(jnp.int32)
    earlier = jnp.cumsum(one_hot, axis=0) - one_hot
    slot_index = jnp.sum(earlier * one_hot, axis=1)
    target = routes.reshape(-1) * capacity + slot_index
    source_row = jnp.arange(row_count * TOP, dtype=jnp.int32) // TOP
    filler = jnp.zeros((expert_count * capacity,), jnp.int32).at[target].set(source_row)
    present = jnp.zeros((expert_count * capacity,), jnp.bool_).at[target].set(True)
    gate_local = w_gate[0]
    up_local = w_up[0]
    down_local = w_down[0]
    full_rows = lax.all_gather(normed, "kv", axis=1, tiled=True)
    picked = full_rows[filler]
    arrived = lax.all_to_all(
        jnp.where(present[:, None], picked, jnp.zeros_like(picked)).reshape(
            expert_count, capacity, full_rows.shape[1]
        ),
        "ep",
        split_axis=0,
        concat_axis=0,
        tiled=True,
    )
    inbound = arrived.reshape(-1, arrived.shape[2])
    gate_proj = jnp.dot(inbound, gate_local, preferred_element_type=jnp.float32)
    up_proj = jnp.dot(inbound, up_local, preferred_element_type=jnp.float32)
    activation = (jax.nn.silu(gate_proj) * up_proj).astype(jnp.bfloat16)
    feature_cols = residual.shape[1]
    summed = lax.psum_scatter(
        lax.dot_general(
            down_local, activation, (((0,), (1,)), ((), ())), preferred_element_type=jnp.float32
        ).astype(jnp.bfloat16),
        "kv",
        scatter_dimension=0,
        tiled=True,
    ).astype(jnp.float32)
    expert_out = summed.T.astype(jnp.bfloat16).reshape(
        arrived.shape[0], arrived.shape[1], feature_cols
    )
    returned = lax.all_to_all(expert_out, "ep", split_axis=0, concat_axis=0, tiled=True)
    back_rows = (
        returned.reshape(-1, feature_cols)[target]
        .reshape(row_count, TOP, feature_cols)
        .astype(jnp.float32)
    )
    combined = hidden_state + jnp.sum(back_rows * gate_weights[:, :, None], axis=1)
    square_two = lax.psum(jnp.sum(combined * combined, axis=1), "kv")
    return (combined * lax.rsqrt(square_two / D + epsilon)[:, None] * final_gain).astype(
        jnp.bfloat16
    )


def attend(place_ref, slots_ref, lengths_ref, q_ref, k_ref, v_ref, out_ref, kbuf, vbuf, ksem, vsem):
    requests = q_ref.shape[0]
    pages_each = kbuf.shape[0] // requests
    page_rows = kbuf.shape[1]
    holder = place_ref[0]
    holders = place_ref[1]
    for i in range(requests * pages_each):
        pltpu.make_async_copy(k_ref.at[slots_ref[i]], kbuf.at[i], ksem.at[i]).start()
    for i in range(requests * pages_each):
        pltpu.make_async_copy(v_ref.at[slots_ref[i]], vbuf.at[i], vsem.at[i]).start()
    head_row = lax.broadcasted_iota(jnp.int32, (HEADS, D), 0)
    head_lane = lax.broadcasted_iota(jnp.int32, (HEADS, D), 1) // HEAD_DIM
    own_head = head_row == head_lane
    for r in range(requests):
        q = jnp.where(own_head, q_ref[r : r + 1, :], 0.0).astype(jnp.bfloat16)
        parts, seen = [], []
        for j in range(pages_each):
            i = r * pages_each + j
            pltpu.make_async_copy(k_ref.at[0], kbuf.at[i], ksem.at[i]).wait()
            part = lax.dot_general(
                q, kbuf[i], (((1,), (1,)), ((), ())), preferred_element_type=jnp.float32
            )
            start = (j * holders + holder) * page_rows
            position = start + lax.broadcasted_iota(jnp.int32, (HEADS, page_rows), 1)
            visible = position < lengths_ref[r]
            seen.append(visible)
            parts.append(jnp.where(visible, part / math.sqrt(HEAD_DIM), floor_score))
        peak = parts[0].max(axis=1, keepdims=True)
        for part in parts[1:]:
            peak = jnp.maximum(peak, part.max(axis=1, keepdims=True))
        mass = jnp.zeros((HEADS, 1), jnp.float32)
        total = jnp.zeros((2 * HEADS, D), jnp.float32)
        for j in range(pages_each):
            i = r * pages_each + j
            weight = jnp.where(seen[j], jnp.exp(parts[j] - peak), 0.0)
            mass += weight.sum(axis=1, keepdims=True)
            high = weight.astype(jnp.bfloat16)
            low = (weight - high.astype(jnp.float32)).astype(jnp.bfloat16)
            pltpu.make_async_copy(v_ref.at[0], vbuf.at[i], vsem.at[i]).wait()
            total += jnp.dot(
                jnp.concatenate([high, low], axis=0), vbuf[i], preferred_element_type=jnp.float32
            )
        both = total[:HEADS] + total[HEADS:]
        out_ref[r : r + 1, :] = jnp.sum(jnp.where(own_head, both, 0.0), axis=0, keepdims=True)
        out_ref[requests + r : requests + r + 1, :] = jnp.sum(
            jnp.where(own_head, peak, 0.0), axis=0, keepdims=True
        )
        out_ref[2 * requests + r : 2 * requests + r + 1, :] = jnp.sum(
            jnp.where(own_head, mass, 0.0), axis=0, keepdims=True
        )


def local_attention(queries, key_pool, value_pool, page_table, lengths):
    requests = queries.shape[0]
    used = requests * page_table.shape[2]
    page = key_pool.shape[1:]
    place = jnp.stack([lax.axis_index("kv"), jnp.int32(lax.axis_size("kv"))]).astype(jnp.int32)
    smem = pl.BlockSpec(memory_space=pltpu.SMEM)
    vmem = pl.BlockSpec(memory_space=pltpu.VMEM)
    hbm = pl.BlockSpec(memory_space=pl.ANY)
    return pl.pallas_call(
        attend,
        out_shape=jax.ShapeDtypeStruct((3 * requests, D), jnp.float32),
        in_specs=[smem, smem, smem, vmem, hbm, hbm],
        out_specs=vmem,
        scratch_shapes=[
            pltpu.VMEM((used,) + page, jnp.bfloat16),
            pltpu.VMEM((used,) + page, jnp.bfloat16),
            pltpu.SemaphoreType.DMA((used,)),
            pltpu.SemaphoreType.DMA((used,)),
        ],
        compiler_params=pltpu.CompilerParams(vmem_limit_bytes=40 * 2**20),
        cost_estimate=pl.CostEstimate(flops=4 * 10**8, bytes_accessed=7 * 2**20, transcendentals=0),
        name="local_attention",
    )(place, page_table.reshape(-1), lengths, queries.astype(jnp.float32), key_pool, value_pool)


LABELS = ((0, 0), (0, 1), (1, 0), (1, 1))


def where_held(a, b, path):
    if a == b:
        return a, a
    if a == 1:
        return path, 1 - path
    return 1 - path, path


def expert_kernel(pairs, place_ref, side_ref, gate_ref, up_ref, down_ref, *rest):
    count = len(pairs)
    blocks = rest[: 4 * count]
    outs = rest[4 * count : 8 * count]
    xbuf, obuf, gbuf, ubuf, dbuf, wsem, xsem, osem = rest[8 * count :]
    holder, core = place_ref[0], place_ref[1]
    cols = xbuf.shape[3]
    per = xbuf.shape[1] // xsem.shape[0]
    paths = [core if d == 0 else 1 - core for _, d in pairs]
    for f in range(2):
        half = holder if f == 0 else 1 - holder
        pltpu.make_async_copy(gate_ref.at[half], gbuf.at[f], wsem.at[0, f]).start()
        pltpu.make_async_copy(up_ref.at[half], ubuf.at[f], wsem.at[1, f]).start()
    for p in range(count):
        for n, (a, b) in enumerate(LABELS):
            t, f = where_held(a, b, paths[p])
            pltpu.make_async_copy(
                blocks[4 * p + n], xbuf.at[f, 2 * p + t], xsem.at[2 * p // per]
            ).start()
    for f in range(2):
        half = holder if f == 0 else 1 - holder
        pltpu.make_async_copy(
            down_ref.at[:, pl.ds(pl.multiple_of(half * cols, cols), cols)], dbuf.at[f], wsem.at[2, f]
        ).start()
    rows = per * xbuf.shape[2]

    def step(m, carry):
        @pl.when(m == 0)
        def _():
            for f in range(2):
                pltpu.make_async_copy(gbuf.at[f], gbuf.at[f], wsem.at[0, f]).wait()
                pltpu.make_async_copy(ubuf.at[f], ubuf.at[f], wsem.at[1, f]).wait()

        part = xbuf.at[:, pl.ds(m * per, per)]
        pltpu.make_async_copy(part, part, xsem.at[m]).wait()
        first = xbuf[0, pl.ds(m * per, per)].reshape(rows, cols)
        second = xbuf[1, pl.ds(m * per, per)].reshape(rows, cols)
        side = side_ref[pl.ds(pl.multiple_of(m * rows, rows), rows), :]
        scale, share = side[:, 0:1], side[:, 1:2]
        gate = jnp.dot(first, gbuf[0], preferred_element_type=jnp.float32)
        gate += jnp.dot(second, gbuf[1], preferred_element_type=jnp.float32)
        gate *= scale
        up = jnp.dot(first, ubuf[0], preferred_element_type=jnp.float32)
        up += jnp.dot(second, ubuf[1], preferred_element_type=jnp.float32)
        up *= scale
        act = (gate / (1.0 + jnp.exp(-gate)) * up).astype(jnp.bfloat16)

        @pl.when(m == 0)
        def _():
            for f in range(2):
                pltpu.make_async_copy(dbuf.at[f], dbuf.at[f], wsem.at[2, f]).wait()

        for f in range(2):
            out = jnp.dot(act, dbuf[f], preferred_element_type=jnp.float32) * share
            obuf[f, pl.ds(m * per, per)] = out.astype(jnp.bfloat16).reshape(per, -1, cols)
        return carry

    steps = xsem.shape[0]
    for m in range(steps):
        step(m, 0)
        for p in range(m * per // 2, (m + 1) * per // 2):
            for n, (a, b) in enumerate(LABELS):
                t, f = where_held(a, b, paths[p])
                pltpu.make_async_copy(
                    obuf.at[f, 2 * p + t], outs[4 * p + n], osem.at[4 * p + n]
                ).start()
    for p in range(count):
        for n in range(4):
            pltpu.make_async_copy(obuf.at[0, 0], outs[4 * p + n], osem.at[4 * p + n]).wait()


def run_experts(pairs, place, side, gate, up, down, blocks):
    count = len(pairs)
    row_count, cols = blocks[0].shape
    hidden = gate.shape[2]
    groups = 2 * count
    per = 4 if groups % 4 == 0 else 2
    smem = pl.BlockSpec(memory_space=pltpu.SMEM)
    vmem = pl.BlockSpec(memory_space=pltpu.VMEM)
    hbm = pl.BlockSpec(memory_space=pl.ANY)

    def body(*refs):
        expert_kernel(pairs, *refs)

    return pl.pallas_call(
        body,
        out_shape=[jax.ShapeDtypeStruct((row_count, cols), jnp.bfloat16)] * (4 * count),
        in_specs=[smem, vmem, hbm, hbm, hbm] + [hbm] * (4 * count),
        out_specs=[hbm] * (4 * count),
        scratch_shapes=[
            pltpu.VMEM((2, groups, row_count, cols), jnp.bfloat16),
            pltpu.VMEM((2, groups, row_count, cols), jnp.bfloat16),
            pltpu.VMEM((2, cols, hidden), jnp.bfloat16),
            pltpu.VMEM((2, cols, hidden), jnp.bfloat16),
            pltpu.VMEM((2, hidden, cols), jnp.bfloat16),
            pltpu.SemaphoreType.DMA((3, 2)),
            pltpu.SemaphoreType.DMA((groups // per,)),
            pltpu.SemaphoreType.DMA((4 * count,)),
        ],
        compiler_params=pltpu.CompilerParams(vmem_limit_bytes=48 * 2**20),
        cost_estimate=pl.CostEstimate(
            flops=2 * groups * row_count * 2 * cols * hidden * 3,
            bytes_accessed=groups * row_count * cols * 8 + 12 * cols * hidden,
            transcendentals=0,
        ),
        name="experts",
    )(place, side, gate, up, down, *blocks)


def add(first, second):
    return (first.astype(jnp.float32) + second.astype(jnp.float32)).astype(jnp.bfloat16)


def dense(
    queries,
    key_pool,
    value_pool,
    page_table,
    lengths,
    prefill_attn,
    residual,
    w_out,
    norm_gain,
    router,
    w_gate,
    w_up,
    w_down,
    final_gain,
    routes,
):
    request_count = queries.shape[0]
    row_count, cols = residual.shape
    expert_count = router.shape[1]
    ep_size = lax.axis_size("ep")
    depth = ep_size // 4
    axes = ("ep", "kv")

    def number(z, y, c, x):
        return ((z * 2 + y) * 2 + c) * 2 + x

    places = [(z, y, c, x) for z in range(depth) for y in range(2) for c in range(2) for x in range(2)]

    def sent(array, target):
        return lax.ppermute(array, axes, [(number(*p), number(*target(*p))) for p in places])

    def across(array):
        return sent(array, lambda z, y, c, x: (z, y, c, 1 - x))

    def along(array, s):
        return sent(array, lambda z, y, c, x: ((z + s) % depth, y, c, x))

    def hop_one(array):
        return sent(array, lambda z, y, c, x: (z, y, c, 1 - x) if c == 0 else (z, 1 - y, c, x))

    def hop_two(array):
        return sent(array, lambda z, y, c, x: (z, 1 - y, c, x) if c == 0 else (z, y, c, 1 - x))

    def sibling(array):
        return sent(array, lambda z, y, c, x: (z, y, 1 - c, x))

    local = local_attention(queries, key_pool, value_pool, page_table, lengths)
    other = across(local)
    sum_one, sum_two = local[:request_count], other[:request_count]
    peak_one, peak_two = (v[request_count : 2 * request_count] for v in (local, other))
    mass_one, mass_two = (v[2 * request_count :] for v in (local, other))
    peak = jnp.maximum(peak_one, peak_two)
    factor_one, factor_two = jnp.exp(peak_one - peak), jnp.exp(peak_two - peak)
    decode_attn = (sum_one * factor_one + sum_two * factor_two) / (
        mass_one * factor_one + mass_two * factor_two
    )
    attn_rows = jnp.concatenate([prefill_attn, decode_attn.astype(jnp.bfloat16)], axis=0)
    hidden_state = residual.astype(jnp.float32) + jnp.dot(
        attn_rows, w_out, preferred_element_type=jnp.float32
    )
    scaled = (hidden_state * norm_gain).astype(jnp.bfloat16)

    held = {}
    column = [scaled] + [along(scaled, s) for s in range(1, depth)]
    for s in range(depth):
        zero = column[s]
        one = hop_one(zero)
        two, three = hop_two(zero), hop_two(one)
        for label, block in zip(LABELS, (zero, two, one, three)):
            held[s, 0, label] = block
            held[s, 1, label] = sibling(block)

    square_part = jnp.sum(hidden_state * hidden_state, axis=1)
    logit_part = jnp.dot(scaled, router, preferred_element_type=jnp.float32)
    stats = jnp.concatenate([logit_part, square_part[:, None]], axis=1).T
    stats = stats + across(stats)
    inv_first = lax.rsqrt(stats[expert_count] / D + epsilon)
    logits = stats[:expert_count].T * inv_first[:, None]
    matches = routes[:, :, None] == jnp.arange(expert_count, dtype=jnp.int32)[None, None, :]
    chosen = jnp.sum(jnp.where(matches, logits[:, None, :], 0.0), axis=2)
    raised = jnp.exp(chosen)
    gate_weights = raised / jnp.sum(raised, axis=1, keepdims=True)
    by_expert = jnp.sum(jnp.where(matches, gate_weights[:, :, None], 0.0), axis=1)
    side = jnp.concatenate([by_expert, inv_first[:, None]], axis=1).T
    sides = lax.all_gather(side, "ep", axis=0, tiled=False)
    own = lax.axis_index("ep")
    holder = lax.axis_index("kv")
    core, row_y, row_z = own % 2, (own // 2) % 2, own // 4
    share = lax.dynamic_index_in_dim(sides, own, axis=1, keepdims=False)
    scale = sides[:, expert_count]
    both = jnp.stack([scale, share], axis=-1)
    place = jnp.stack([holder, core]).astype(jnp.int32)
    gate_local = w_gate[0].reshape(2, cols, -1)
    up_local = w_up[0].reshape(2, cols, -1)
    down_local = w_down[0]

    half = depth // 2
    chunks = [
        [(s, d) for s in range(half) for d in range(2)],
        [(s, d) for s in range(half, depth) for d in range(2)],
    ]
    made = {}
    for pairs in chunks:
        order = jnp.stack(
            [
                (((row_z + depth - s) % depth) * 2 + (row_y + t) % 2) * 2 + (core + d) % 2
                for s, d in pairs
                for t in range(2)
            ]
        )
        chunk_side = both[order].reshape(-1, 2)
        blocks = [held[s, d, label] for s, d in pairs for label in LABELS]
        outs = run_experts(pairs, place, chunk_side, gate_local, up_local, down_local, blocks)
        for n, (s, d) in enumerate(pairs):
            for m, label in enumerate(LABELS):
                made[s, d, label] = outs[4 * n + m]

    sums = []
    for s in range(depth):
        got = {label: add(made[s, 0, label], sibling(made[s, 1, label])) for label in LABELS}
        near = [add(got[a, 0], hop_two(got[a, 1])) for a in range(2)]
        whole = add(near[0], hop_one(near[1]))
        sums.append(whole if s == 0 else along(whole, depth - s))
    combined = hidden_state
    for part in sums:
        combined = combined + part.astype(jnp.float32)
    square_two = jnp.sum(combined * combined, axis=1)[None, :]
    square_two = (square_two + across(square_two))[0]
    return (combined * lax.rsqrt(square_two / D + epsilon)[:, None] * final_gain).astype(
        jnp.bfloat16
    )


def per_device(*arrays):
    row_count, expert_count = arrays[6].shape[0], arrays[9].shape[1]
    capacity = min(row_count, 2 * row_count * TOP // expert_count)
    fits = lax.axis_size("kv") == 2 and lax.axis_size("ep") % 8 == 0
    if capacity == row_count and fits:
        return dense(*arrays)
    return routed(*arrays)


def solution(mesh):
    placed = (
        P("ep", None),
        P(("ep", "kv"), None, None),
        P(("ep", "kv"), None, None),
        P("ep", "kv", None),
        P("ep"),
        P("ep", None),
        P("ep", "kv"),
        P(None, "kv"),
        P("kv"),
        P("kv", None),
        P("ep", None, "kv"),
        P("ep", None, "kv"),
        P("ep", "kv", None),
        P("kv"),
        P("ep", None),
    )
    return jax.shard_map(
        per_device, mesh=mesh, in_specs=placed, out_specs=P("ep", "kv"), check_vma=False
    )
```

```python
import math

import jax
import jax.numpy as jnp
from jax import lax
from jax.experimental import pallas as pl
from jax.experimental.pallas import tpu as pltpu
from jax.sharding import PartitionSpec as P

D = 2048
HEADS = 16
HEAD_DIM = 128
TOP = 8


epsilon = 1e-06
floor_score = -1e30


def routed(
    queries,
    key_pool,
    value_pool,
    page_table,
    lengths,
    prefill_attn,
    residual,
    w_out,
    norm_gain,
    router,
    w_gate,
    w_up,
    w_down,
    final_gain,
    routes,
):
    holders = lax.axis_size("kv")
    holder = lax.axis_index("kv")
    request_count = queries.shape[0]
    pool_pages = key_pool.shape[0]
    page_rows = key_pool.shape[1]
    pages_each = page_table.shape[2]
    query_heads = queries.reshape(request_count, HEADS, HEAD_DIM)
    page_slots = page_table[:, 0, :]
    picked_keys = key_pool.reshape(pool_pages, page_rows, HEADS, HEAD_DIM)[page_slots]
    picked_values = value_pool.reshape(pool_pages, page_rows, HEADS, HEAD_DIM)[page_slots]
    scores = jnp.einsum(
        "rhd,rjphd->rhjp", query_heads, picked_keys, preferred_element_type=jnp.float32
    ) / math.sqrt(HEAD_DIM)
    page_number = jnp.arange(pages_each, dtype=jnp.int32) * holders + holder
    position = page_number[:, None] * page_rows + jnp.arange(page_rows, dtype=jnp.int32)[None, :]
    visible = position[None, None, :, :] < lengths[:, None, None, None]
    masked = jnp.where(visible, scores, floor_score)
    local_peak = jnp.max(masked, axis=(2, 3))
    weights = jnp.where(visible, jnp.exp(masked - local_peak[:, :, None, None]), 0.0)
    local_mass = jnp.sum(weights, axis=(2, 3))
    local_sum = jnp.einsum(
        "rhjp,rjphd->rhd",
        weights,
        picked_values.astype(jnp.float32),
        precision=lax.Precision.HIGHEST,
    )
    peak_rows, masses, gathered_sums = (
        lax.all_gather(local_peak[None], "kv", axis=0, tiled=True),
        lax.all_gather(local_mass[None], "kv", axis=0, tiled=True),
        lax.all_gather(local_sum[None], "kv", axis=0, tiled=True),
    )
    all_peak = jnp.max(peak_rows, axis=0)
    factors = jnp.exp(peak_rows - all_peak[None])
    all_mass = jnp.sum(masses * factors, axis=0)
    all_sum = jnp.sum(gathered_sums * factors[..., None], axis=0)
    decode_attn = (all_sum / all_mass[..., None]).reshape(request_count, D).astype(jnp.bfloat16)
    attn_rows = jnp.concatenate([prefill_attn, decode_attn], axis=0)
    hidden_state = residual.astype(jnp.float32) + jnp.dot(
        attn_rows, w_out, preferred_element_type=jnp.float32
    )
    scaled = (hidden_state * norm_gain).astype(jnp.bfloat16)
    square_sum, logit_parts = lax.psum(
        (
            jnp.sum(hidden_state * hidden_state, axis=1),
            jnp.dot(scaled, router, preferred_element_type=jnp.float32),
        ),
        "kv",
    )
    inv_first = lax.rsqrt(square_sum / D + epsilon)
    logits = logit_parts * inv_first[:, None]
    normed = (hidden_state * norm_gain * inv_first[:, None]).astype(jnp.bfloat16)
    row_count = residual.shape[0]
    expert_count = router.shape[1]
    capacity = min(row_count, 2 * row_count * TOP // expert_count)
    matches = routes[:, :, None] == jnp.arange(expert_count, dtype=jnp.int32)[None, None, :]
    chosen = jnp.sum(jnp.where(matches, logits[:, None, :], 0.0), axis=2)
    raised = jnp.exp(chosen)
    gate_weights = raised / jnp.sum(raised, axis=1, keepdims=True)
    one_hot = matches.reshape(row_count * TOP, expert_count).astype(jnp.int32)
    earlier = jnp.cumsum(one_hot, axis=0) - one_hot
    slot_index = jnp.sum(earlier * one_hot, axis=1)
    target = routes.reshape(-1) * capacity + slot_index
    source_row = jnp.arange(row_count * TOP, dtype=jnp.int32) // TOP
    filler = jnp.zeros((expert_count * capacity,), jnp.int32).at[target].set(source_row)
    present = jnp.zeros((expert_count * capacity,), jnp.bool_).at[target].set(True)
    gate_local = w_gate[0]
    up_local = w_up[0]
    down_local = w_down[0]
    full_rows = lax.all_gather(normed, "kv", axis=1, tiled=True)
    picked = full_rows[filler]
    arrived = lax.all_to_all(
        jnp.where(present[:, None], picked, jnp.zeros_like(picked)).reshape(
            expert_count, capacity, full_rows.shape[1]
        ),
        "ep",
        split_axis=0,
        concat_axis=0,
        tiled=True,
    )
    inbound = arrived.reshape(-1, arrived.shape[2])
    gate_proj = jnp.dot(inbound, gate_local, preferred_element_type=jnp.float32)
    up_proj = jnp.dot(inbound, up_local, preferred_element_type=jnp.float32)
    activation = (jax.nn.silu(gate_proj) * up_proj).astype(jnp.bfloat16)
    feature_cols = residual.shape[1]
    summed = lax.psum_scatter(
        lax.dot_general(
            down_local, activation, (((0,), (1,)), ((), ())), preferred_element_type=jnp.float32
        ).astype(jnp.bfloat16),
        "kv",
        scatter_dimension=0,
        tiled=True,
    ).astype(jnp.float32)
    expert_out = summed.T.astype(jnp.bfloat16).reshape(
        arrived.shape[0], arrived.shape[1], feature_cols
    )
    returned = lax.all_to_all(expert_out, "ep", split_axis=0, concat_axis=0, tiled=True)
    back_rows = (
        returned.reshape(-1, feature_cols)[target]
        .reshape(row_count, TOP, feature_cols)
        .astype(jnp.float32)
    )
    combined = hidden_state + jnp.sum(back_rows * gate_weights[:, :, None], axis=1)
    square_two = lax.psum(jnp.sum(combined * combined, axis=1), "kv")
    return (combined * lax.rsqrt(square_two / D + epsilon)[:, None] * final_gain).astype(
        jnp.bfloat16
    )


def attend(place_ref, slots_ref, lengths_ref, q_ref, k_ref, v_ref, out_ref, kbuf, vbuf, ksem, vsem):
    requests = q_ref.shape[0]
    pages_each = kbuf.shape[0] // requests
    page_rows = kbuf.shape[1]
    holder = place_ref[0]
    holders = place_ref[1]
    for i in range(requests * pages_each):
        pltpu.make_async_copy(k_ref.at[slots_ref[i]], kbuf.at[i], ksem.at[i]).start()
    for i in range(requests * pages_each):
        pltpu.make_async_copy(v_ref.at[slots_ref[i]], vbuf.at[i], vsem.at[i]).start()
    head_row = lax.broadcasted_iota(jnp.int32, (HEADS, D), 0)
    head_lane = lax.broadcasted_iota(jnp.int32, (HEADS, D), 1) // HEAD_DIM
    own_head = head_row == head_lane
    for r in range(requests):
        q = jnp.where(own_head, q_ref[r : r + 1, :], 0.0).astype(jnp.bfloat16)
        parts, seen = [], []
        for j in range(pages_each):
            i = r * pages_each + j
            pltpu.make_async_copy(k_ref.at[0], kbuf.at[i], ksem.at[i]).wait()
            part = lax.dot_general(
                q, kbuf[i], (((1,), (1,)), ((), ())), preferred_element_type=jnp.float32
            )
            start = (j * holders + holder) * page_rows
            position = start + lax.broadcasted_iota(jnp.int32, (HEADS, page_rows), 1)
            visible = position < lengths_ref[r]
            seen.append(visible)
            parts.append(jnp.where(visible, part / math.sqrt(HEAD_DIM), floor_score))
        peak = parts[0].max(axis=1, keepdims=True)
        for part in parts[1:]:
            peak = jnp.maximum(peak, part.max(axis=1, keepdims=True))
        mass = jnp.zeros((HEADS, 1), jnp.float32)
        total = jnp.zeros((2 * HEADS, D), jnp.float32)
        for j in range(pages_each):
            i = r * pages_each + j
            weight = jnp.where(seen[j], jnp.exp(parts[j] - peak), 0.0)
            mass += weight.sum(axis=1, keepdims=True)
            high = weight.astype(jnp.bfloat16)
            low = (weight - high.astype(jnp.float32)).astype(jnp.bfloat16)
            pltpu.make_async_copy(v_ref.at[0], vbuf.at[i], vsem.at[i]).wait()
            total += jnp.dot(
                jnp.concatenate([high, low], axis=0), vbuf[i], preferred_element_type=jnp.float32
            )
        both = total[:HEADS] + total[HEADS:]
        out_ref[r : r + 1, :] = jnp.sum(jnp.where(own_head, both, 0.0), axis=0, keepdims=True)
        out_ref[requests + r : requests + r + 1, :] = jnp.sum(
            jnp.where(own_head, peak, 0.0), axis=0, keepdims=True
        )
        out_ref[2 * requests + r : 2 * requests + r + 1, :] = jnp.sum(
            jnp.where(own_head, mass, 0.0), axis=0, keepdims=True
        )


def local_attention(queries, key_pool, value_pool, page_table, lengths):
    requests = queries.shape[0]
    used = requests * page_table.shape[2]
    page = key_pool.shape[1:]
    place = jnp.stack([lax.axis_index("kv"), jnp.int32(lax.axis_size("kv"))]).astype(jnp.int32)
    smem = pl.BlockSpec(memory_space=pltpu.SMEM)
    vmem = pl.BlockSpec(memory_space=pltpu.VMEM)
    hbm = pl.BlockSpec(memory_space=pl.ANY)
    return pl.pallas_call(
        attend,
        out_shape=jax.ShapeDtypeStruct((3 * requests, D), jnp.float32),
        in_specs=[smem, smem, smem, vmem, hbm, hbm],
        out_specs=vmem,
        scratch_shapes=[
            pltpu.VMEM((used,) + page, jnp.bfloat16),
            pltpu.VMEM((used,) + page, jnp.bfloat16),
            pltpu.SemaphoreType.DMA((used,)),
            pltpu.SemaphoreType.DMA((used,)),
        ],
        compiler_params=pltpu.CompilerParams(vmem_limit_bytes=60 * 2**20),
        cost_estimate=pl.CostEstimate(flops=4 * 10**8, bytes_accessed=7 * 2**20, transcendentals=0),
        name="local_attention",
    )(place, page_table.reshape(-1), lengths, queries.astype(jnp.float32), key_pool, value_pool)


LABELS = ((0, 0), (0, 1), (1, 0), (1, 1))


def where_held(a, b, path):
    if a == b:
        return a, a
    if a == 1:
        return path, 1 - path
    return 1 - path, path


def expert_kernel(place_ref, side_ref, gate_ref, up_ref, down_ref, *rest):
    blocks = rest[:8]
    outs = rest[8:16]
    xbuf, obuf, gbuf, ubuf, dbuf, wsem, xsem, osem = rest[16:]
    holder, core = place_ref[0], place_ref[1]
    pair = blocks[0].shape[0]
    cols = xbuf.shape[4]
    rows = 2 * pair * xbuf.shape[3]
    halves = (holder, 1 - holder)
    paths = (core, 1 - core)

    def fetch(d):
        for n, (a, b) in enumerate(LABELS):
            t, f = where_held(a, b, paths[d])
            pltpu.make_async_copy(
                blocks[4 * d + n], xbuf.at[d, f, pl.ds(t * pair, pair)], xsem.at[d]
            ).start()

    pltpu.make_async_copy(gate_ref.at[halves[0]], gbuf.at[0], wsem.at[0, 0]).start()
    fetch(0)
    pltpu.make_async_copy(gate_ref.at[halves[1]], gbuf.at[1], wsem.at[0, 1]).start()
    for f in range(2):
        pltpu.make_async_copy(up_ref.at[halves[f]], ubuf.at[f], wsem.at[1, f]).start()
    fetch(1)
    for f in range(2):
        start = pl.multiple_of(halves[f] * cols, cols)
        pltpu.make_async_copy(
            down_ref.at[:, pl.ds(start, cols)], dbuf.at[f], wsem.at[2, f]
        ).start()

    def ready(d, buffer, kind, f):
        if d == 0:
            pltpu.make_async_copy(buffer.at[f], buffer.at[f], wsem.at[kind, f]).wait()

    for d in range(2):
        pltpu.make_async_copy(xbuf.at[d], xbuf.at[d], xsem.at[d]).wait()
        first = xbuf[d, 0].reshape(rows, cols)
        second = xbuf[d, 1].reshape(rows, cols)
        side = side_ref[d * rows : (d + 1) * rows, :]
        scale, share = side[:, 0:1], side[:, 1:2]
        ready(d, gbuf, 0, 0)
        gate = jnp.dot(first, gbuf[0], preferred_element_type=jnp.float32)
        ready(d, gbuf, 0, 1)
        gate += jnp.dot(second, gbuf[1], preferred_element_type=jnp.float32)
        gate *= scale
        ready(d, ubuf, 1, 0)
        up = jnp.dot(first, ubuf[0], preferred_element_type=jnp.float32)
        ready(d, ubuf, 1, 1)
        up += jnp.dot(second, ubuf[1], preferred_element_type=jnp.float32)
        up *= scale
        act = (gate / (1.0 + jnp.exp(-gate)) * up).astype(jnp.bfloat16)
        for f in range(2):
            ready(d, dbuf, 2, f)
            out = jnp.dot(act, dbuf[f], preferred_element_type=jnp.float32) * share
            obuf[d, f] = out.astype(jnp.bfloat16).reshape(2 * pair, -1, cols)
        for n, (a, b) in enumerate(LABELS):
            t, f = where_held(a, b, paths[d])
            pltpu.make_async_copy(
                obuf.at[d, f, pl.ds(t * pair, pair)], outs[4 * d + n], osem.at[4 * d + n]
            ).start()
    for n in range(8):
        pltpu.make_async_copy(obuf.at[0, 0, pl.ds(0, pair)], outs[n], osem.at[n]).wait()


def run_experts(place, side, gate, up, down, blocks):
    pair, row_count, cols = blocks[0].shape
    hidden = gate.shape[2]
    smem = pl.BlockSpec(memory_space=pltpu.SMEM)
    vmem = pl.BlockSpec(memory_space=pltpu.VMEM)
    hbm = pl.BlockSpec(memory_space=pl.ANY)
    return pl.pallas_call(
        expert_kernel,
        out_shape=[jax.ShapeDtypeStruct(blocks[0].shape, jnp.bfloat16)] * 8,
        in_specs=[smem, vmem, hbm, hbm, hbm] + [hbm] * 8,
        out_specs=[hbm] * 8,
        scratch_shapes=[
            pltpu.VMEM((2, 2, 2 * pair, row_count, cols), jnp.bfloat16),
            pltpu.VMEM((2, 2, 2 * pair, row_count, cols), jnp.bfloat16),
            pltpu.VMEM((2, cols, hidden), jnp.bfloat16),
            pltpu.VMEM((2, cols, hidden), jnp.bfloat16),
            pltpu.VMEM((2, hidden, cols), jnp.bfloat16),
            pltpu.SemaphoreType.DMA((3, 2)),
            pltpu.SemaphoreType.DMA((2,)),
            pltpu.SemaphoreType.DMA((8,)),
        ],
        compiler_params=pltpu.CompilerParams(vmem_limit_bytes=28 * 2**20),
        cost_estimate=pl.CostEstimate(
            flops=4 * pair * row_count * 12 * cols * hidden,
            bytes_accessed=pair * row_count * cols * 32 + 12 * cols * hidden,
            transcendentals=0,
        ),
        name="experts",
    )(place, side, gate, up, down, *blocks)


def add(first, second):
    return (first.astype(jnp.float32) + second.astype(jnp.float32)).astype(jnp.bfloat16)


def dense(
    queries,
    key_pool,
    value_pool,
    page_table,
    lengths,
    prefill_attn,
    residual,
    w_out,
    norm_gain,
    router,
    w_gate,
    w_up,
    w_down,
    final_gain,
    routes,
):
    request_count = queries.shape[0]
    row_count, cols = residual.shape
    expert_count = router.shape[1]
    ep_size = lax.axis_size("ep")
    depth = ep_size // 4
    axes = ("ep", "kv")

    def number(z, y, c, x):
        return ((z * 2 + y) * 2 + c) * 2 + x

    places = [(z, y, c, x) for z in range(depth) for y in range(2) for c in range(2) for x in range(2)]

    def sent(array, target):
        return lax.ppermute(array, axes, [(number(*p), number(*target(*p))) for p in places])

    def across(array):
        return sent(array, lambda z, y, c, x: (z, y, c, 1 - x))

    def along(array, s):
        return sent(array, lambda z, y, c, x: ((z + s) % depth, y, c, x))

    def hop_one(array):
        return sent(array, lambda z, y, c, x: (z, y, c, 1 - x) if c == 0 else (z, 1 - y, c, x))

    def hop_two(array):
        return sent(array, lambda z, y, c, x: (z, 1 - y, c, x) if c == 0 else (z, y, c, 1 - x))

    def sibling(array):
        return sent(array, lambda z, y, c, x: (z, y, 1 - c, x))

    def returned(total, chunk, got):
        far = add(got[2], hop_two(got[3]))
        near = add(got[0], hop_two(got[1]))
        whole = add(near, hop_one(far))
        for i, s in enumerate(chunk):
            part = whole[i] if s == 0 else along(whole[i], depth - s)
            total = total + part.astype(jnp.float32)
        return total

    local = local_attention(queries, key_pool, value_pool, page_table, lengths)
    other = across(local)
    sum_one, sum_two = local[:request_count], other[:request_count]
    peak_one, peak_two = (v[request_count : 2 * request_count] for v in (local, other))
    mass_one, mass_two = (v[2 * request_count :] for v in (local, other))
    peak = jnp.maximum(peak_one, peak_two)
    factor_one, factor_two = jnp.exp(peak_one - peak), jnp.exp(peak_two - peak)
    decode_attn = (sum_one * factor_one + sum_two * factor_two) / (
        mass_one * factor_one + mass_two * factor_two
    )
    attn_rows = jnp.concatenate([prefill_attn, decode_attn.astype(jnp.bfloat16)], axis=0)
    hidden_state = residual.astype(jnp.float32) + jnp.dot(
        attn_rows, w_out, preferred_element_type=jnp.float32
    )
    scaled = (hidden_state * norm_gain).astype(jnp.bfloat16)

    half = depth // 2
    slots = list(range(half)) + list(range(depth - 1, half - 1, -1))
    column = {0: scaled}
    for s in slots[1:]:
        column[s] = along(scaled, s)
    chunks = [slots[:half], slots[half:]]
    fetched = []
    for chunk in chunks:
        zero = jnp.stack([column[s] for s in chunk])
        one = hop_one(zero)
        blocks = [zero, hop_two(zero), one, hop_two(one)]
        fetched.append(blocks + [sibling(block) for block in blocks])

    square_part = jnp.sum(hidden_state * hidden_state, axis=1)
    logit_part = jnp.dot(scaled, router, preferred_element_type=jnp.float32)
    stats = jnp.concatenate([logit_part, square_part[:, None]], axis=1).T
    stats = stats + across(stats)
    inv_first = lax.rsqrt(stats[expert_count] / D + epsilon)
    logits = stats[:expert_count].T * inv_first[:, None]
    matches = routes[:, :, None] == jnp.arange(expert_count, dtype=jnp.int32)[None, None, :]
    chosen = jnp.sum(jnp.where(matches, logits[:, None, :], 0.0), axis=2)
    raised = jnp.exp(chosen)
    gate_weights = raised / jnp.sum(raised, axis=1, keepdims=True)
    by_expert = jnp.sum(jnp.where(matches, gate_weights[:, :, None], 0.0), axis=1)
    side = jnp.concatenate([by_expert, inv_first[:, None]], axis=1).T
    own = lax.axis_index("ep")
    sides = side[None]
    bit = 1
    while bit < ep_size:
        moved = lax.ppermute(sides, "ep", [(i, i ^ bit) for i in range(ep_size)])
        sides = jnp.concatenate([sides, moved], axis=0)
        bit *= 2
    holder = lax.axis_index("kv")
    core, row_y, row_z = own % 2, (own // 2) % 2, own // 4
    share = lax.dynamic_index_in_dim(sides, own, axis=1, keepdims=False)
    scale = sides[:, expert_count]
    order = jnp.stack(
        [
            ((((row_z + depth - s) % depth) * 2 + (row_y + t) % 2) * 2 + (core + d) % 2) ^ own
            for chunk in chunks
            for d in range(2)
            for t in range(2)
            for s in chunk
        ]
    )
    both = jnp.stack([scale, share], axis=-1)[order].reshape(2, -1, 2)
    place = jnp.stack([holder, core]).astype(jnp.int32)
    gate_local = w_gate[0].reshape(2, cols, -1)
    up_local = w_up[0].reshape(2, cols, -1)
    down_local = w_down[0]

    combined = hidden_state
    for n, chunk in enumerate(chunks):
        blocks = fetched[n]
        if n:
            blocks, got = lax.optimization_barrier((blocks, got))
            combined = returned(combined, chunks[n - 1], got)
        made = run_experts(place, both[n], gate_local, up_local, down_local, blocks)
        got = [add(made[m], sibling(made[4 + m])) for m in range(4)]
    combined = returned(combined, chunks[-1], got)
    square_two = jnp.sum(combined * combined, axis=1)[None, :]
    square_two = (square_two + across(square_two))[0]
    return (combined * lax.rsqrt(square_two / D + epsilon)[:, None] * final_gain).astype(
        jnp.bfloat16
    )


def per_device(*arrays):
    row_count, expert_count = arrays[6].shape[0], arrays[9].shape[1]
    capacity = min(row_count, 2 * row_count * TOP // expert_count)
    fits = lax.axis_size("kv") == 2 and lax.axis_size("ep") == 16
    if capacity == row_count and fits:
        return dense(*arrays)
    return routed(*arrays)


def solution(mesh):
    placed = (
        P("ep", None),
        P(("ep", "kv"), None, None),
        P(("ep", "kv"), None, None),
        P("ep", "kv", None),
        P("ep"),
        P("ep", None),
        P("ep", "kv"),
        P(None, "kv"),
        P("kv"),
        P("kv", None),
        P("ep", None, "kv"),
        P("ep", None, "kv"),
        P("ep", "kv", None),
        P("kv"),
        P("ep", None),
    )
    return jax.shard_map(
        per_device, mesh=mesh, in_specs=placed, out_specs=P("ep", "kv"), check_vma=False
    )
```

```python
import math

import jax
import jax.numpy as jnp
from jax import lax
from jax.experimental import pallas as pl
from jax.experimental.pallas import tpu as pltpu
from jax.sharding import PartitionSpec as P

D = 2048
HEADS = 16
HEAD_DIM = 128
TOP = 8


epsilon = 1e-06
floor_score = -1e30


def routed(
    queries,
    key_pool,
    value_pool,
    page_table,
    lengths,
    prefill_attn,
    residual,
    w_out,
    norm_gain,
    router,
    w_gate,
    w_up,
    w_down,
    final_gain,
    routes,
):
    holders = lax.axis_size("kv")
    holder = lax.axis_index("kv")
    request_count = queries.shape[0]
    pool_pages = key_pool.shape[0]
    page_rows = key_pool.shape[1]
    pages_each = page_table.shape[2]
    query_heads = queries.reshape(request_count, HEADS, HEAD_DIM)
    page_slots = page_table[:, 0, :]
    picked_keys = key_pool.reshape(pool_pages, page_rows, HEADS, HEAD_DIM)[page_slots]
    picked_values = value_pool.reshape(pool_pages, page_rows, HEADS, HEAD_DIM)[page_slots]
    scores = jnp.einsum(
        "rhd,rjphd->rhjp", query_heads, picked_keys, preferred_element_type=jnp.float32
    ) / math.sqrt(HEAD_DIM)
    page_number = jnp.arange(pages_each, dtype=jnp.int32) * holders + holder
    position = page_number[:, None] * page_rows + jnp.arange(page_rows, dtype=jnp.int32)[None, :]
    visible = position[None, None, :, :] < lengths[:, None, None, None]
    masked = jnp.where(visible, scores, floor_score)
    local_peak = jnp.max(masked, axis=(2, 3))
    weights = jnp.where(visible, jnp.exp(masked - local_peak[:, :, None, None]), 0.0)
    local_mass = jnp.sum(weights, axis=(2, 3))
    local_sum = jnp.einsum(
        "rhjp,rjphd->rhd",
        weights,
        picked_values.astype(jnp.float32),
        precision=lax.Precision.HIGHEST,
    )
    peak_rows, masses, gathered_sums = (
        lax.all_gather(local_peak[None], "kv", axis=0, tiled=True),
        lax.all_gather(local_mass[None], "kv", axis=0, tiled=True),
        lax.all_gather(local_sum[None], "kv", axis=0, tiled=True),
    )
    all_peak = jnp.max(peak_rows, axis=0)
    factors = jnp.exp(peak_rows - all_peak[None])
    all_mass = jnp.sum(masses * factors, axis=0)
    all_sum = jnp.sum(gathered_sums * factors[..., None], axis=0)
    decode_attn = (all_sum / all_mass[..., None]).reshape(request_count, D).astype(jnp.bfloat16)
    attn_rows = jnp.concatenate([prefill_attn, decode_attn], axis=0)
    hidden_state = residual.astype(jnp.float32) + jnp.dot(
        attn_rows, w_out, preferred_element_type=jnp.float32
    )
    scaled = (hidden_state * norm_gain).astype(jnp.bfloat16)
    square_sum, logit_parts = lax.psum(
        (
            jnp.sum(hidden_state * hidden_state, axis=1),
            jnp.dot(scaled, router, preferred_element_type=jnp.float32),
        ),
        "kv",
    )
    inv_first = lax.rsqrt(square_sum / D + epsilon)
    logits = logit_parts * inv_first[:, None]
    normed = (hidden_state * norm_gain * inv_first[:, None]).astype(jnp.bfloat16)
    row_count = residual.shape[0]
    expert_count = router.shape[1]
    capacity = min(row_count, 2 * row_count * TOP // expert_count)
    matches = routes[:, :, None] == jnp.arange(expert_count, dtype=jnp.int32)[None, None, :]
    chosen = jnp.sum(jnp.where(matches, logits[:, None, :], 0.0), axis=2)
    raised = jnp.exp(chosen)
    gate_weights = raised / jnp.sum(raised, axis=1, keepdims=True)
    one_hot = matches.reshape(row_count * TOP, expert_count).astype(jnp.int32)
    earlier = jnp.cumsum(one_hot, axis=0) - one_hot
    slot_index = jnp.sum(earlier * one_hot, axis=1)
    target = routes.reshape(-1) * capacity + slot_index
    source_row = jnp.arange(row_count * TOP, dtype=jnp.int32) // TOP
    filler = jnp.zeros((expert_count * capacity,), jnp.int32).at[target].set(source_row)
    present = jnp.zeros((expert_count * capacity,), jnp.bool_).at[target].set(True)
    gate_local = w_gate[0]
    up_local = w_up[0]
    down_local = w_down[0]
    full_rows = lax.all_gather(normed, "kv", axis=1, tiled=True)
    picked = full_rows[filler]
    arrived = lax.all_to_all(
        jnp.where(present[:, None], picked, jnp.zeros_like(picked)).reshape(
            expert_count, capacity, full_rows.shape[1]
        ),
        "ep",
        split_axis=0,
        concat_axis=0,
        tiled=True,
    )
    inbound = arrived.reshape(-1, arrived.shape[2])
    gate_proj = jnp.dot(inbound, gate_local, preferred_element_type=jnp.float32)
    up_proj = jnp.dot(inbound, up_local, preferred_element_type=jnp.float32)
    activation = (jax.nn.silu(gate_proj) * up_proj).astype(jnp.bfloat16)
    feature_cols = residual.shape[1]
    summed = lax.psum_scatter(
        lax.dot_general(
            down_local, activation, (((0,), (1,)), ((), ())), preferred_element_type=jnp.float32
        ).astype(jnp.bfloat16),
        "kv",
        scatter_dimension=0,
        tiled=True,
    ).astype(jnp.float32)
    expert_out = summed.T.astype(jnp.bfloat16).reshape(
        arrived.shape[0], arrived.shape[1], feature_cols
    )
    returned = lax.all_to_all(expert_out, "ep", split_axis=0, concat_axis=0, tiled=True)
    back_rows = (
        returned.reshape(-1, feature_cols)[target]
        .reshape(row_count, TOP, feature_cols)
        .astype(jnp.float32)
    )
    combined = hidden_state + jnp.sum(back_rows * gate_weights[:, :, None], axis=1)
    square_two = lax.psum(jnp.sum(combined * combined, axis=1), "kv")
    return (combined * lax.rsqrt(square_two / D + epsilon)[:, None] * final_gain).astype(
        jnp.bfloat16
    )


def attend(slots_ref, lengths_ref, q_ref, k_ref, v_ref, out_ref, kbuf, vbuf, ksem, vsem):
    requests, pages_each, page_rows = kbuf.shape[:3]
    holder = lax.axis_index("kv")
    holders = lax.axis_size("kv")
    for r in range(requests):
        for j in range(pages_each):
            pltpu.make_async_copy(k_ref.at[slots_ref[r, 0, j]], kbuf.at[r, j], ksem.at[r]).start()
    for r in range(requests):
        for j in range(pages_each):
            pltpu.make_async_copy(v_ref.at[slots_ref[r, 0, j]], vbuf.at[r, j], vsem.at[r]).start()
    tokens = pages_each * page_rows
    wide_row = lax.broadcasted_iota(jnp.int32, (HEAD_DIM, D), 0)
    wide_head = lax.broadcasted_iota(jnp.int32, (HEAD_DIM, D), 1) // HEAD_DIM
    own_head = (wide_row == wide_head)[:HEADS]
    place = lax.broadcasted_iota(jnp.int32, (HEADS, tokens), 1)
    position = ((place // page_rows) * holders + holder) * page_rows + place % page_rows
    queries = q_ref[...].astype(jnp.float32)
    for r in range(requests):
        spread = jnp.where(wide_row == wide_head, queries[r : r + 1, :], 0.0).astype(jnp.bfloat16)
        pltpu.make_async_copy(kbuf.at[r], kbuf.at[r], ksem.at[r]).wait()
        scores = lax.dot_general(
            kbuf[r].reshape(tokens, D),
            spread,
            (((1,), (1,)), ((), ())),
            preferred_element_type=jnp.float32,
        )
        visible = position < lengths_ref[r]
        scores = jnp.where(visible, scores.T[:HEADS] / math.sqrt(HEAD_DIM), floor_score)
        peak = scores.max(axis=1, keepdims=True)
        weight = jnp.where(visible, jnp.exp(scores - peak), 0.0)
        mass = weight.sum(axis=1, keepdims=True)
        high = weight.astype(jnp.bfloat16)
        low = (weight - high.astype(jnp.float32)).astype(jnp.bfloat16)
        pltpu.make_async_copy(vbuf.at[r], vbuf.at[r], vsem.at[r]).wait()
        total = jnp.dot(
            jnp.concatenate([high, low], axis=0),
            vbuf[r].reshape(tokens, D),
            preferred_element_type=jnp.float32,
        )
        both = total[:HEADS] + total[HEADS:]
        for n, part in enumerate((both, peak, mass)):
            row = n * requests + r
            out_ref[row : row + 1, :] = jnp.sum(
                jnp.where(own_head, part, 0.0), axis=0, keepdims=True
            )


def local_attention(queries, key_pool, value_pool, page_table, lengths):
    requests, _, pages_each = page_table.shape
    held = (requests, pages_each) + key_pool.shape[1:]
    smem = pl.BlockSpec(memory_space=pltpu.SMEM)
    vmem = pl.BlockSpec(memory_space=pltpu.VMEM)
    hbm = pl.BlockSpec(memory_space=pl.ANY)
    return pl.pallas_call(
        attend,
        out_shape=jax.ShapeDtypeStruct((3 * requests, D), jnp.float32),
        in_specs=[smem, smem, vmem, hbm, hbm],
        out_specs=vmem,
        scratch_shapes=[
            pltpu.VMEM(held, jnp.bfloat16),
            pltpu.VMEM(held, jnp.bfloat16),
            pltpu.SemaphoreType.DMA((requests,)),
            pltpu.SemaphoreType.DMA((requests,)),
        ],
        compiler_params=pltpu.CompilerParams(vmem_limit_bytes=60 * 2**20),
        cost_estimate=pl.CostEstimate(flops=4 * 10**8, bytes_accessed=7 * 2**20, transcendentals=0),
        name="local_attention",
    )(page_table, lengths, queries, key_pool, value_pool)


LABELS = ((0, 0), (0, 1), (1, 0), (1, 1))


def where_held(a, b, path):
    if a == b:
        return a, a
    if a == 1:
        return path, 1 - path
    return 1 - path, path


def expert_kernel(d, side_ref, gate_ref, up_ref, down_ref, *rest):
    blocks = rest[:4]
    outs = rest[4:8]
    xbuf, obuf, gbuf, ubuf, dbuf, wsem, xsem, osem = rest[8:]
    holder, core = lax.axis_index("kv"), lax.axis_index("ep") % 2
    pair = blocks[0].shape[0]
    cols = xbuf.shape[3]
    rows = 2 * pair * xbuf.shape[2]
    halves = (holder, 1 - holder)
    path = core if d == 0 else 1 - core

    for n, (a, b) in enumerate(LABELS):
        t, f = where_held(a, b, path)
        pltpu.make_async_copy(blocks[n], xbuf.at[f, pl.ds(t * pair, pair)], xsem).start()
    for kind, (source, buffer) in enumerate(((gate_ref, gbuf), (up_ref, ubuf))):
        for f in range(2):
            pltpu.make_async_copy(source.at[halves[f]], buffer.at[f], wsem.at[kind, f]).start()
    for f in range(2):
        start = pl.multiple_of(halves[f] * cols, cols)
        pltpu.make_async_copy(
            down_ref.at[:, pl.ds(start, cols)], dbuf.at[f], wsem.at[2, f]
        ).start()

    def ready(buffer, kind, f):
        pltpu.make_async_copy(buffer.at[f], buffer.at[f], wsem.at[kind, f]).wait()

    pltpu.make_async_copy(xbuf, xbuf, xsem).wait()
    first = xbuf[0].reshape(rows, cols)
    second = xbuf[1].reshape(rows, cols)
    side = side_ref[...]
    scale, share = side[:, 0:1], side[:, 1:2]
    ready(gbuf, 0, 0)
    gate = jnp.dot(first, gbuf[0], preferred_element_type=jnp.float32)
    ready(gbuf, 0, 1)
    gate += jnp.dot(second, gbuf[1], preferred_element_type=jnp.float32)
    gate *= scale
    ready(ubuf, 1, 0)
    up = jnp.dot(first, ubuf[0], preferred_element_type=jnp.float32)
    ready(ubuf, 1, 1)
    up += jnp.dot(second, ubuf[1], preferred_element_type=jnp.float32)
    up *= scale
    act = (gate / (1.0 + jnp.exp(-gate)) * up).astype(jnp.bfloat16)
    for f in range(2):
        ready(dbuf, 2, f)
        out = jnp.dot(act, dbuf[f], preferred_element_type=jnp.float32) * share
        obuf[f] = out.astype(jnp.bfloat16).reshape(2 * pair, -1, cols)
    for n, (a, b) in enumerate(LABELS):
        t, f = where_held(a, b, path)
        pltpu.make_async_copy(obuf.at[f, pl.ds(t * pair, pair)], outs[n], osem.at[n]).start()
    for n in range(4):
        pltpu.make_async_copy(obuf.at[0, pl.ds(0, pair)], outs[n], osem.at[n]).wait()


def run_experts(d, side, gate, up, down, blocks):
    pair, row_count, cols = blocks[0].shape
    hidden = gate.shape[2]
    vmem = pl.BlockSpec(memory_space=pltpu.VMEM)
    hbm = pl.BlockSpec(memory_space=pl.ANY)

    def body(*refs):
        expert_kernel(d, *refs)

    return pl.pallas_call(
        body,
        out_shape=[jax.ShapeDtypeStruct(blocks[0].shape, jnp.bfloat16)] * 4,
        in_specs=[vmem, hbm, hbm, hbm] + [hbm] * 4,
        out_specs=[hbm] * 4,
        scratch_shapes=[
            pltpu.VMEM((2, 2 * pair, row_count, cols), jnp.bfloat16),
            pltpu.VMEM((2, 2 * pair, row_count, cols), jnp.bfloat16),
            pltpu.VMEM((2, cols, hidden), jnp.bfloat16),
            pltpu.VMEM((2, cols, hidden), jnp.bfloat16),
            pltpu.VMEM((2, hidden, cols), jnp.bfloat16),
            pltpu.SemaphoreType.DMA((3, 2)),
            pltpu.SemaphoreType.DMA,
            pltpu.SemaphoreType.DMA((4,)),
        ],
        compiler_params=pltpu.CompilerParams(vmem_limit_bytes=60 * 2**20),
        cost_estimate=pl.CostEstimate(
            flops=2 * pair * row_count * 12 * cols * hidden,
            bytes_accessed=pair * row_count * cols * 16 + 12 * cols * hidden,
            transcendentals=0,
        ),
        name="experts",
    )(side, gate, up, down, *blocks)


def add(first, second):
    return (first.astype(jnp.float32) + second.astype(jnp.float32)).astype(jnp.bfloat16)


def dense(
    queries,
    key_pool,
    value_pool,
    page_table,
    lengths,
    prefill_attn,
    residual,
    w_out,
    norm_gain,
    router,
    w_gate,
    w_up,
    w_down,
    final_gain,
    routes,
):
    request_count = queries.shape[0]
    row_count, cols = residual.shape
    expert_count = router.shape[1]
    ep_size = lax.axis_size("ep")
    depth = ep_size // 4
    axes = ("ep", "kv")

    def number(z, y, c, x):
        return ((z * 2 + y) * 2 + c) * 2 + x

    places = [(z, y, c, x) for z in range(depth) for y in range(2) for c in range(2) for x in range(2)]

    def sent(array, target):
        return lax.ppermute(array, axes, [(number(*p), number(*target(*p))) for p in places])

    def across(array):
        return sent(array, lambda z, y, c, x: (z, y, c, 1 - x))

    def along(array, s):
        return sent(array, lambda z, y, c, x: ((z + s) % depth, y, c, x))

    def hop_one(array):
        return sent(array, lambda z, y, c, x: (z, y, c, 1 - x) if c == 0 else (z, 1 - y, c, x))

    def hop_two(array):
        return sent(array, lambda z, y, c, x: (z, 1 - y, c, x) if c == 0 else (z, y, c, 1 - x))

    def sibling(array):
        return sent(array, lambda z, y, c, x: (z, y, 1 - c, x))

    def fence(*values):
        return lax.optimization_barrier(values)

    local = local_attention(queries, key_pool, value_pool, page_table, lengths)
    other = across(local)
    sum_one, sum_two = local[:request_count], other[:request_count]
    peak_one, peak_two = (v[request_count : 2 * request_count] for v in (local, other))
    mass_one, mass_two = (v[2 * request_count :] for v in (local, other))
    peak = jnp.maximum(peak_one, peak_two)
    factor_one, factor_two = jnp.exp(peak_one - peak), jnp.exp(peak_two - peak)
    decode_attn = (sum_one * factor_one + sum_two * factor_two) / (
        mass_one * factor_one + mass_two * factor_two
    )
    attn_rows = jnp.concatenate([prefill_attn, decode_attn.astype(jnp.bfloat16)], axis=0)
    hidden_state = residual.astype(jnp.float32) + jnp.dot(
        attn_rows, w_out, preferred_element_type=jnp.float32
    )
    scaled = (hidden_state * norm_gain).astype(jnp.bfloat16)

    square_part = jnp.sum(hidden_state * hidden_state, axis=1)
    logit_part = jnp.dot(scaled, router, preferred_element_type=jnp.float32)
    stats = jnp.concatenate([logit_part, square_part[:, None]], axis=1).T

    slots = ((0, 1), (3, 2))
    far_one = along(scaled, 1)
    stats = stats + across(stats)
    far_one, scaled = fence(far_one, scaled)

    pair = jnp.stack([scaled, far_one])
    far_three, one, pair_s = along(scaled, 3), hop_one(pair), sibling(pair)

    inv_first = lax.rsqrt(stats[expert_count] / D + epsilon)
    logits = stats[:expert_count].T * inv_first[:, None]
    matches = routes[:, :, None] == jnp.arange(expert_count, dtype=jnp.int32)[None, None, :]
    chosen = jnp.sum(jnp.where(matches, logits[:, None, :], 0.0), axis=2)
    raised = jnp.exp(chosen)
    gate_weights = raised / jnp.sum(raised, axis=1, keepdims=True)
    by_expert = jnp.sum(jnp.where(matches, gate_weights[:, :, None], 0.0), axis=1)
    side = jnp.concatenate([by_expert, inv_first[:, None]], axis=1).T
    own = lax.axis_index("ep")
    sides = side[None]
    bit = 1
    while bit < ep_size:
        moved = lax.ppermute(sides, "ep", [(i, i ^ bit) for i in range(ep_size)])
        sides = jnp.concatenate([sides, moved], axis=0)
        bit *= 2
    core, row_y, row_z = own % 2, (own // 2) % 2, own // 4
    share = lax.dynamic_index_in_dim(sides, own, axis=1, keepdims=False)
    scale = sides[:, expert_count]
    order = jnp.stack(
        [
            ((((row_z + depth - s) % depth) * 2 + (row_y + t) % 2) * 2 + (core + d) % 2) ^ own
            for chunk in slots
            for d in range(2)
            for t in range(2)
            for s in chunk
        ]
    )
    both = jnp.stack([scale, share], axis=-1)[order].reshape(2, 2, -1, 2)
    gate_local = w_gate[0].reshape(2, cols, -1)
    up_local = w_up[0].reshape(2, cols, -1)
    down_local = w_down[0]

    def experts(n, d, *blocks):
        return run_experts(d, both[n, d], gate_local, up_local, down_local, blocks)

    far_three, one, pair_s, pair, scaled = fence(far_three, one, pair_s, pair, scaled)
    far_two, two, three, one_s = along(scaled, 2), hop_two(pair), hop_two(one), sibling(one)
    far_two, far_three, two, three, one_s, pair, one = fence(
        far_two, far_three, two, three, one_s, pair, one
    )

    later = jnp.stack([far_three, far_two])
    later_one, two_s, three_s, later_s = hop_one(later), sibling(two), sibling(three), sibling(later)
    made = experts(0, 0, pair, two, one, three)
    later_one, two_s, three_s, later_s, later, made = fence(
        later_one, two_s, three_s, later_s, later, made
    )

    later_two, later_three, later_one_s = hop_two(later), hop_two(later_one), sibling(later_one)
    made_s = experts(0, 1, pair_s, two_s, one_s, three_s)
    got = [add(a, sibling(b)) for a, b in zip(made, made_s)]
    later_two, later_three, later_one_s, got, later, later_one = fence(
        later_two, later_three, later_one_s, got, later, later_one
    )

    from_one, from_three = hop_two(got[1]), hop_two(got[3])
    later_two_s, later_three_s = sibling(later_two), sibling(later_three)
    made = experts(1, 0, later, later_two, later_one, later_three)
    made_s = experts(1, 1, later_s, later_two_s, later_one_s, later_three_s)
    from_one, from_three, made, made_s = fence(from_one, from_three, made, made_s)

    near, far = add(got[0], from_one), add(got[2], from_three)
    moved = hop_one(far)
    got = [add(a, sibling(b)) for a, b in zip(made, made_s)]
    moved, near, got = fence(moved, near, got)

    whole = add(near, moved)
    combined = hidden_state + whole[0].astype(jnp.float32)
    part = along(whole[1], depth - 1)
    from_one, from_three = hop_two(got[1]), hop_two(got[3])
    part, from_one, from_three = fence(part, from_one, from_three)
    combined = combined + part.astype(jnp.float32)
    near, far = add(got[0], from_one), add(got[2], from_three)
    whole = add(near, hop_one(far))
    for i, s in enumerate(slots[1]):
        combined = combined + along(whole[i], depth - s).astype(jnp.float32)
    square_two = jnp.sum(combined * combined, axis=1)[None, :]
    square_two = (square_two + across(square_two))[0]
    return (combined * lax.rsqrt(square_two / D + epsilon)[:, None] * final_gain).astype(
        jnp.bfloat16
    )


def per_device(*arrays):
    row_count, expert_count = arrays[6].shape[0], arrays[9].shape[1]
    capacity = min(row_count, 2 * row_count * TOP // expert_count)
    fits = lax.axis_size("kv") == 2 and lax.axis_size("ep") == 16
    if capacity == row_count and fits:
        return dense(*arrays)
    return routed(*arrays)


def solution(mesh):
    placed = (
        P("ep", None),
        P(("ep", "kv"), None, None),
        P(("ep", "kv"), None, None),
        P("ep", "kv", None),
        P("ep"),
        P("ep", None),
        P("ep", "kv"),
        P(None, "kv"),
        P("kv"),
        P("kv", None),
        P("ep", None, "kv"),
        P("ep", None, "kv"),
        P("ep", "kv", None),
        P("kv"),
        P("ep", None),
    )
    return jax.shard_map(
        per_device, mesh=mesh, in_specs=placed, out_specs=P("ep", "kv"), check_vma=False
    )
```

```python
import math

import jax
import jax.numpy as jnp
from jax import lax
from jax.experimental import pallas as pl
from jax.experimental.pallas import tpu as pltpu
from jax.sharding import PartitionSpec as P

D = 2048
HEADS = 16
HEAD_DIM = 128
TOP = 8


epsilon = 1e-06
floor_score = -1e30


def routed(
    queries,
    key_pool,
    value_pool,
    page_table,
    lengths,
    prefill_attn,
    residual,
    w_out,
    norm_gain,
    router,
    w_gate,
    w_up,
    w_down,
    final_gain,
    routes,
):
    holders = lax.axis_size("kv")
    holder = lax.axis_index("kv")
    request_count = queries.shape[0]
    pool_pages = key_pool.shape[0]
    page_rows = key_pool.shape[1]
    pages_each = page_table.shape[2]
    query_heads = queries.reshape(request_count, HEADS, HEAD_DIM)
    page_slots = page_table[:, 0, :]
    picked_keys = key_pool.reshape(pool_pages, page_rows, HEADS, HEAD_DIM)[page_slots]
    picked_values = value_pool.reshape(pool_pages, page_rows, HEADS, HEAD_DIM)[page_slots]
    scores = jnp.einsum(
        "rhd,rjphd->rhjp", query_heads, picked_keys, preferred_element_type=jnp.float32
    ) / math.sqrt(HEAD_DIM)
    page_number = jnp.arange(pages_each, dtype=jnp.int32) * holders + holder
    position = page_number[:, None] * page_rows + jnp.arange(page_rows, dtype=jnp.int32)[None, :]
    visible = position[None, None, :, :] < lengths[:, None, None, None]
    masked = jnp.where(visible, scores, floor_score)
    local_peak = jnp.max(masked, axis=(2, 3))
    weights = jnp.where(visible, jnp.exp(masked - local_peak[:, :, None, None]), 0.0)
    local_mass = jnp.sum(weights, axis=(2, 3))
    local_sum = jnp.einsum(
        "rhjp,rjphd->rhd",
        weights,
        picked_values.astype(jnp.float32),
        precision=lax.Precision.HIGHEST,
    )
    peak_rows, masses, gathered_sums = (
        lax.all_gather(local_peak[None], "kv", axis=0, tiled=True),
        lax.all_gather(local_mass[None], "kv", axis=0, tiled=True),
        lax.all_gather(local_sum[None], "kv", axis=0, tiled=True),
    )
    all_peak = jnp.max(peak_rows, axis=0)
    factors = jnp.exp(peak_rows - all_peak[None])
    all_mass = jnp.sum(masses * factors, axis=0)
    all_sum = jnp.sum(gathered_sums * factors[..., None], axis=0)
    decode_attn = (all_sum / all_mass[..., None]).reshape(request_count, D).astype(jnp.bfloat16)
    attn_rows = jnp.concatenate([prefill_attn, decode_attn], axis=0)
    hidden_state = residual.astype(jnp.float32) + jnp.dot(
        attn_rows, w_out, preferred_element_type=jnp.float32
    )
    scaled = (hidden_state * norm_gain).astype(jnp.bfloat16)
    square_sum, logit_parts = lax.psum(
        (
            jnp.sum(hidden_state * hidden_state, axis=1),
            jnp.dot(scaled, router, preferred_element_type=jnp.float32),
        ),
        "kv",
    )
    inv_first = lax.rsqrt(square_sum / D + epsilon)
    logits = logit_parts * inv_first[:, None]
    normed = (hidden_state * norm_gain * inv_first[:, None]).astype(jnp.bfloat16)
    row_count = residual.shape[0]
    expert_count = router.shape[1]
    capacity = min(row_count, 2 * row_count * TOP // expert_count)
    matches = routes[:, :, None] == jnp.arange(expert_count, dtype=jnp.int32)[None, None, :]
    chosen = jnp.sum(jnp.where(matches, logits[:, None, :], 0.0), axis=2)
    raised = jnp.exp(chosen)
    gate_weights = raised / jnp.sum(raised, axis=1, keepdims=True)
    one_hot = matches.reshape(row_count * TOP, expert_count).astype(jnp.int32)
    earlier = jnp.cumsum(one_hot, axis=0) - one_hot
    slot_index = jnp.sum(earlier * one_hot, axis=1)
    target = routes.reshape(-1) * capacity + slot_index
    source_row = jnp.arange(row_count * TOP, dtype=jnp.int32) // TOP
    filler = jnp.zeros((expert_count * capacity,), jnp.int32).at[target].set(source_row)
    present = jnp.zeros((expert_count * capacity,), jnp.bool_).at[target].set(True)
    gate_local = w_gate[0]
    up_local = w_up[0]
    down_local = w_down[0]
    full_rows = lax.all_gather(normed, "kv", axis=1, tiled=True)
    picked = full_rows[filler]
    arrived = lax.all_to_all(
        jnp.where(present[:, None], picked, jnp.zeros_like(picked)).reshape(
            expert_count, capacity, full_rows.shape[1]
        ),
        "ep",
        split_axis=0,
        concat_axis=0,
        tiled=True,
    )
    inbound = arrived.reshape(-1, arrived.shape[2])
    gate_proj = jnp.dot(inbound, gate_local, preferred_element_type=jnp.float32)
    up_proj = jnp.dot(inbound, up_local, preferred_element_type=jnp.float32)
    activation = (jax.nn.silu(gate_proj) * up_proj).astype(jnp.bfloat16)
    feature_cols = residual.shape[1]
    summed = lax.psum_scatter(
        lax.dot_general(
            down_local, activation, (((0,), (1,)), ((), ())), preferred_element_type=jnp.float32
        ).astype(jnp.bfloat16),
        "kv",
        scatter_dimension=0,
        tiled=True,
    ).astype(jnp.float32)
    expert_out = summed.T.astype(jnp.bfloat16).reshape(
        arrived.shape[0], arrived.shape[1], feature_cols
    )
    returned = lax.all_to_all(expert_out, "ep", split_axis=0, concat_axis=0, tiled=True)
    back_rows = (
        returned.reshape(-1, feature_cols)[target]
        .reshape(row_count, TOP, feature_cols)
        .astype(jnp.float32)
    )
    combined = hidden_state + jnp.sum(back_rows * gate_weights[:, :, None], axis=1)
    square_two = lax.psum(jnp.sum(combined * combined, axis=1), "kv")
    return (combined * lax.rsqrt(square_two / D + epsilon)[:, None] * final_gain).astype(
        jnp.bfloat16
    )


def attend(slots_ref, lengths_ref, q_ref, k_ref, v_ref, out_ref, kbuf, vbuf, ksem, vsem):
    requests, pages_each, page_rows = kbuf.shape[:3]
    holder = lax.axis_index("kv")
    holders = lax.axis_size("kv")
    for r in range(requests):
        for j in range(pages_each):
            pltpu.make_async_copy(k_ref.at[slots_ref[r, 0, j]], kbuf.at[r, j], ksem.at[r]).start()
    for r in range(requests):
        for j in range(pages_each):
            pltpu.make_async_copy(v_ref.at[slots_ref[r, 0, j]], vbuf.at[r, j], vsem.at[r]).start()
    tokens = pages_each * page_rows
    wide_row = lax.broadcasted_iota(jnp.int32, (HEAD_DIM, D), 0)
    wide_head = lax.broadcasted_iota(jnp.int32, (HEAD_DIM, D), 1) // HEAD_DIM
    own_head = (wide_row == wide_head)[:HEADS]
    place = lax.broadcasted_iota(jnp.int32, (HEADS, tokens), 1)
    position = ((place // page_rows) * holders + holder) * page_rows + place % page_rows
    queries = q_ref[...].astype(jnp.float32)
    for r in range(requests):
        spread = jnp.where(wide_row == wide_head, queries[r : r + 1, :], 0.0).astype(jnp.bfloat16)
        pltpu.make_async_copy(kbuf.at[r], kbuf.at[r], ksem.at[r]).wait()
        scores = lax.dot_general(
            kbuf[r].reshape(tokens, D),
            spread,
            (((1,), (1,)), ((), ())),
            preferred_element_type=jnp.float32,
        )
        visible = position < lengths_ref[r]
        scores = jnp.where(visible, scores.T[:HEADS] / math.sqrt(HEAD_DIM), floor_score)
        peak = scores.max(axis=1, keepdims=True)
        weight = jnp.where(visible, jnp.exp(scores - peak), 0.0)
        mass = weight.sum(axis=1, keepdims=True)
        high = weight.astype(jnp.bfloat16)
        low = (weight - high.astype(jnp.float32)).astype(jnp.bfloat16)
        pltpu.make_async_copy(vbuf.at[r], vbuf.at[r], vsem.at[r]).wait()
        total = jnp.dot(
            jnp.concatenate([high, low], axis=0),
            vbuf[r].reshape(tokens, D),
            preferred_element_type=jnp.float32,
        )
        both = total[:HEADS] + total[HEADS:]
        for n, part in enumerate((both, peak, mass)):
            row = n * requests + r
            out_ref[row : row + 1, :] = jnp.sum(
                jnp.where(own_head, part, 0.0), axis=0, keepdims=True
            )


def local_attention(queries, key_pool, value_pool, page_table, lengths):
    requests, _, pages_each = page_table.shape
    held = (requests, pages_each) + key_pool.shape[1:]
    smem = pl.BlockSpec(memory_space=pltpu.SMEM)
    vmem = pl.BlockSpec(memory_space=pltpu.VMEM)
    hbm = pl.BlockSpec(memory_space=pl.ANY)
    return pl.pallas_call(
        attend,
        out_shape=jax.ShapeDtypeStruct((3 * requests, D), jnp.float32),
        in_specs=[smem, smem, vmem, hbm, hbm],
        out_specs=vmem,
        scratch_shapes=[
            pltpu.VMEM(held, jnp.bfloat16),
            pltpu.VMEM(held, jnp.bfloat16),
            pltpu.SemaphoreType.DMA((requests,)),
            pltpu.SemaphoreType.DMA((requests,)),
        ],
        compiler_params=pltpu.CompilerParams(vmem_limit_bytes=60 * 2**20),
        cost_estimate=pl.CostEstimate(flops=4 * 10**8, bytes_accessed=7 * 2**20, transcendentals=0),
        name="local_attention",
    )(page_table, lengths, queries, key_pool, value_pool)


LABELS = ((0, 0), (0, 1), (1, 0), (1, 1))


def where_held(a, b, path):
    if a == b:
        return a, a
    if a == 1:
        return path, 1 - path
    return 1 - path, path


def expert_kernel(side_ref, gate_ref, up_ref, down_ref, *rest):
    blocks = rest[:8]
    outs = rest[8:16]
    xbuf, obuf, gbuf, ubuf, dbuf, wsem, xsem, osem = rest[16:]
    holder, core = lax.axis_index("kv"), lax.axis_index("ep") % 2
    pair = blocks[0].shape[0]
    cols = xbuf.shape[4]
    rows = 2 * pair * xbuf.shape[3]
    halves = (holder, 1 - holder)
    paths = (core, 1 - core)

    def fetch(d, labels):
        for a, b in labels:
            t, f = where_held(a, b, paths[d])
            pltpu.make_async_copy(
                blocks[4 * d + 2 * a + b], xbuf.at[d, f, pl.ds(t * pair, pair)], xsem.at[d, f]
            ).start()

    def load(source, buffer, kind, f):
        pltpu.make_async_copy(source.at[halves[f]], buffer.at[f], wsem.at[kind, f]).start()

    fetch(0, LABELS)
    load(gate_ref, gbuf, 0, 0)
    load(gate_ref, gbuf, 0, 1)
    load(up_ref, ubuf, 1, 0)
    load(up_ref, ubuf, 1, 1)
    for f in range(2):
        start = pl.multiple_of(halves[f] * cols, cols)
        pltpu.make_async_copy(
            down_ref.at[:, pl.ds(start, cols)], dbuf.at[f], wsem.at[2, f]
        ).start()
    fetch(1, LABELS)

    def ready(d, buffer, kind, f):
        if d == 0:
            pltpu.make_async_copy(buffer.at[f], buffer.at[f], wsem.at[kind, f]).wait()

    def came(d, f):
        pltpu.make_async_copy(xbuf.at[d, f], xbuf.at[d, f], xsem.at[d, f]).wait()

    side = side_ref[...].T
    for d in range(2):
        came(d, 0)
        first = xbuf[d, 0].reshape(rows, cols)
        ready(d, gbuf, 0, 0)
        gate = jnp.dot(first, gbuf[0], preferred_element_type=jnp.float32)
        came(d, 1)
        second = xbuf[d, 1].reshape(rows, cols)
        ready(d, gbuf, 0, 1)
        gate += jnp.dot(second, gbuf[1], preferred_element_type=jnp.float32)
        groups = range(2 * pair * d, 2 * pair * (d + 1))
        scale = jnp.concatenate([side[:, g : g + 1] for g in groups])
        share = jnp.concatenate([side[:, 4 * pair + g : 4 * pair + g + 1] for g in groups])
        gate *= scale
        ready(d, ubuf, 1, 0)
        up = jnp.dot(first, ubuf[0], preferred_element_type=jnp.float32)
        ready(d, ubuf, 1, 1)
        up += jnp.dot(second, ubuf[1], preferred_element_type=jnp.float32)
        up *= scale
        act = (gate / (1.0 + jnp.exp(-gate)) * up).astype(jnp.bfloat16)
        for f in range(2):
            ready(d, dbuf, 2, f)
            out = jnp.dot(act, dbuf[f], preferred_element_type=jnp.float32) * share
            obuf[d, f] = out.astype(jnp.bfloat16).reshape(2 * pair, -1, cols)
        for n, (a, b) in enumerate(LABELS):
            t, f = where_held(a, b, paths[d])
            pltpu.make_async_copy(
                obuf.at[d, f, pl.ds(t * pair, pair)], outs[4 * d + n], osem.at[4 * d + n]
            ).start()
    for n in range(8):
        pltpu.make_async_copy(obuf.at[0, 0, pl.ds(0, pair)], outs[n], osem.at[n]).wait()


def run_experts(side, gate, up, down, blocks):
    pair, row_count, cols = blocks[0].shape
    hidden = gate.shape[2]
    vmem = pl.BlockSpec(memory_space=pltpu.VMEM)
    hbm = pl.BlockSpec(memory_space=pl.ANY)
    return pl.pallas_call(
        expert_kernel,
        out_shape=[jax.ShapeDtypeStruct(blocks[0].shape, jnp.bfloat16)] * 8,
        in_specs=[vmem, hbm, hbm, hbm] + [hbm] * 8,
        out_specs=[hbm] * 8,
        scratch_shapes=[
            pltpu.VMEM((2, 2, 2 * pair, row_count, cols), jnp.bfloat16),
            pltpu.VMEM((2, 2, 2 * pair, row_count, cols), jnp.bfloat16),
            pltpu.VMEM((2, cols, hidden), jnp.bfloat16),
            pltpu.VMEM((2, cols, hidden), jnp.bfloat16),
            pltpu.VMEM((2, hidden, cols), jnp.bfloat16),
            pltpu.SemaphoreType.DMA((3, 2)),
            pltpu.SemaphoreType.DMA((2, 2)),
            pltpu.SemaphoreType.DMA((8,)),
        ],
        compiler_params=pltpu.CompilerParams(vmem_limit_bytes=60 * 2**20),
        cost_estimate=pl.CostEstimate(
            flops=4 * pair * row_count * 12 * cols * hidden,
            bytes_accessed=pair * row_count * cols * 32 + 12 * cols * hidden,
            transcendentals=0,
        ),
        name="experts",
    )(side, gate, up, down, *blocks)


def add(first, second):
    return (first.astype(jnp.float32) + second.astype(jnp.float32)).astype(jnp.bfloat16)


def dense(
    queries,
    key_pool,
    value_pool,
    page_table,
    lengths,
    prefill_attn,
    residual,
    w_out,
    norm_gain,
    router,
    w_gate,
    w_up,
    w_down,
    final_gain,
    routes,
):
    request_count = queries.shape[0]
    row_count, cols = residual.shape
    expert_count = router.shape[1]
    ep_size = lax.axis_size("ep")
    depth = ep_size // 4
    axes = ("ep", "kv")

    def number(z, y, c, x):
        return ((z * 2 + y) * 2 + c) * 2 + x

    places = [(z, y, c, x) for z in range(depth) for y in range(2) for c in range(2) for x in range(2)]

    def sent(array, target):
        return lax.ppermute(array, axes, [(number(*p), number(*target(*p))) for p in places])

    def across(array):
        return sent(array, lambda z, y, c, x: (z, y, c, 1 - x))

    def along(array, s):
        return sent(array, lambda z, y, c, x: ((z + s) % depth, y, c, x))

    def hop_one(array):
        return sent(array, lambda z, y, c, x: (z, y, c, 1 - x) if c == 0 else (z, 1 - y, c, x))

    def hop_two(array):
        return sent(array, lambda z, y, c, x: (z, 1 - y, c, x) if c == 0 else (z, y, c, 1 - x))

    def sibling(array):
        return sent(array, lambda z, y, c, x: (z, y, 1 - c, x))

    def fence(*values):
        return lax.optimization_barrier(values)

    local = local_attention(queries, key_pool, value_pool, page_table, lengths)
    other = across(local)
    sum_one, sum_two = local[:request_count], other[:request_count]
    peak_one, peak_two = (v[request_count : 2 * request_count] for v in (local, other))
    mass_one, mass_two = (v[2 * request_count :] for v in (local, other))
    peak = jnp.maximum(peak_one, peak_two)
    factor_one, factor_two = jnp.exp(peak_one - peak), jnp.exp(peak_two - peak)
    decode_attn = (sum_one * factor_one + sum_two * factor_two) / (
        mass_one * factor_one + mass_two * factor_two
    )
    attn_rows = jnp.concatenate([prefill_attn, decode_attn.astype(jnp.bfloat16)], axis=0)
    hidden_state = residual.astype(jnp.float32) + jnp.dot(
        attn_rows, w_out, preferred_element_type=jnp.float32
    )
    scaled = (hidden_state * norm_gain).astype(jnp.bfloat16)

    square_part = jnp.sum(hidden_state * hidden_state, axis=1)
    logit_part = jnp.dot(scaled, router, preferred_element_type=jnp.float32)
    stats = jnp.concatenate([logit_part, square_part[:, None]], axis=1).T

    slots = ((0, 1), (3, 2))
    far_one = along(scaled, 1)
    stats = stats + across(stats)
    far_one, scaled = fence(far_one, scaled)

    pair = jnp.stack([scaled, far_one])
    far_three, one, pair_s = along(scaled, 3), hop_one(pair), sibling(pair)
    inv_first = lax.rsqrt(stats[expert_count] / D + epsilon)
    logits = stats[:expert_count].T * inv_first[:, None]
    matches = routes[:, :, None] == jnp.arange(expert_count, dtype=jnp.int32)[None, None, :]
    chosen = jnp.sum(jnp.where(matches, logits[:, None, :], 0.0), axis=2)
    raised = jnp.exp(chosen)
    gate_weights = raised / jnp.sum(raised, axis=1, keepdims=True)
    by_expert = jnp.sum(jnp.where(matches, gate_weights[:, :, None], 0.0), axis=1)
    side = jnp.concatenate([by_expert, inv_first[:, None]], axis=1).T[None]
    side_s = sibling(side)
    far_three, one, pair_s, pair, scaled, side_s = fence(
        far_three, one, pair_s, pair, scaled, side_s
    )

    far_two, two, three, one_s = along(scaled, 2), hop_two(pair), hop_two(one), sibling(one)
    side = jnp.concatenate([side, side_s], axis=0)
    side_y = sent(side, lambda z, y, c, x: (z, 1 - y, c, x))
    far_two, far_three, two, three, one_s, pair, one, side_y = fence(
        far_two, far_three, two, three, one_s, pair, one, side_y
    )

    later = jnp.stack([far_three, far_two])
    later_one, two_s, three_s = hop_one(later), sibling(two), sibling(three)
    side = jnp.concatenate([side, side_y], axis=0)
    sides = [side] + [along(side, s) for s in range(1, depth)]
    own = lax.axis_index("ep")

    held = jnp.stack(sides)
    share = lax.dynamic_index_in_dim(held, own, axis=2, keepdims=False)
    held = jnp.stack([held[:, :, expert_count], share]).reshape(2, depth, 2, 2, row_count)
    both = [
        jnp.stack([held[:, s] for s in chunk], axis=1).transpose(0, 3, 2, 1, 4).reshape(-1, row_count)
        for chunk in slots
    ]
    later_one, two_s, three_s, later, both = fence(later_one, two_s, three_s, later, both)

    gate_local = w_gate[0].reshape(2, cols, -1)
    up_local = w_up[0].reshape(2, cols, -1)
    down_local = w_down[0]
    later_two, later_three = hop_two(later), hop_two(later_one)
    later_s, later_one_s = sibling(later), sibling(later_one)
    blocks = (pair, two, one, three, pair_s, two_s, one_s, three_s)
    made = run_experts(both[0], gate_local, up_local, down_local, blocks)
    later_two, later_three, later_one_s, later_s, later, later_one, made = fence(
        later_two, later_three, later_one_s, later_s, later, later_one, made
    )

    later_two_s, later_three_s = sibling(later_two), sibling(later_three)
    got = [add(made[m], sibling(made[4 + m])) for m in range(4)]
    later_two_s, later_three_s, got = fence(later_two_s, later_three_s, got)

    from_one, from_three = hop_two(got[1]), hop_two(got[3])
    blocks = (later, later_two, later_one, later_three)
    blocks += (later_s, later_two_s, later_one_s, later_three_s)
    made = run_experts(both[1], gate_local, up_local, down_local, blocks)
    from_one, from_three, made = fence(from_one, from_three, made)

    near, far = add(got[0], from_one), add(got[2], from_three)
    moved = hop_one(far)
    back = [sibling(made[4 + m]) for m in range(4)]
    got = [[add(made[m][i], back[m][i]) for m in range(4)] for i in range(2)]
    moved, near, got = fence(moved, near, got)

    whole = add(near, moved)
    part_one = along(whole[1], depth - 1)
    (three_got, two_got) = got
    two_parts = hop_two(two_got[1]), hop_two(two_got[3])
    three_parts = hop_two(three_got[1]), hop_two(three_got[3])
    part_one, two_parts = fence(part_one, two_parts)
    combined = hidden_state + whole[0].astype(jnp.float32) + part_one.astype(jnp.float32)
    moved = hop_one(add(two_got[2], two_parts[1]))
    moved, three_parts = fence(moved, three_parts)
    part_two = along(add(add(two_got[0], two_parts[0]), moved), depth - 2)
    moved = hop_one(add(three_got[2], three_parts[1]))
    part_three = along(add(add(three_got[0], three_parts[0]), moved), depth - 3)
    combined = combined + part_two.astype(jnp.float32) + part_three.astype(jnp.float32)
    square_two = jnp.sum(combined * combined, axis=1)[None, :]
    square_two = (square_two + across(square_two))[0]
    return (combined * lax.rsqrt(square_two / D + epsilon)[:, None] * final_gain).astype(
        jnp.bfloat16
    )


def per_device(*arrays):
    row_count, expert_count = arrays[6].shape[0], arrays[9].shape[1]
    capacity = min(row_count, 2 * row_count * TOP // expert_count)
    fits = lax.axis_size("kv") == 2 and lax.axis_size("ep") == 16
    if capacity == row_count and fits:
        return dense(*arrays)
    return routed(*arrays)


def solution(mesh):
    placed = (
        P("ep", None),
        P(("ep", "kv"), None, None),
        P(("ep", "kv"), None, None),
        P("ep", "kv", None),
        P("ep"),
        P("ep", None),
        P("ep", "kv"),
        P(None, "kv"),
        P("kv"),
        P("kv", None),
        P("ep", None, "kv"),
        P("ep", None, "kv"),
        P("ep", "kv", None),
        P("kv"),
        P("ep", None),
    )
    return jax.shard_map(
        per_device, mesh=mesh, in_specs=placed, out_specs=P("ep", "kv"), check_vma=False
    )
```

```python
import math

import jax
import jax.numpy as jnp
from jax import lax
from jax.experimental import pallas as pl
from jax.experimental.pallas import tpu as pltpu
from jax.sharding import PartitionSpec as P

D = 2048
HEADS = 16
HEAD_DIM = 128
TOP = 8


epsilon = 1e-06
floor_score = -1e30


def routed(
    queries,
    key_pool,
    value_pool,
    page_table,
    lengths,
    prefill_attn,
    residual,
    w_out,
    norm_gain,
    router,
    w_gate,
    w_up,
    w_down,
    final_gain,
    routes,
):
    holders = lax.axis_size("kv")
    holder = lax.axis_index("kv")
    request_count = queries.shape[0]
    pool_pages = key_pool.shape[0]
    page_rows = key_pool.shape[1]
    pages_each = page_table.shape[2]
    query_heads = queries.reshape(request_count, HEADS, HEAD_DIM)
    page_slots = page_table[:, 0, :]
    picked_keys = key_pool.reshape(pool_pages, page_rows, HEADS, HEAD_DIM)[page_slots]
    picked_values = value_pool.reshape(pool_pages, page_rows, HEADS, HEAD_DIM)[page_slots]
    scores = jnp.einsum(
        "rhd,rjphd->rhjp", query_heads, picked_keys, preferred_element_type=jnp.float32
    ) / math.sqrt(HEAD_DIM)
    page_number = jnp.arange(pages_each, dtype=jnp.int32) * holders + holder
    position = page_number[:, None] * page_rows + jnp.arange(page_rows, dtype=jnp.int32)[None, :]
    visible = position[None, None, :, :] < lengths[:, None, None, None]
    masked = jnp.where(visible, scores, floor_score)
    local_peak = jnp.max(masked, axis=(2, 3))
    weights = jnp.where(visible, jnp.exp(masked - local_peak[:, :, None, None]), 0.0)
    local_mass = jnp.sum(weights, axis=(2, 3))
    local_sum = jnp.einsum(
        "rhjp,rjphd->rhd",
        weights,
        picked_values.astype(jnp.float32),
        precision=lax.Precision.HIGHEST,
    )
    peak_rows, masses, gathered_sums = (
        lax.all_gather(local_peak[None], "kv", axis=0, tiled=True),
        lax.all_gather(local_mass[None], "kv", axis=0, tiled=True),
        lax.all_gather(local_sum[None], "kv", axis=0, tiled=True),
    )
    all_peak = jnp.max(peak_rows, axis=0)
    factors = jnp.exp(peak_rows - all_peak[None])
    all_mass = jnp.sum(masses * factors, axis=0)
    all_sum = jnp.sum(gathered_sums * factors[..., None], axis=0)
    decode_attn = (all_sum / all_mass[..., None]).reshape(request_count, D).astype(jnp.bfloat16)
    attn_rows = jnp.concatenate([prefill_attn, decode_attn], axis=0)
    hidden_state = residual.astype(jnp.float32) + jnp.dot(
        attn_rows, w_out, preferred_element_type=jnp.float32
    )
    scaled = (hidden_state * norm_gain).astype(jnp.bfloat16)
    square_sum, logit_parts = lax.psum(
        (
            jnp.sum(hidden_state * hidden_state, axis=1),
            jnp.dot(scaled, router, preferred_element_type=jnp.float32),
        ),
        "kv",
    )
    inv_first = lax.rsqrt(square_sum / D + epsilon)
    logits = logit_parts * inv_first[:, None]
    normed = (hidden_state * norm_gain * inv_first[:, None]).astype(jnp.bfloat16)
    row_count = residual.shape[0]
    expert_count = router.shape[1]
    capacity = min(row_count, 2 * row_count * TOP // expert_count)
    matches = routes[:, :, None] == jnp.arange(expert_count, dtype=jnp.int32)[None, None, :]
    chosen = jnp.sum(jnp.where(matches, logits[:, None, :], 0.0), axis=2)
    raised = jnp.exp(chosen)
    gate_weights = raised / jnp.sum(raised, axis=1, keepdims=True)
    one_hot = matches.reshape(row_count * TOP, expert_count).astype(jnp.int32)
    earlier = jnp.cumsum(one_hot, axis=0) - one_hot
    slot_index = jnp.sum(earlier * one_hot, axis=1)
    target = routes.reshape(-1) * capacity + slot_index
    source_row = jnp.arange(row_count * TOP, dtype=jnp.int32) // TOP
    filler = jnp.zeros((expert_count * capacity,), jnp.int32).at[target].set(source_row)
    present = jnp.zeros((expert_count * capacity,), jnp.bool_).at[target].set(True)
    gate_local = w_gate[0]
    up_local = w_up[0]
    down_local = w_down[0]
    full_rows = lax.all_gather(normed, "kv", axis=1, tiled=True)
    picked = full_rows[filler]
    arrived = lax.all_to_all(
        jnp.where(present[:, None], picked, jnp.zeros_like(picked)).reshape(
            expert_count, capacity, full_rows.shape[1]
        ),
        "ep",
        split_axis=0,
        concat_axis=0,
        tiled=True,
    )
    inbound = arrived.reshape(-1, arrived.shape[2])
    gate_proj = jnp.dot(inbound, gate_local, preferred_element_type=jnp.float32)
    up_proj = jnp.dot(inbound, up_local, preferred_element_type=jnp.float32)
    activation = (jax.nn.silu(gate_proj) * up_proj).astype(jnp.bfloat16)
    feature_cols = residual.shape[1]
    summed = lax.psum_scatter(
        lax.dot_general(
            down_local, activation, (((0,), (1,)), ((), ())), preferred_element_type=jnp.float32
        ).astype(jnp.bfloat16),
        "kv",
        scatter_dimension=0,
        tiled=True,
    ).astype(jnp.float32)
    expert_out = summed.T.astype(jnp.bfloat16).reshape(
        arrived.shape[0], arrived.shape[1], feature_cols
    )
    returned = lax.all_to_all(expert_out, "ep", split_axis=0, concat_axis=0, tiled=True)
    back_rows = (
        returned.reshape(-1, feature_cols)[target]
        .reshape(row_count, TOP, feature_cols)
        .astype(jnp.float32)
    )
    combined = hidden_state + jnp.sum(back_rows * gate_weights[:, :, None], axis=1)
    square_two = lax.psum(jnp.sum(combined * combined, axis=1), "kv")
    return (combined * lax.rsqrt(square_two / D + epsilon)[:, None] * final_gain).astype(
        jnp.bfloat16
    )


def attend(slots_ref, lengths_ref, q_ref, k_ref, v_ref, out_ref, kbuf, vbuf, ksem, vsem):
    requests, pages_each, page_rows = kbuf.shape[:3]
    holder = lax.axis_index("kv")
    holders = lax.axis_size("kv")
    for r in range(requests):
        for j in range(pages_each):
            pltpu.make_async_copy(k_ref.at[slots_ref[r, 0, j]], kbuf.at[r, j], ksem.at[r]).start()
    for r in range(requests):
        for j in range(pages_each):
            pltpu.make_async_copy(v_ref.at[slots_ref[r, 0, j]], vbuf.at[r, j], vsem.at[r]).start()
    tokens = pages_each * page_rows
    wide_row = lax.broadcasted_iota(jnp.int32, (HEAD_DIM, D), 0)
    wide_head = lax.broadcasted_iota(jnp.int32, (HEAD_DIM, D), 1) // HEAD_DIM
    own_head = (wide_row == wide_head)[:HEADS]
    place = lax.broadcasted_iota(jnp.int32, (HEADS, tokens), 1)
    position = ((place // page_rows) * holders + holder) * page_rows + place % page_rows
    queries = q_ref[...].astype(jnp.float32)
    for r in range(requests):
        spread = jnp.where(wide_row == wide_head, queries[r : r + 1, :], 0.0).astype(jnp.bfloat16)
        pltpu.make_async_copy(kbuf.at[r], kbuf.at[r], ksem.at[r]).wait()
        scores = lax.dot_general(
            kbuf[r].reshape(tokens, D),
            spread,
            (((1,), (1,)), ((), ())),
            preferred_element_type=jnp.float32,
        )
        visible = position < lengths_ref[r]
        scores = jnp.where(visible, scores.T[:HEADS] / math.sqrt(HEAD_DIM), floor_score)
        peak = scores.max(axis=1, keepdims=True)
        weight = jnp.where(visible, jnp.exp(scores - peak), 0.0)
        mass = weight.sum(axis=1, keepdims=True)
        high = weight.astype(jnp.bfloat16)
        low = (weight - high.astype(jnp.float32)).astype(jnp.bfloat16)
        pltpu.make_async_copy(vbuf.at[r], vbuf.at[r], vsem.at[r]).wait()
        total = jnp.dot(
            jnp.concatenate([high, low], axis=0),
            vbuf[r].reshape(tokens, D),
            preferred_element_type=jnp.float32,
        )
        both = total[:HEADS] + total[HEADS:]
        for n, part in enumerate((both, peak, mass)):
            row = n * requests + r
            out_ref[row : row + 1, :] = jnp.sum(
                jnp.where(own_head, part, 0.0), axis=0, keepdims=True
            )


def local_attention(queries, key_pool, value_pool, page_table, lengths):
    requests, _, pages_each = page_table.shape
    held = (requests, pages_each) + key_pool.shape[1:]
    smem = pl.BlockSpec(memory_space=pltpu.SMEM)
    vmem = pl.BlockSpec(memory_space=pltpu.VMEM)
    hbm = pl.BlockSpec(memory_space=pl.ANY)
    return pl.pallas_call(
        attend,
        out_shape=jax.ShapeDtypeStruct((3 * requests, D), jnp.float32),
        in_specs=[smem, smem, vmem, hbm, hbm],
        out_specs=vmem,
        scratch_shapes=[
            pltpu.VMEM(held, jnp.bfloat16),
            pltpu.VMEM(held, jnp.bfloat16),
            pltpu.SemaphoreType.DMA((requests,)),
            pltpu.SemaphoreType.DMA((requests,)),
        ],
        compiler_params=pltpu.CompilerParams(vmem_limit_bytes=60 * 2**20),
        cost_estimate=pl.CostEstimate(flops=4 * 10**8, bytes_accessed=7 * 2**20, transcendentals=0),
        name="local_attention",
    )(page_table, lengths, queries, key_pool, value_pool)


LABELS = ((0, 0), (0, 1), (1, 0), (1, 1))


def where_held(a, b, path):
    if a == b:
        return a, a
    if a == 1:
        return path, 1 - path
    return 1 - path, path


def expert_kernel(side_ref, gate_ref, up_ref, down_ref, *rest):
    blocks = rest[:8]
    outs = rest[8:16]
    xbuf, obuf, gbuf, ubuf, dbuf, wsem, xsem, osem = rest[16:]
    holder, core = lax.axis_index("kv"), lax.axis_index("ep") % 2
    pair = blocks[0].shape[0]
    cols = xbuf.shape[4]
    rows = 2 * pair * xbuf.shape[3]
    halves = (holder, 1 - holder)
    paths = (core, 1 - core)

    def fetch(d, labels):
        for a, b in labels:
            t, f = where_held(a, b, paths[d])
            pltpu.make_async_copy(
                blocks[4 * d + 2 * a + b], xbuf.at[d, f, pl.ds(t * pair, pair)], xsem.at[d, f]
            ).start()

    def load(source, buffer, kind, f):
        pltpu.make_async_copy(source.at[halves[f]], buffer.at[f], wsem.at[kind, f]).start()

    fetch(0, LABELS)
    load(gate_ref, gbuf, 0, 0)
    load(gate_ref, gbuf, 0, 1)
    load(up_ref, ubuf, 1, 0)
    load(up_ref, ubuf, 1, 1)
    for f in range(2):
        start = pl.multiple_of(halves[f] * cols, cols)
        pltpu.make_async_copy(
            down_ref.at[:, pl.ds(start, cols)], dbuf.at[f], wsem.at[2, f]
        ).start()
    fetch(1, LABELS)

    def ready(d, buffer, kind, f):
        if d == 0:
            pltpu.make_async_copy(buffer.at[f], buffer.at[f], wsem.at[kind, f]).wait()

    def came(d, f):
        pltpu.make_async_copy(xbuf.at[d, f], xbuf.at[d, f], xsem.at[d, f]).wait()

    side = side_ref[...].T
    for d in range(2):
        came(d, 0)
        first = xbuf[d, 0].reshape(rows, cols)
        ready(d, gbuf, 0, 0)
        gate = jnp.dot(first, gbuf[0], preferred_element_type=jnp.float32)
        came(d, 1)
        second = xbuf[d, 1].reshape(rows, cols)
        ready(d, gbuf, 0, 1)
        gate += jnp.dot(second, gbuf[1], preferred_element_type=jnp.float32)
        groups = range(2 * pair * d, 2 * pair * (d + 1))
        scale = jnp.concatenate([side[:, g : g + 1] for g in groups])
        share = jnp.concatenate([side[:, 4 * pair + g : 4 * pair + g + 1] for g in groups])
        gate *= scale
        ready(d, ubuf, 1, 0)
        up = jnp.dot(first, ubuf[0], preferred_element_type=jnp.float32)
        ready(d, ubuf, 1, 1)
        up += jnp.dot(second, ubuf[1], preferred_element_type=jnp.float32)
        up *= scale
        act = (gate / (1.0 + jnp.exp(-gate)) * up).astype(jnp.bfloat16)
        for f in range(2):
            ready(d, dbuf, 2, f)
            out = jnp.dot(act, dbuf[f], preferred_element_type=jnp.float32) * share
            obuf[d, f] = out.astype(jnp.bfloat16).reshape(2 * pair, -1, cols)
        for n, (a, b) in enumerate(LABELS):
            t, f = where_held(a, b, paths[d])
            pltpu.make_async_copy(
                obuf.at[d, f, pl.ds(t * pair, pair)], outs[4 * d + n], osem.at[4 * d + n]
            ).start()
    for n in range(8):
        pltpu.make_async_copy(obuf.at[0, 0, pl.ds(0, pair)], outs[n], osem.at[n]).wait()


def run_experts(side, gate, up, down, blocks):
    pair, row_count, cols = blocks[0].shape
    hidden = gate.shape[2]
    vmem = pl.BlockSpec(memory_space=pltpu.VMEM)
    hbm = pl.BlockSpec(memory_space=pl.ANY)
    return pl.pallas_call(
        expert_kernel,
        out_shape=[jax.ShapeDtypeStruct(blocks[0].shape, jnp.bfloat16)] * 8,
        in_specs=[vmem, hbm, hbm, hbm] + [hbm] * 8,
        out_specs=[hbm] * 8,
        scratch_shapes=[
            pltpu.VMEM((2, 2, 2 * pair, row_count, cols), jnp.bfloat16),
            pltpu.VMEM((2, 2, 2 * pair, row_count, cols), jnp.bfloat16),
            pltpu.VMEM((2, cols, hidden), jnp.bfloat16),
            pltpu.VMEM((2, cols, hidden), jnp.bfloat16),
            pltpu.VMEM((2, hidden, cols), jnp.bfloat16),
            pltpu.SemaphoreType.DMA((3, 2)),
            pltpu.SemaphoreType.DMA((2, 2)),
            pltpu.SemaphoreType.DMA((8,)),
        ],
        compiler_params=pltpu.CompilerParams(vmem_limit_bytes=60 * 2**20),
        cost_estimate=pl.CostEstimate(
            flops=4 * pair * row_count * 12 * cols * hidden,
            bytes_accessed=pair * row_count * cols * 32 + 12 * cols * hidden,
            transcendentals=0,
        ),
        name="experts",
    )(side, gate, up, down, *blocks)


def add(first, second):
    return (first.astype(jnp.float32) + second.astype(jnp.float32)).astype(jnp.bfloat16)


def dense(
    queries,
    key_pool,
    value_pool,
    page_table,
    lengths,
    prefill_attn,
    residual,
    w_out,
    norm_gain,
    router,
    w_gate,
    w_up,
    w_down,
    final_gain,
    routes,
):
    request_count = queries.shape[0]
    row_count, cols = residual.shape
    expert_count = router.shape[1]
    ep_size = lax.axis_size("ep")
    depth = ep_size // 4
    axes = ("ep", "kv")

    def number(z, y, c, x):
        return ((z * 2 + y) * 2 + c) * 2 + x

    places = [(z, y, c, x) for z in range(depth) for y in range(2) for c in range(2) for x in range(2)]

    def sent(array, target):
        return lax.ppermute(array, axes, [(number(*p), number(*target(*p))) for p in places])

    def across(array):
        return sent(array, lambda z, y, c, x: (z, y, c, 1 - x))

    def along(array, s):
        return sent(array, lambda z, y, c, x: ((z + s) % depth, y, c, x))

    def hop_one(array):
        return sent(array, lambda z, y, c, x: (z, y, c, 1 - x) if c == 0 else (z, 1 - y, c, x))

    def hop_two(array):
        return sent(array, lambda z, y, c, x: (z, 1 - y, c, x) if c == 0 else (z, y, c, 1 - x))

    def sibling(array):
        return sent(array, lambda z, y, c, x: (z, y, 1 - c, x))

    def fence(*values):
        return lax.optimization_barrier(values)

    early = (row_count - request_count) // 16 * 16

    def hidden_of(rows, part):
        product = jnp.dot(rows, w_out, preferred_element_type=jnp.float32)
        state = residual[part].astype(jnp.float32) + product
        return state, (state * norm_gain).astype(jnp.bfloat16)

    first_hidden, first_scaled = hidden_of(prefill_attn[:early], slice(0, early))
    first_one = along(first_scaled, 1)
    local = local_attention(queries, key_pool, value_pool, page_table, lengths)
    first_one, local, first_scaled = fence(first_one, local, first_scaled)

    first_two = along(first_scaled, 2)
    other = across(local)
    sum_one, sum_two = local[:request_count], other[:request_count]
    peak_one, peak_two = (v[request_count : 2 * request_count] for v in (local, other))
    mass_one, mass_two = (v[2 * request_count :] for v in (local, other))
    peak = jnp.maximum(peak_one, peak_two)
    factor_one, factor_two = jnp.exp(peak_one - peak), jnp.exp(peak_two - peak)
    decode_attn = (sum_one * factor_one + sum_two * factor_two) / (
        mass_one * factor_one + mass_two * factor_two
    )
    last_rows = jnp.concatenate([prefill_attn[early:], decode_attn.astype(jnp.bfloat16)], axis=0)
    last_hidden, last_scaled = hidden_of(last_rows, slice(early, row_count))
    first_two, last_scaled, last_hidden = fence(first_two, last_scaled, last_hidden)

    hidden_state = jnp.concatenate([first_hidden, last_hidden], axis=0)
    scaled = jnp.concatenate([first_scaled, last_scaled], axis=0)
    square_part = jnp.sum(hidden_state * hidden_state, axis=1)
    logit_part = jnp.dot(scaled, router, preferred_element_type=jnp.float32)
    stats = jnp.concatenate([logit_part, square_part[:, None]], axis=1).T

    slots = ((1, 2), (3, 0))
    last_one, last_two = along(last_scaled, 1), along(last_scaled, 2)
    stats = stats + across(stats)
    last_one, last_two, stats, scaled = fence(last_one, last_two, stats, scaled)

    pair = jnp.stack(
        [
            jnp.concatenate([first_one, last_one], axis=0),
            jnp.concatenate([first_two, last_two], axis=0),
        ]
    )
    far_three, one = along(scaled, 3), hop_one(pair)
    inv_first = lax.rsqrt(stats[expert_count] / D + epsilon)
    logits = stats[:expert_count].T * inv_first[:, None]
    matches = routes[:, :, None] == jnp.arange(expert_count, dtype=jnp.int32)[None, None, :]
    chosen = jnp.sum(jnp.where(matches, logits[:, None, :], 0.0), axis=2)
    raised = jnp.exp(chosen)
    gate_weights = raised / jnp.sum(raised, axis=1, keepdims=True)
    by_expert = jnp.sum(jnp.where(matches, gate_weights[:, :, None], 0.0), axis=1)
    side = jnp.concatenate([by_expert, inv_first[:, None]], axis=1).T[None]
    side_s = sibling(side)
    side_y = sent(side, lambda z, y, c, x: (z, 1 - y, c, x))
    side_ys = sent(side, lambda z, y, c, x: (z, 1 - y, 1 - c, x))
    far_three, one, pair, scaled, side, side_s, side_y, side_ys = fence(
        far_three, one, pair, scaled, side, side_s, side_y, side_ys
    )

    two, three, one_s, pair_s = hop_two(pair), hop_two(one), sibling(one), sibling(pair)
    side = jnp.concatenate([side, side_s, side_y, side_ys], axis=0)
    sides = [side] + [along(side, s) for s in range(1, depth)]
    two, three, one_s, pair_s, sides = fence(two, three, one_s, pair_s, sides)

    later = jnp.stack([far_three, scaled])
    later_one, two_s, three_s = hop_one(later), sibling(two), sibling(three)
    own = lax.axis_index("ep")

    held = jnp.stack(sides)
    share = lax.dynamic_index_in_dim(held, own, axis=2, keepdims=False)
    held = jnp.stack([held[:, :, expert_count], share]).reshape(2, depth, 2, 2, row_count)
    both = [
        jnp.stack([held[:, s] for s in chunk], axis=1).transpose(0, 3, 2, 1, 4).reshape(-1, row_count)
        for chunk in slots
    ]
    later_one, two_s, three_s, later, both = fence(later_one, two_s, three_s, later, both)

    gate_local = w_gate[0].reshape(2, cols, -1)
    up_local = w_up[0].reshape(2, cols, -1)
    down_local = w_down[0]
    later_two, later_three = hop_two(later), hop_two(later_one)
    later_s, later_one_s = sibling(later), sibling(later_one)
    blocks = (pair, two, one, three, pair_s, two_s, one_s, three_s)
    made = run_experts(both[0], gate_local, up_local, down_local, blocks)
    later_two, later_three, later_one_s, later_s, later, later_one, made = fence(
        later_two, later_three, later_one_s, later_s, later, later_one, made
    )

    later_two_s, later_three_s = sibling(later_two), sibling(later_three)
    got = [add(made[m], sibling(made[4 + m])) for m in range(4)]
    later_two_s, later_three_s, got = fence(later_two_s, later_three_s, got)

    from_one, from_three = hop_two(got[1]), hop_two(got[3])
    blocks = (later, later_two, later_one, later_three)
    blocks += (later_s, later_two_s, later_one_s, later_three_s)
    made = run_experts(both[1], gate_local, up_local, down_local, blocks)
    from_one, from_three, made = fence(from_one, from_three, made)

    near, far = add(got[0], from_one), add(got[2], from_three)
    moved = hop_one(far)
    back = [sibling(made[4 + m]) for m in range(4)]
    got = [[add(made[m][i], back[m][i]) for m in range(4)] for i in range(2)]
    moved, near, got = fence(moved, near, got)

    whole = add(near, moved)
    part_one, part_two = along(whole[0], depth - 1), along(whole[1], depth - 2)
    (three_got, zero_got) = got
    three_parts = hop_two(three_got[1]), hop_two(three_got[3])
    zero_parts = hop_two(zero_got[1]), hop_two(zero_got[3])
    part_one, three_parts = fence(part_one, three_parts)
    moved = hop_one(add(three_got[2], three_parts[1]))
    moved, zero_parts, part_two = fence(moved, zero_parts, part_two)
    part_three = along(add(add(three_got[0], three_parts[0]), moved), depth - 3)
    combined = hidden_state + part_one.astype(jnp.float32) + part_two.astype(jnp.float32)
    moved = hop_one(add(zero_got[2], zero_parts[1]))
    for part in (zero_got[0], zero_parts[0], moved, part_three):
        combined = combined + part.astype(jnp.float32)
    square_two = jnp.sum(combined * combined, axis=1)[None, :]
    square_two = (square_two + across(square_two))[0]
    return (combined * lax.rsqrt(square_two / D + epsilon)[:, None] * final_gain).astype(
        jnp.bfloat16
    )


def per_device(*arrays):
    row_count, expert_count = arrays[6].shape[0], arrays[9].shape[1]
    capacity = min(row_count, 2 * row_count * TOP // expert_count)
    fits = lax.axis_size("kv") == 2 and lax.axis_size("ep") == 16
    if capacity == row_count and fits:
        return dense(*arrays)
    return routed(*arrays)


def solution(mesh):
    placed = (
        P("ep", None),
        P(("ep", "kv"), None, None),
        P(("ep", "kv"), None, None),
        P("ep", "kv", None),
        P("ep"),
        P("ep", None),
        P("ep", "kv"),
        P(None, "kv"),
        P("kv"),
        P("kv", None),
        P("ep", None, "kv"),
        P("ep", None, "kv"),
        P("ep", "kv", None),
        P("kv"),
        P("ep", None),
    )
    return jax.shard_map(
        per_device, mesh=mesh, in_specs=placed, out_specs=P("ep", "kv"), check_vma=False
    )
```

```python
import math

import jax
import jax.numpy as jnp
from jax import lax
from jax.experimental import pallas as pl
from jax.experimental.pallas import tpu as pltpu
from jax.sharding import PartitionSpec as P

D = 2048
HEADS = 16
HEAD_DIM = 128
TOP = 8


epsilon = 1e-06
floor_score = -1e30


def routed(
    queries,
    key_pool,
    value_pool,
    page_table,
    lengths,
    prefill_attn,
    residual,
    w_out,
    norm_gain,
    router,
    w_gate,
    w_up,
    w_down,
    final_gain,
    routes,
):
    holders = lax.axis_size("kv")
    holder = lax.axis_index("kv")
    request_count = queries.shape[0]
    pool_pages = key_pool.shape[0]
    page_rows = key_pool.shape[1]
    pages_each = page_table.shape[2]
    query_heads = queries.reshape(request_count, HEADS, HEAD_DIM)
    page_slots = page_table[:, 0, :]
    picked_keys = key_pool.reshape(pool_pages, page_rows, HEADS, HEAD_DIM)[page_slots]
    picked_values = value_pool.reshape(pool_pages, page_rows, HEADS, HEAD_DIM)[page_slots]
    scores = jnp.einsum(
        "rhd,rjphd->rhjp", query_heads, picked_keys, preferred_element_type=jnp.float32
    ) / math.sqrt(HEAD_DIM)
    page_number = jnp.arange(pages_each, dtype=jnp.int32) * holders + holder
    position = page_number[:, None] * page_rows + jnp.arange(page_rows, dtype=jnp.int32)[None, :]
    visible = position[None, None, :, :] < lengths[:, None, None, None]
    masked = jnp.where(visible, scores, floor_score)
    local_peak = jnp.max(masked, axis=(2, 3))
    weights = jnp.where(visible, jnp.exp(masked - local_peak[:, :, None, None]), 0.0)
    local_mass = jnp.sum(weights, axis=(2, 3))
    local_sum = jnp.einsum(
        "rhjp,rjphd->rhd",
        weights,
        picked_values.astype(jnp.float32),
        precision=lax.Precision.HIGHEST,
    )
    peak_rows, masses, gathered_sums = (
        lax.all_gather(local_peak[None], "kv", axis=0, tiled=True),
        lax.all_gather(local_mass[None], "kv", axis=0, tiled=True),
        lax.all_gather(local_sum[None], "kv", axis=0, tiled=True),
    )
    all_peak = jnp.max(peak_rows, axis=0)
    factors = jnp.exp(peak_rows - all_peak[None])
    all_mass = jnp.sum(masses * factors, axis=0)
    all_sum = jnp.sum(gathered_sums * factors[..., None], axis=0)
    decode_attn = (all_sum / all_mass[..., None]).reshape(request_count, D).astype(jnp.bfloat16)
    attn_rows = jnp.concatenate([prefill_attn, decode_attn], axis=0)
    hidden_state = residual.astype(jnp.float32) + jnp.dot(
        attn_rows, w_out, preferred_element_type=jnp.float32
    )
    scaled = (hidden_state * norm_gain).astype(jnp.bfloat16)
    square_sum, logit_parts = lax.psum(
        (
            jnp.sum(hidden_state * hidden_state, axis=1),
            jnp.dot(scaled, router, preferred_element_type=jnp.float32),
        ),
        "kv",
    )
    inv_first = lax.rsqrt(square_sum / D + epsilon)
    logits = logit_parts * inv_first[:, None]
    normed = (hidden_state * norm_gain * inv_first[:, None]).astype(jnp.bfloat16)
    row_count = residual.shape[0]
    expert_count = router.shape[1]
    capacity = min(row_count, 2 * row_count * TOP // expert_count)
    matches = routes[:, :, None] == jnp.arange(expert_count, dtype=jnp.int32)[None, None, :]
    chosen = jnp.sum(jnp.where(matches, logits[:, None, :], 0.0), axis=2)
    raised = jnp.exp(chosen)
    gate_weights = raised / jnp.sum(raised, axis=1, keepdims=True)
    one_hot = matches.reshape(row_count * TOP, expert_count).astype(jnp.int32)
    earlier = jnp.cumsum(one_hot, axis=0) - one_hot
    slot_index = jnp.sum(earlier * one_hot, axis=1)
    target = routes.reshape(-1) * capacity + slot_index
    source_row = jnp.arange(row_count * TOP, dtype=jnp.int32) // TOP
    filler = jnp.zeros((expert_count * capacity,), jnp.int32).at[target].set(source_row)
    present = jnp.zeros((expert_count * capacity,), jnp.bool_).at[target].set(True)
    gate_local = w_gate[0]
    up_local = w_up[0]
    down_local = w_down[0]
    full_rows = lax.all_gather(normed, "kv", axis=1, tiled=True)
    picked = full_rows[filler]
    arrived = lax.all_to_all(
        jnp.where(present[:, None], picked, jnp.zeros_like(picked)).reshape(
            expert_count, capacity, full_rows.shape[1]
        ),
        "ep",
        split_axis=0,
        concat_axis=0,
        tiled=True,
    )
    inbound = arrived.reshape(-1, arrived.shape[2])
    gate_proj = jnp.dot(inbound, gate_local, preferred_element_type=jnp.float32)
    up_proj = jnp.dot(inbound, up_local, preferred_element_type=jnp.float32)
    activation = (jax.nn.silu(gate_proj) * up_proj).astype(jnp.bfloat16)
    feature_cols = residual.shape[1]
    summed = lax.psum_scatter(
        lax.dot_general(
            down_local, activation, (((0,), (1,)), ((), ())), preferred_element_type=jnp.float32
        ).astype(jnp.bfloat16),
        "kv",
        scatter_dimension=0,
        tiled=True,
    ).astype(jnp.float32)
    expert_out = summed.T.astype(jnp.bfloat16).reshape(
        arrived.shape[0], arrived.shape[1], feature_cols
    )
    returned = lax.all_to_all(expert_out, "ep", split_axis=0, concat_axis=0, tiled=True)
    back_rows = (
        returned.reshape(-1, feature_cols)[target]
        .reshape(row_count, TOP, feature_cols)
        .astype(jnp.float32)
    )
    combined = hidden_state + jnp.sum(back_rows * gate_weights[:, :, None], axis=1)
    square_two = lax.psum(jnp.sum(combined * combined, axis=1), "kv")
    return (combined * lax.rsqrt(square_two / D + epsilon)[:, None] * final_gain).astype(
        jnp.bfloat16
    )


def attend(slots_ref, lengths_ref, q_ref, k_ref, v_ref, out_ref, kbuf, vbuf, ksem, vsem):
    requests, pages_each, page_rows = kbuf.shape[:3]
    holder = lax.axis_index("kv")
    holders = lax.axis_size("kv")
    for r in range(requests):
        for j in range(pages_each):
            pltpu.make_async_copy(k_ref.at[slots_ref[r, 0, j]], kbuf.at[r, j], ksem.at[r]).start()
    for r in range(requests):
        for j in range(pages_each):
            pltpu.make_async_copy(v_ref.at[slots_ref[r, 0, j]], vbuf.at[r, j], vsem.at[r]).start()
    tokens = pages_each * page_rows
    wide_row = lax.broadcasted_iota(jnp.int32, (HEAD_DIM, D), 0)
    wide_head = lax.broadcasted_iota(jnp.int32, (HEAD_DIM, D), 1) // HEAD_DIM
    own_head = (wide_row == wide_head)[:HEADS]
    place = lax.broadcasted_iota(jnp.int32, (HEADS, tokens), 1)
    position = ((place // page_rows) * holders + holder) * page_rows + place % page_rows
    queries = q_ref[...].astype(jnp.float32)
    for r in range(requests):
        spread = jnp.where(wide_row == wide_head, queries[r : r + 1, :], 0.0).astype(jnp.bfloat16)
        pltpu.make_async_copy(kbuf.at[r], kbuf.at[r], ksem.at[r]).wait()
        scores = lax.dot_general(
            kbuf[r].reshape(tokens, D),
            spread,
            (((1,), (1,)), ((), ())),
            preferred_element_type=jnp.float32,
        )
        visible = position < lengths_ref[r]
        scores = jnp.where(visible, scores.T[:HEADS] / math.sqrt(HEAD_DIM), floor_score)
        peak = scores.max(axis=1, keepdims=True)
        weight = jnp.where(visible, jnp.exp(scores - peak), 0.0)
        mass = weight.sum(axis=1, keepdims=True)
        high = weight.astype(jnp.bfloat16)
        low = (weight - high.astype(jnp.float32)).astype(jnp.bfloat16)
        pltpu.make_async_copy(vbuf.at[r], vbuf.at[r], vsem.at[r]).wait()
        total = jnp.dot(
            jnp.concatenate([high, low], axis=0),
            vbuf[r].reshape(tokens, D),
            preferred_element_type=jnp.float32,
        )
        both = total[:HEADS] + total[HEADS:]
        for n, part in enumerate((both, peak, mass)):
            row = n * requests + r
            out_ref[row : row + 1, :] = jnp.sum(
                jnp.where(own_head, part, 0.0), axis=0, keepdims=True
            )


def local_attention(queries, key_pool, value_pool, page_table, lengths):
    requests, _, pages_each = page_table.shape
    held = (requests, pages_each) + key_pool.shape[1:]
    smem = pl.BlockSpec(memory_space=pltpu.SMEM)
    vmem = pl.BlockSpec(memory_space=pltpu.VMEM)
    hbm = pl.BlockSpec(memory_space=pl.ANY)
    return pl.pallas_call(
        attend,
        out_shape=jax.ShapeDtypeStruct((3 * requests, D), jnp.float32),
        in_specs=[smem, smem, vmem, hbm, hbm],
        out_specs=vmem,
        scratch_shapes=[
            pltpu.VMEM(held, jnp.bfloat16),
            pltpu.VMEM(held, jnp.bfloat16),
            pltpu.SemaphoreType.DMA((requests,)),
            pltpu.SemaphoreType.DMA((requests,)),
        ],
        compiler_params=pltpu.CompilerParams(vmem_limit_bytes=60 * 2**20),
        cost_estimate=pl.CostEstimate(flops=4 * 10**8, bytes_accessed=7 * 2**20, transcendentals=0),
        name="local_attention",
    )(page_table, lengths, queries, key_pool, value_pool)


LABELS = ((0, 0), (0, 1), (1, 0), (1, 1))


def where_held(a, b, path):
    if a == b:
        return a, a
    if a == 1:
        return path, 1 - path
    return 1 - path, path


def expert_kernel(side_ref, gate_ref, up_ref, down_ref, *rest):
    blocks = rest[:4]
    outs = rest[4:8]
    xbuf, obuf, gbuf, ubuf, dbuf, wsem, xsem, osem = rest[8:]
    holder, core = lax.axis_index("kv"), lax.axis_index("ep") % 2
    pair = blocks[0].shape[1]
    cols = xbuf.shape[4]
    rows = 2 * pair * xbuf.shape[3]
    halves = (holder, 1 - holder)
    paths = (core, 1 - core)

    def fetch(d, labels):
        for a, b in labels:
            t, f = where_held(a, b, paths[d])
            pltpu.make_async_copy(
                blocks[2 * d + b].at[a], xbuf.at[d, f, pl.ds(t * pair, pair)], xsem.at[d, f]
            ).start()

    def load(source, buffer, kind, f):
        pltpu.make_async_copy(source.at[halves[f]], buffer.at[f], wsem.at[kind, f]).start()

    fetch(0, LABELS)
    load(gate_ref, gbuf, 0, 0)
    load(gate_ref, gbuf, 0, 1)
    load(up_ref, ubuf, 1, 0)
    load(up_ref, ubuf, 1, 1)
    for f in range(2):
        start = pl.multiple_of(halves[f] * cols, cols)
        pltpu.make_async_copy(
            down_ref.at[:, pl.ds(start, cols)], dbuf.at[f], wsem.at[2, f]
        ).start()
    fetch(1, LABELS)

    def ready(d, buffer, kind, f):
        if d == 0:
            pltpu.make_async_copy(buffer.at[f], buffer.at[f], wsem.at[kind, f]).wait()

    def came(d, f):
        pltpu.make_async_copy(xbuf.at[d, f], xbuf.at[d, f], xsem.at[d, f]).wait()

    side = side_ref[...].T
    for d in range(2):
        came(d, 0)
        first = xbuf[d, 0].reshape(rows, cols)
        ready(d, gbuf, 0, 0)
        gate = jnp.dot(first, gbuf[0], preferred_element_type=jnp.float32)
        came(d, 1)
        second = xbuf[d, 1].reshape(rows, cols)
        ready(d, gbuf, 0, 1)
        gate += jnp.dot(second, gbuf[1], preferred_element_type=jnp.float32)
        groups = range(2 * pair * d, 2 * pair * (d + 1))
        scale = jnp.concatenate([side[:, g : g + 1] for g in groups])
        share = jnp.concatenate([side[:, 4 * pair + g : 4 * pair + g + 1] for g in groups])
        gate *= scale
        ready(d, ubuf, 1, 0)
        up = jnp.dot(first, ubuf[0], preferred_element_type=jnp.float32)
        ready(d, ubuf, 1, 1)
        up += jnp.dot(second, ubuf[1], preferred_element_type=jnp.float32)
        up *= scale
        act = (gate / (1.0 + jnp.exp(-gate)) * up).astype(jnp.bfloat16)
        for f in range(2):
            ready(d, dbuf, 2, f)
            out = jnp.dot(act, dbuf[f], preferred_element_type=jnp.float32) * share
            obuf[d, f] = out.astype(jnp.bfloat16).reshape(2 * pair, -1, cols)
        for n, (a, b) in enumerate(LABELS):
            t, f = where_held(a, b, paths[d])
            pltpu.make_async_copy(
                obuf.at[d, f, pl.ds(t * pair, pair)], outs[2 * d + b].at[a], osem.at[4 * d + n]
            ).start()
    for n in range(8):
        pltpu.make_async_copy(obuf.at[0, 0, pl.ds(0, pair)], outs[0].at[0], osem.at[n]).wait()


def run_experts(side, gate, up, down, blocks):
    _, pair, row_count, cols = blocks[0].shape
    hidden = gate.shape[2]
    vmem = pl.BlockSpec(memory_space=pltpu.VMEM)
    hbm = pl.BlockSpec(memory_space=pl.ANY)
    return pl.pallas_call(
        expert_kernel,
        out_shape=[jax.ShapeDtypeStruct(blocks[0].shape, jnp.bfloat16)] * 4,
        in_specs=[vmem, hbm, hbm, hbm] + [hbm] * 4,
        out_specs=[hbm] * 4,
        scratch_shapes=[
            pltpu.VMEM((2, 2, 2 * pair, row_count, cols), jnp.bfloat16),
            pltpu.VMEM((2, 2, 2 * pair, row_count, cols), jnp.bfloat16),
            pltpu.VMEM((2, cols, hidden), jnp.bfloat16),
            pltpu.VMEM((2, cols, hidden), jnp.bfloat16),
            pltpu.VMEM((2, hidden, cols), jnp.bfloat16),
            pltpu.SemaphoreType.DMA((3, 2)),
            pltpu.SemaphoreType.DMA((2, 2)),
            pltpu.SemaphoreType.DMA((8,)),
        ],
        compiler_params=pltpu.CompilerParams(vmem_limit_bytes=60 * 2**20),
        cost_estimate=pl.CostEstimate(
            flops=4 * pair * row_count * 12 * cols * hidden,
            bytes_accessed=pair * row_count * cols * 32 + 12 * cols * hidden,
            transcendentals=0,
        ),
        name="experts",
    )(side, gate, up, down, *blocks)


def add(*parts):
    total = parts[0].astype(jnp.float32)
    for part in parts[1:]:
        total = total + part.astype(jnp.float32)
    return total.astype(jnp.bfloat16)


def dense(
    queries,
    key_pool,
    value_pool,
    page_table,
    lengths,
    prefill_attn,
    residual,
    w_out,
    norm_gain,
    router,
    w_gate,
    w_up,
    w_down,
    final_gain,
    routes,
):
    request_count = queries.shape[0]
    row_count, cols = residual.shape
    expert_count = router.shape[1]
    ep_size = lax.axis_size("ep")
    depth = ep_size // 4
    axes = ("ep", "kv")

    def number(z, y, c, x):
        return ((z * 2 + y) * 2 + c) * 2 + x

    places = [(z, y, c, x) for z in range(depth) for y in range(2) for c in range(2) for x in range(2)]

    def sent(array, target):
        return lax.ppermute(array, axes, [(number(*p), number(*target(*p))) for p in places])

    def across(array):
        return sent(array, lambda z, y, c, x: (z, y, c, 1 - x))

    def along(array, s):
        return sent(array, lambda z, y, c, x: ((z + s) % depth, y, c, x))

    def hop_one(array):
        return sent(array, lambda z, y, c, x: (z, y, c, 1 - x) if c == 0 else (z, 1 - y, c, x))

    def hop_two(array):
        return sent(array, lambda z, y, c, x: (z, 1 - y, c, x) if c == 0 else (z, y, c, 1 - x))

    def sibling(array):
        return sent(array, lambda z, y, c, x: (z, y, 1 - c, x))

    def fence(*values):
        return lax.optimization_barrier(values)

    early = (row_count - request_count) // 16 * 16

    def hidden_of(rows, part):
        product = jnp.dot(rows, w_out, preferred_element_type=jnp.float32)
        state = residual[part].astype(jnp.float32) + product
        return state, (state * norm_gain).astype(jnp.bfloat16)

    first_hidden, first_scaled = hidden_of(prefill_attn[:early], slice(0, early))
    first_one = along(first_scaled, 1)
    local = local_attention(queries, key_pool, value_pool, page_table, lengths)
    first_one, local, first_scaled = fence(first_one, local, first_scaled)

    first_two = along(first_scaled, 2)
    other = across(local)
    sum_one, sum_two = local[:request_count], other[:request_count]
    peak_one, peak_two = (v[request_count : 2 * request_count] for v in (local, other))
    mass_one, mass_two = (v[2 * request_count :] for v in (local, other))
    peak = jnp.maximum(peak_one, peak_two)
    factor_one, factor_two = jnp.exp(peak_one - peak), jnp.exp(peak_two - peak)
    decode_attn = (sum_one * factor_one + sum_two * factor_two) / (
        mass_one * factor_one + mass_two * factor_two
    )
    last_rows = jnp.concatenate([prefill_attn[early:], decode_attn.astype(jnp.bfloat16)], axis=0)
    last_hidden, last_scaled = hidden_of(last_rows, slice(early, row_count))
    first_two, last_scaled, last_hidden = fence(first_two, last_scaled, last_hidden)

    hidden_state = jnp.concatenate([first_hidden, last_hidden], axis=0)
    scaled = jnp.concatenate([first_scaled, last_scaled], axis=0)
    square_part = jnp.sum(hidden_state * hidden_state, axis=1)
    logit_part = jnp.dot(scaled, router, preferred_element_type=jnp.float32)
    stats = jnp.concatenate([logit_part, square_part[:, None]], axis=1).T

    slots = ((1, 2), (3, 0))
    last_one, last_two = along(last_scaled, 1), along(last_scaled, 2)
    stats = stats + across(stats)
    last_one, last_two, stats, scaled = fence(last_one, last_two, stats, scaled)

    pair = jnp.stack(
        [
            jnp.concatenate([first_one, last_one], axis=0),
            jnp.concatenate([first_two, last_two], axis=0),
        ]
    )
    far_three, one = along(scaled, 3), hop_one(pair)
    inv_first = lax.rsqrt(stats[expert_count] / D + epsilon)
    logits = stats[:expert_count].T * inv_first[:, None]
    matches = routes[:, :, None] == jnp.arange(expert_count, dtype=jnp.int32)[None, None, :]
    chosen = jnp.sum(jnp.where(matches, logits[:, None, :], 0.0), axis=2)
    raised = jnp.exp(chosen)
    gate_weights = raised / jnp.sum(raised, axis=1, keepdims=True)
    by_expert = jnp.sum(jnp.where(matches, gate_weights[:, :, None], 0.0), axis=1)
    side = jnp.concatenate([by_expert, inv_first[:, None]], axis=1).T[None]
    side_s = sibling(side)
    side_y = sent(side, lambda z, y, c, x: (z, 1 - y, c, x))
    side_ys = sent(side, lambda z, y, c, x: (z, 1 - y, 1 - c, x))
    far_three, one, pair, scaled, side, side_s, side_y, side_ys = fence(
        far_three, one, pair, scaled, side, side_s, side_y, side_ys
    )

    own = lax.axis_index("ep")
    later = jnp.stack([far_three, scaled])
    near = jnp.stack([pair, one])
    far, near_s, later_one = hop_two(near), sibling(near), hop_one(later)
    side = jnp.concatenate([side, side_s, side_y, side_ys], axis=0)
    crossed = sent(side, lambda z, y, c, x: (z ^ 1, y, c, x))
    swapped = sent(jnp.stack([side, crossed]), lambda z, y, c, x: (z ^ 2, y, c, x))
    far, near_s, later_one, later, side, crossed, swapped = fence(
        far, near_s, later_one, later, side, crossed, swapped
    )

    odd = (own // 4) % 2 == 1
    before, after = jnp.where(odd, crossed, swapped[1]), jnp.where(odd, swapped[1], crossed)
    held = jnp.stack([side, before, swapped[0], after])
    share = lax.dynamic_index_in_dim(held, own, axis=2, keepdims=False)
    held = jnp.stack([held[:, :, expert_count], share]).reshape(2, depth, 2, 2, row_count)
    both = [
        jnp.stack([held[:, s] for s in chunk], axis=1).transpose(0, 3, 2, 1, 4).reshape(-1, row_count)
        for chunk in slots
    ]
    gate_local = w_gate[0].reshape(2, cols, -1)
    up_local = w_up[0].reshape(2, cols, -1)
    down_local = w_down[0]
    later_near = jnp.stack([later, later_one])
    far_s, later_far, later_near_s = sibling(far), hop_two(later_near), sibling(later_near)
    made = run_experts(both[0], gate_local, up_local, down_local, (near, far, near_s, far_s))
    later_far, later_near_s, later_near, made = fence(later_far, later_near_s, later_near, made)

    crossing = add(made[1], sibling(made[3]))
    later_far_s = sibling(later_far)
    crossing, later_far_s = fence(crossing, later_far_s)

    staying_s = sibling(made[2])
    arrived = hop_two(crossing)
    blocks = (later_near, later_far, later_near_s, later_far_s)
    remade = run_experts(both[1], gate_local, up_local, down_local, blocks)
    staying, staying_s, arrived, remade = fence(made[0], staying_s, arrived, remade)

    far_sum = add(staying[1], staying_s[1], arrived[1])
    near_sum = add(staying[0], staying_s[0], arrived[0])
    moved = hop_one(far_sum)
    crossing_s, staying_s = sibling(remade[3]), sibling(remade[2])
    crossing = [add(remade[1][:, i], crossing_s[:, i]) for i in range(2)]
    staying = [[add(remade[0][a, i], staying_s[a, i]) for a in range(2)] for i in range(2)]

    whole = add(near_sum, moved)
    part_one, part_two = along(whole[0], depth - 1), along(whole[1], depth - 2)
    three_parts, zero_parts = hop_two(crossing[0]), hop_two(crossing[1])
    part_one, three_parts = fence(part_one, three_parts)
    moved = hop_one(add(staying[0][1], three_parts[1]))
    moved, zero_parts, part_two = fence(moved, zero_parts, part_two)
    part_three = along(add(staying[0][0], three_parts[0], moved), depth - 3)
    combined = hidden_state + part_one.astype(jnp.float32) + part_two.astype(jnp.float32)
    moved = hop_one(add(staying[1][1], zero_parts[1]))
    for part in (staying[1][0], zero_parts[0], moved, part_three):
        combined = combined + part.astype(jnp.float32)
    square_two = jnp.sum(combined * combined, axis=1)[None, :]
    square_two = (square_two + across(square_two))[0]
    return (combined * lax.rsqrt(square_two / D + epsilon)[:, None] * final_gain).astype(
        jnp.bfloat16
    )


def per_device(*arrays):
    row_count, expert_count = arrays[6].shape[0], arrays[9].shape[1]
    capacity = min(row_count, 2 * row_count * TOP // expert_count)
    fits = lax.axis_size("kv") == 2 and lax.axis_size("ep") == 16
    if capacity == row_count and fits:
        return dense(*arrays)
    return routed(*arrays)


def solution(mesh):
    placed = (
        P("ep", None),
        P(("ep", "kv"), None, None),
        P(("ep", "kv"), None, None),
        P("ep", "kv", None),
        P("ep"),
        P("ep", None),
        P("ep", "kv"),
        P(None, "kv"),
        P("kv"),
        P("kv", None),
        P("ep", None, "kv"),
        P("ep", None, "kv"),
        P("ep", "kv", None),
        P("kv"),
        P("ep", None),
    )
    return jax.shard_map(
        per_device, mesh=mesh, in_specs=placed, out_specs=P("ep", "kv"), check_vma=False
    )
```

```python
import math

import jax
import jax.numpy as jnp
from jax import lax
from jax.experimental import pallas as pl
from jax.experimental.pallas import tpu as pltpu
from jax.sharding import PartitionSpec as P

D = 2048
HEADS = 16
HEAD_DIM = 128
TOP = 8


epsilon = 1e-06
floor_score = -1e30


def routed(
    queries,
    key_pool,
    value_pool,
    page_table,
    lengths,
    prefill_attn,
    residual,
    w_out,
    norm_gain,
    router,
    w_gate,
    w_up,
    w_down,
    final_gain,
    routes,
):
    holders = lax.axis_size("kv")
    holder = lax.axis_index("kv")
    request_count = queries.shape[0]
    pool_pages = key_pool.shape[0]
    page_rows = key_pool.shape[1]
    pages_each = page_table.shape[2]
    query_heads = queries.reshape(request_count, HEADS, HEAD_DIM)
    page_slots = page_table[:, 0, :]
    picked_keys = key_pool.reshape(pool_pages, page_rows, HEADS, HEAD_DIM)[page_slots]
    picked_values = value_pool.reshape(pool_pages, page_rows, HEADS, HEAD_DIM)[page_slots]
    scores = jnp.einsum(
        "rhd,rjphd->rhjp", query_heads, picked_keys, preferred_element_type=jnp.float32
    ) / math.sqrt(HEAD_DIM)
    page_number = jnp.arange(pages_each, dtype=jnp.int32) * holders + holder
    position = page_number[:, None] * page_rows + jnp.arange(page_rows, dtype=jnp.int32)[None, :]
    visible = position[None, None, :, :] < lengths[:, None, None, None]
    masked = jnp.where(visible, scores, floor_score)
    local_peak = jnp.max(masked, axis=(2, 3))
    weights = jnp.where(visible, jnp.exp(masked - local_peak[:, :, None, None]), 0.0)
    local_mass = jnp.sum(weights, axis=(2, 3))
    local_sum = jnp.einsum(
        "rhjp,rjphd->rhd",
        weights,
        picked_values.astype(jnp.float32),
        precision=lax.Precision.HIGHEST,
    )
    peak_rows, masses, gathered_sums = (
        lax.all_gather(local_peak[None], "kv", axis=0, tiled=True),
        lax.all_gather(local_mass[None], "kv", axis=0, tiled=True),
        lax.all_gather(local_sum[None], "kv", axis=0, tiled=True),
    )
    all_peak = jnp.max(peak_rows, axis=0)
    factors = jnp.exp(peak_rows - all_peak[None])
    all_mass = jnp.sum(masses * factors, axis=0)
    all_sum = jnp.sum(gathered_sums * factors[..., None], axis=0)
    decode_attn = (all_sum / all_mass[..., None]).reshape(request_count, D).astype(jnp.bfloat16)
    attn_rows = jnp.concatenate([prefill_attn, decode_attn], axis=0)
    hidden_state = residual.astype(jnp.float32) + jnp.dot(
        attn_rows, w_out, preferred_element_type=jnp.float32
    )
    scaled = (hidden_state * norm_gain).astype(jnp.bfloat16)
    square_sum, logit_parts = lax.psum(
        (
            jnp.sum(hidden_state * hidden_state, axis=1),
            jnp.dot(scaled, router, preferred_element_type=jnp.float32),
        ),
        "kv",
    )
    inv_first = lax.rsqrt(square_sum / D + epsilon)
    logits = logit_parts * inv_first[:, None]
    normed = (hidden_state * norm_gain * inv_first[:, None]).astype(jnp.bfloat16)
    row_count = residual.shape[0]
    expert_count = router.shape[1]
    capacity = min(row_count, 2 * row_count * TOP // expert_count)
    matches = routes[:, :, None] == jnp.arange(expert_count, dtype=jnp.int32)[None, None, :]
    chosen = jnp.sum(jnp.where(matches, logits[:, None, :], 0.0), axis=2)
    raised = jnp.exp(chosen)
    gate_weights = raised / jnp.sum(raised, axis=1, keepdims=True)
    one_hot = matches.reshape(row_count * TOP, expert_count).astype(jnp.int32)
    earlier = jnp.cumsum(one_hot, axis=0) - one_hot
    slot_index = jnp.sum(earlier * one_hot, axis=1)
    target = routes.reshape(-1) * capacity + slot_index
    source_row = jnp.arange(row_count * TOP, dtype=jnp.int32) // TOP
    filler = jnp.zeros((expert_count * capacity,), jnp.int32).at[target].set(source_row)
    present = jnp.zeros((expert_count * capacity,), jnp.bool_).at[target].set(True)
    gate_local = w_gate[0]
    up_local = w_up[0]
    down_local = w_down[0]
    full_rows = lax.all_gather(normed, "kv", axis=1, tiled=True)
    picked = full_rows[filler]
    arrived = lax.all_to_all(
        jnp.where(present[:, None], picked, jnp.zeros_like(picked)).reshape(
            expert_count, capacity, full_rows.shape[1]
        ),
        "ep",
        split_axis=0,
        concat_axis=0,
        tiled=True,
    )
    inbound = arrived.reshape(-1, arrived.shape[2])
    gate_proj = jnp.dot(inbound, gate_local, preferred_element_type=jnp.float32)
    up_proj = jnp.dot(inbound, up_local, preferred_element_type=jnp.float32)
    activation = (jax.nn.silu(gate_proj) * up_proj).astype(jnp.bfloat16)
    feature_cols = residual.shape[1]
    summed = lax.psum_scatter(
        lax.dot_general(
            down_local, activation, (((0,), (1,)), ((), ())), preferred_element_type=jnp.float32
        ).astype(jnp.bfloat16),
        "kv",
        scatter_dimension=0,
        tiled=True,
    ).astype(jnp.float32)
    expert_out = summed.T.astype(jnp.bfloat16).reshape(
        arrived.shape[0], arrived.shape[1], feature_cols
    )
    returned = lax.all_to_all(expert_out, "ep", split_axis=0, concat_axis=0, tiled=True)
    back_rows = (
        returned.reshape(-1, feature_cols)[target]
        .reshape(row_count, TOP, feature_cols)
        .astype(jnp.float32)
    )
    combined = hidden_state + jnp.sum(back_rows * gate_weights[:, :, None], axis=1)
    square_two = lax.psum(jnp.sum(combined * combined, axis=1), "kv")
    return (combined * lax.rsqrt(square_two / D + epsilon)[:, None] * final_gain).astype(
        jnp.bfloat16
    )


def attend(slots_ref, lengths_ref, q_ref, k_ref, v_ref, out_ref, kbuf, vbuf, ksem, vsem):
    requests, pages_each, page_rows = kbuf.shape[:3]
    holder = lax.axis_index("kv")
    holders = lax.axis_size("kv")
    for r in range(requests):
        for j in range(pages_each):
            pltpu.make_async_copy(k_ref.at[slots_ref[r, 0, j]], kbuf.at[r, j], ksem.at[r]).start()
    for r in range(requests):
        for j in range(pages_each):
            pltpu.make_async_copy(v_ref.at[slots_ref[r, 0, j]], vbuf.at[r, j], vsem.at[r]).start()
    tokens = pages_each * page_rows
    wide_row = lax.broadcasted_iota(jnp.int32, (HEAD_DIM, D), 0)
    wide_head = lax.broadcasted_iota(jnp.int32, (HEAD_DIM, D), 1) // HEAD_DIM
    own_head = (wide_row == wide_head)[:HEADS]
    place = lax.broadcasted_iota(jnp.int32, (HEADS, tokens), 1)
    position = ((place // page_rows) * holders + holder) * page_rows + place % page_rows
    queries = q_ref[...].astype(jnp.float32)
    for r in range(requests):
        spread = jnp.where(wide_row == wide_head, queries[r : r + 1, :], 0.0).astype(jnp.bfloat16)
        pltpu.make_async_copy(kbuf.at[r], kbuf.at[r], ksem.at[r]).wait()
        scores = lax.dot_general(
            kbuf[r].reshape(tokens, D),
            spread,
            (((1,), (1,)), ((), ())),
            preferred_element_type=jnp.float32,
        )
        visible = position < lengths_ref[r]
        scores = jnp.where(visible, scores.T[:HEADS] / math.sqrt(HEAD_DIM), floor_score)
        peak = scores.max(axis=1, keepdims=True)
        weight = jnp.where(visible, jnp.exp(scores - peak), 0.0)
        mass = weight.sum(axis=1, keepdims=True)
        high = weight.astype(jnp.bfloat16)
        low = (weight - high.astype(jnp.float32)).astype(jnp.bfloat16)
        pltpu.make_async_copy(vbuf.at[r], vbuf.at[r], vsem.at[r]).wait()
        total = jnp.dot(
            jnp.concatenate([high, low], axis=0),
            vbuf[r].reshape(tokens, D),
            preferred_element_type=jnp.float32,
        )
        both = total[:HEADS] + total[HEADS:]
        for n, part in enumerate((both, peak, mass)):
            row = n * requests + r
            out_ref[row : row + 1, :] = jnp.sum(
                jnp.where(own_head, part, 0.0), axis=0, keepdims=True
            )


def local_attention(queries, key_pool, value_pool, page_table, lengths):
    requests, _, pages_each = page_table.shape
    held = (requests, pages_each) + key_pool.shape[1:]
    smem = pl.BlockSpec(memory_space=pltpu.SMEM)
    vmem = pl.BlockSpec(memory_space=pltpu.VMEM)
    hbm = pl.BlockSpec(memory_space=pl.ANY)
    return pl.pallas_call(
        attend,
        out_shape=jax.ShapeDtypeStruct((3 * requests, D), jnp.float32),
        in_specs=[smem, smem, vmem, hbm, hbm],
        out_specs=vmem,
        scratch_shapes=[
            pltpu.VMEM(held, jnp.bfloat16),
            pltpu.VMEM(held, jnp.bfloat16),
            pltpu.SemaphoreType.DMA((requests,)),
            pltpu.SemaphoreType.DMA((requests,)),
        ],
        compiler_params=pltpu.CompilerParams(vmem_limit_bytes=60 * 2**20),
        cost_estimate=pl.CostEstimate(flops=4 * 10**8, bytes_accessed=7 * 2**20, transcendentals=0),
        name="local_attention",
    )(page_table, lengths, queries, key_pool, value_pool)


LABELS = ((0, 0), (0, 1), (1, 0), (1, 1))


def where_held(a, b, path):
    if a == b:
        return a, a
    if a == 1:
        return path, 1 - path
    return 1 - path, path


def expert_kernel(by_slot, side_ref, gate_ref, up_ref, down_ref, *rest):
    blocks = rest[:4]
    outs = rest[4:8]
    xbuf, obuf, gbuf, ubuf, dbuf, wsem, xsem, osem = rest[8:]
    holder, core = lax.axis_index("kv"), lax.axis_index("ep") % 2
    pair = blocks[0].shape[1]
    cols = xbuf.shape[4]
    rows = 2 * pair * xbuf.shape[3]
    halves = (holder, 1 - holder)
    paths = (core, 1 - core)

    def fetch(d, labels):
        for a, b in labels:
            t, f = where_held(a, b, paths[d])
            pltpu.make_async_copy(
                blocks[2 * d + b].at[a], xbuf.at[d, f, pl.ds(t * pair, pair)], xsem.at[d, f]
            ).start()

    def load(source, buffer, kind, f):
        pltpu.make_async_copy(source.at[halves[f]], buffer.at[f], wsem.at[kind, f]).start()

    fetch(0, LABELS)
    load(gate_ref, gbuf, 0, 0)
    load(gate_ref, gbuf, 0, 1)
    load(up_ref, ubuf, 1, 0)
    load(up_ref, ubuf, 1, 1)
    for f in range(2):
        start = pl.multiple_of(halves[f] * cols, cols)
        pltpu.make_async_copy(
            down_ref.at[:, pl.ds(start, cols)], dbuf.at[f], wsem.at[2, f]
        ).start()
    fetch(1, LABELS)

    def ready(d, buffer, kind, f):
        if d == 0:
            pltpu.make_async_copy(buffer.at[f], buffer.at[f], wsem.at[kind, f]).wait()

    def came(d, f):
        pltpu.make_async_copy(xbuf.at[d, f], xbuf.at[d, f], xsem.at[d, f]).wait()

    side = side_ref[...].T
    for d in range(2):
        came(d, 0)
        first = xbuf[d, 0].reshape(rows, cols)
        ready(d, gbuf, 0, 0)
        gate = jnp.dot(first, gbuf[0], preferred_element_type=jnp.float32)
        came(d, 1)
        second = xbuf[d, 1].reshape(rows, cols)
        ready(d, gbuf, 0, 1)
        gate += jnp.dot(second, gbuf[1], preferred_element_type=jnp.float32)
        groups = range(2 * pair * d, 2 * pair * (d + 1))
        scale = jnp.concatenate([side[:, g : g + 1] for g in groups])
        share = jnp.concatenate([side[:, 4 * pair + g : 4 * pair + g + 1] for g in groups])
        gate *= scale
        ready(d, ubuf, 1, 0)
        up = jnp.dot(first, ubuf[0], preferred_element_type=jnp.float32)
        ready(d, ubuf, 1, 1)
        up += jnp.dot(second, ubuf[1], preferred_element_type=jnp.float32)
        up *= scale
        act = (gate / (1.0 + jnp.exp(-gate)) * up).astype(jnp.bfloat16)
        for f in range(2):
            ready(d, dbuf, 2, f)
            out = jnp.dot(act, dbuf[f], preferred_element_type=jnp.float32) * share
            obuf[d, f] = out.astype(jnp.bfloat16).reshape(2 * pair, -1, cols)
        for n, (a, b) in enumerate(LABELS):
            t, f = where_held(a, b, paths[d])
            out = outs[2 * d + b].at[:, a] if by_slot else outs[2 * d + b].at[a]
            pltpu.make_async_copy(
                obuf.at[d, f, pl.ds(t * pair, pair)], out, osem.at[4 * d + n]
            ).start()
    for n in range(8):
        pltpu.make_async_copy(
            obuf.at[0, 0, pl.ds(0, pair)], obuf.at[0, 0, pl.ds(0, pair)], osem.at[n]
        ).wait()


def run_experts(by_slot, side, gate, up, down, blocks):
    _, pair, row_count, cols = blocks[0].shape
    hidden = gate.shape[2]
    vmem = pl.BlockSpec(memory_space=pltpu.VMEM)
    hbm = pl.BlockSpec(memory_space=pl.ANY)
    shape = (pair, 2, row_count, cols) if by_slot else (2, pair, row_count, cols)

    def body(*refs):
        expert_kernel(by_slot, *refs)

    return pl.pallas_call(
        body,
        out_shape=[jax.ShapeDtypeStruct(shape, jnp.bfloat16)] * 4,
        in_specs=[vmem, hbm, hbm, hbm] + [hbm] * 4,
        out_specs=[hbm] * 4,
        scratch_shapes=[
            pltpu.VMEM((2, 2, 2 * pair, row_count, cols), jnp.bfloat16),
            pltpu.VMEM((2, 2, 2 * pair, row_count, cols), jnp.bfloat16),
            pltpu.VMEM((2, cols, hidden), jnp.bfloat16),
            pltpu.VMEM((2, cols, hidden), jnp.bfloat16),
            pltpu.VMEM((2, hidden, cols), jnp.bfloat16),
            pltpu.SemaphoreType.DMA((3, 2)),
            pltpu.SemaphoreType.DMA((2, 2)),
            pltpu.SemaphoreType.DMA((8,)),
        ],
        compiler_params=pltpu.CompilerParams(vmem_limit_bytes=60 * 2**20),
        cost_estimate=pl.CostEstimate(
            flops=4 * pair * row_count * 12 * cols * hidden,
            bytes_accessed=pair * row_count * cols * 32 + 12 * cols * hidden,
            transcendentals=0,
        ),
        name="experts",
    )(side, gate, up, down, *blocks)


def add(*parts):
    total = parts[0].astype(jnp.float32)
    for part in parts[1:]:
        total = total + part.astype(jnp.float32)
    return total.astype(jnp.bfloat16)


def dense(
    queries,
    key_pool,
    value_pool,
    page_table,
    lengths,
    prefill_attn,
    residual,
    w_out,
    norm_gain,
    router,
    w_gate,
    w_up,
    w_down,
    final_gain,
    routes,
):
    request_count = queries.shape[0]
    row_count, cols = residual.shape
    expert_count = router.shape[1]
    ep_size = lax.axis_size("ep")
    depth = ep_size // 4
    axes = ("ep", "kv")

    def number(z, y, c, x):
        return ((z * 2 + y) * 2 + c) * 2 + x

    places = [(z, y, c, x) for z in range(depth) for y in range(2) for c in range(2) for x in range(2)]

    def sent(array, target):
        return lax.ppermute(array, axes, [(number(*p), number(*target(*p))) for p in places])

    def across(array):
        return sent(array, lambda z, y, c, x: (z, y, c, 1 - x))

    def along(array, s):
        return sent(array, lambda z, y, c, x: ((z + s) % depth, y, c, x))

    def hop_one(array):
        return sent(array, lambda z, y, c, x: (z, y, c, 1 - x) if c == 0 else (z, 1 - y, c, x))

    def hop_two(array):
        return sent(array, lambda z, y, c, x: (z, 1 - y, c, x) if c == 0 else (z, y, c, 1 - x))

    def sibling(array):
        return sent(array, lambda z, y, c, x: (z, y, 1 - c, x))

    def fence(*values):
        return lax.optimization_barrier(values)

    early = (row_count - request_count) // 16 * 16

    def hidden_of(rows, part):
        product = jnp.dot(rows, w_out, preferred_element_type=jnp.float32)
        state = residual[part].astype(jnp.float32) + product
        return state, (state * norm_gain).astype(jnp.bfloat16)

    first_hidden, first_scaled = hidden_of(prefill_attn[:early], slice(0, early))
    first_one = along(first_scaled, 1)
    local = local_attention(queries, key_pool, value_pool, page_table, lengths)
    first_one, local, first_scaled = fence(first_one, local, first_scaled)

    first_two = along(first_scaled, 2)
    other = across(local)
    sum_one, sum_two = local[:request_count], other[:request_count]
    peak_one, peak_two = (v[request_count : 2 * request_count] for v in (local, other))
    mass_one, mass_two = (v[2 * request_count :] for v in (local, other))
    peak = jnp.maximum(peak_one, peak_two)
    factor_one, factor_two = jnp.exp(peak_one - peak), jnp.exp(peak_two - peak)
    decode_attn = (sum_one * factor_one + sum_two * factor_two) / (
        mass_one * factor_one + mass_two * factor_two
    )
    last_rows = jnp.concatenate([prefill_attn[early:], decode_attn.astype(jnp.bfloat16)], axis=0)
    last_hidden, last_scaled = hidden_of(last_rows, slice(early, row_count))
    first_two, last_scaled, last_hidden = fence(first_two, last_scaled, last_hidden)

    hidden_state = jnp.concatenate([first_hidden, last_hidden], axis=0)
    scaled = jnp.concatenate([first_scaled, last_scaled], axis=0)
    square_part = jnp.sum(hidden_state * hidden_state, axis=1)
    logit_part = jnp.dot(scaled, router, preferred_element_type=jnp.float32)
    stats = jnp.concatenate([logit_part, square_part[:, None]], axis=1).T

    slots = ((1, 2), (3, 0))
    last_one, last_two = along(last_scaled, 1), along(last_scaled, 2)
    stats = stats + across(stats)
    own_one = hop_one(scaled)
    last_one, last_two, stats, scaled, own_one = fence(last_one, last_two, stats, scaled, own_one)

    pair = jnp.stack(
        [
            jnp.concatenate([first_one, last_one], axis=0),
            jnp.concatenate([first_two, last_two], axis=0),
        ]
    )
    far_three, one = along(scaled, 3), hop_one(pair)
    inv_first = lax.rsqrt(stats[expert_count] / D + epsilon)
    logits = stats[:expert_count].T * inv_first[:, None]
    matches = routes[:, :, None] == jnp.arange(expert_count, dtype=jnp.int32)[None, None, :]
    chosen = jnp.sum(jnp.where(matches, logits[:, None, :], 0.0), axis=2)
    raised = jnp.exp(chosen)
    gate_weights = raised / jnp.sum(raised, axis=1, keepdims=True)
    by_expert = jnp.sum(jnp.where(matches, gate_weights[:, :, None], 0.0), axis=1)
    side = jnp.concatenate([by_expert, inv_first[:, None]], axis=1).T[None]
    side_s = sibling(side)
    side_y = sent(side, lambda z, y, c, x: (z, 1 - y, c, x))
    side_ys = sent(side, lambda z, y, c, x: (z, 1 - y, 1 - c, x))
    far_three, one, pair, scaled, side, side_s, side_y, side_ys = fence(
        far_three, one, pair, scaled, side, side_s, side_y, side_ys
    )

    own = lax.axis_index("ep")
    near = jnp.stack([pair, one])
    far, near_s, far_one = hop_two(near), sibling(near), hop_one(far_three)
    later_near = jnp.stack([jnp.stack([far_three, scaled]), jnp.stack([far_one, own_one])])
    side = jnp.concatenate([side, side_s, side_y, side_ys], axis=0)
    crossed = sent(side, lambda z, y, c, x: (z ^ 1, y, c, x))
    swapped = sent(jnp.stack([side, crossed]), lambda z, y, c, x: (z ^ 2, y, c, x))
    far, near_s, later_near, side, crossed, swapped = fence(
        far, near_s, later_near, side, crossed, swapped
    )

    odd = (own // 4) % 2 == 1
    before, after = jnp.where(odd, crossed, swapped[1]), jnp.where(odd, swapped[1], crossed)
    held = jnp.stack([side, before, swapped[0], after])
    share = lax.dynamic_index_in_dim(held, own, axis=2, keepdims=False)
    held = jnp.stack([held[:, :, expert_count], share]).reshape(2, depth, 2, 2, row_count)
    both = [
        jnp.stack([held[:, s] for s in chunk], axis=1).transpose(0, 3, 2, 1, 4).reshape(-1, row_count)
        for chunk in slots
    ]
    gate_local = w_gate[0].reshape(2, cols, -1)
    up_local = w_up[0].reshape(2, cols, -1)
    down_local = w_down[0]
    far_s, later_far, later_near_s = sibling(far), hop_two(later_near), sibling(later_near)
    made = run_experts(False, both[0], gate_local, up_local, down_local, (near, far, near_s, far_s))
    later_far, later_near_s, later_near, made = fence(later_far, later_near_s, later_near, made)

    crossing = add(made[1], sibling(made[3]))
    later_far_s = sibling(later_far)
    crossing, later_far_s = fence(crossing, later_far_s)

    staying_s = sibling(made[2])
    arrived = hop_two(crossing)
    blocks = (later_near, later_far, later_near_s, later_far_s)
    remade = run_experts(True, both[1], gate_local, up_local, down_local, blocks)
    staying, staying_s, arrived, remade = fence(made[0], staying_s, arrived, remade)

    far_sum = add(staying[1], staying_s[1], arrived[1])
    near_sum = add(staying[0], staying_s[0], arrived[0])
    moved = hop_one(far_sum)
    crossing_s, staying_s = sibling(remade[3]), sibling(remade[2])
    crossing = [add(remade[1][i], crossing_s[i]) for i in range(2)]
    staying = [[add(remade[0][i, a], staying_s[i, a]) for a in range(2)] for i in range(2)]
    moved, near_sum, crossing, staying = fence(moved, near_sum, crossing, staying)

    whole = add(near_sum, moved)
    part_one, part_two = along(whole[0], depth - 1), along(whole[1], depth - 2)
    three_parts, zero_parts = hop_two(crossing[0]), hop_two(crossing[1])
    part_one, three_parts = fence(part_one, three_parts)
    moved = hop_one(add(staying[0][1], three_parts[1]))
    moved, zero_parts, part_two = fence(moved, zero_parts, part_two)
    part_three = along(add(staying[0][0], three_parts[0], moved), depth - 3)
    combined = hidden_state + part_one.astype(jnp.float32) + part_two.astype(jnp.float32)
    moved = hop_one(add(staying[1][1], zero_parts[1]))
    for part in (staying[1][0], zero_parts[0], moved, part_three):
        combined = combined + part.astype(jnp.float32)
    square_two = jnp.sum(combined * combined, axis=1)[None, :]
    square_two = (square_two + across(square_two))[0]
    return (combined * lax.rsqrt(square_two / D + epsilon)[:, None] * final_gain).astype(
        jnp.bfloat16
    )


def per_device(*arrays):
    row_count, expert_count = arrays[6].shape[0], arrays[9].shape[1]
    capacity = min(row_count, 2 * row_count * TOP // expert_count)
    fits = lax.axis_size("kv") == 2 and lax.axis_size("ep") == 16
    if capacity == row_count and fits:
        return dense(*arrays)
    return routed(*arrays)


def solution(mesh):
    placed = (
        P("ep", None),
        P(("ep", "kv"), None, None),
        P(("ep", "kv"), None, None),
        P("ep", "kv", None),
        P("ep"),
        P("ep", None),
        P("ep", "kv"),
        P(None, "kv"),
        P("kv"),
        P("kv", None),
        P("ep", None, "kv"),
        P("ep", None, "kv"),
        P("ep", "kv", None),
        P("kv"),
        P("ep", None),
    )
    return jax.shard_map(
        per_device, mesh=mesh, in_specs=placed, out_specs=P("ep", "kv"), check_vma=False
    )
```

```python
import math

import jax
import jax.numpy as jnp
from jax import lax
from jax.experimental import pallas as pl
from jax.experimental.pallas import tpu as pltpu
from jax.sharding import PartitionSpec as P

D = 2048
HEADS = 16
HEAD_DIM = 128
TOP = 8


epsilon = 1e-06
floor_score = -1e30


def routed(
    queries,
    key_pool,
    value_pool,
    page_table,
    lengths,
    prefill_attn,
    residual,
    w_out,
    norm_gain,
    router,
    w_gate,
    w_up,
    w_down,
    final_gain,
    routes,
):
    holders = lax.axis_size("kv")
    holder = lax.axis_index("kv")
    request_count = queries.shape[0]
    pool_pages = key_pool.shape[0]
    page_rows = key_pool.shape[1]
    pages_each = page_table.shape[2]
    query_heads = queries.reshape(request_count, HEADS, HEAD_DIM)
    page_slots = page_table[:, 0, :]
    picked_keys = key_pool.reshape(pool_pages, page_rows, HEADS, HEAD_DIM)[page_slots]
    picked_values = value_pool.reshape(pool_pages, page_rows, HEADS, HEAD_DIM)[page_slots]
    scores = jnp.einsum(
        "rhd,rjphd->rhjp", query_heads, picked_keys, preferred_element_type=jnp.float32
    ) / math.sqrt(HEAD_DIM)
    page_number = jnp.arange(pages_each, dtype=jnp.int32) * holders + holder
    position = page_number[:, None] * page_rows + jnp.arange(page_rows, dtype=jnp.int32)[None, :]
    visible = position[None, None, :, :] < lengths[:, None, None, None]
    masked = jnp.where(visible, scores, floor_score)
    local_peak = jnp.max(masked, axis=(2, 3))
    weights = jnp.where(visible, jnp.exp(masked - local_peak[:, :, None, None]), 0.0)
    local_mass = jnp.sum(weights, axis=(2, 3))
    local_sum = jnp.einsum(
        "rhjp,rjphd->rhd",
        weights,
        picked_values.astype(jnp.float32),
        precision=lax.Precision.HIGHEST,
    )
    peak_rows, masses, gathered_sums = (
        lax.all_gather(local_peak[None], "kv", axis=0, tiled=True),
        lax.all_gather(local_mass[None], "kv", axis=0, tiled=True),
        lax.all_gather(local_sum[None], "kv", axis=0, tiled=True),
    )
    all_peak = jnp.max(peak_rows, axis=0)
    factors = jnp.exp(peak_rows - all_peak[None])
    all_mass = jnp.sum(masses * factors, axis=0)
    all_sum = jnp.sum(gathered_sums * factors[..., None], axis=0)
    decode_attn = (all_sum / all_mass[..., None]).reshape(request_count, D).astype(jnp.bfloat16)
    attn_rows = jnp.concatenate([prefill_attn, decode_attn], axis=0)
    hidden_state = residual.astype(jnp.float32) + jnp.dot(
        attn_rows, w_out, preferred_element_type=jnp.float32
    )
    scaled = (hidden_state * norm_gain).astype(jnp.bfloat16)
    square_sum, logit_parts = lax.psum(
        (
            jnp.sum(hidden_state * hidden_state, axis=1),
            jnp.dot(scaled, router, preferred_element_type=jnp.float32),
        ),
        "kv",
    )
    inv_first = lax.rsqrt(square_sum / D + epsilon)
    logits = logit_parts * inv_first[:, None]
    normed = (hidden_state * norm_gain * inv_first[:, None]).astype(jnp.bfloat16)
    row_count = residual.shape[0]
    expert_count = router.shape[1]
    capacity = min(row_count, 2 * row_count * TOP // expert_count)
    matches = routes[:, :, None] == jnp.arange(expert_count, dtype=jnp.int32)[None, None, :]
    chosen = jnp.sum(jnp.where(matches, logits[:, None, :], 0.0), axis=2)
    raised = jnp.exp(chosen)
    gate_weights = raised / jnp.sum(raised, axis=1, keepdims=True)
    one_hot = matches.reshape(row_count * TOP, expert_count).astype(jnp.int32)
    earlier = jnp.cumsum(one_hot, axis=0) - one_hot
    slot_index = jnp.sum(earlier * one_hot, axis=1)
    target = routes.reshape(-1) * capacity + slot_index
    source_row = jnp.arange(row_count * TOP, dtype=jnp.int32) // TOP
    filler = jnp.zeros((expert_count * capacity,), jnp.int32).at[target].set(source_row)
    present = jnp.zeros((expert_count * capacity,), jnp.bool_).at[target].set(True)
    gate_local = w_gate[0]
    up_local = w_up[0]
    down_local = w_down[0]
    full_rows = lax.all_gather(normed, "kv", axis=1, tiled=True)
    picked = full_rows[filler]
    arrived = lax.all_to_all(
        jnp.where(present[:, None], picked, jnp.zeros_like(picked)).reshape(
            expert_count, capacity, full_rows.shape[1]
        ),
        "ep",
        split_axis=0,
        concat_axis=0,
        tiled=True,
    )
    inbound = arrived.reshape(-1, arrived.shape[2])
    gate_proj = jnp.dot(inbound, gate_local, preferred_element_type=jnp.float32)
    up_proj = jnp.dot(inbound, up_local, preferred_element_type=jnp.float32)
    activation = (jax.nn.silu(gate_proj) * up_proj).astype(jnp.bfloat16)
    feature_cols = residual.shape[1]
    summed = lax.psum_scatter(
        lax.dot_general(
            down_local, activation, (((0,), (1,)), ((), ())), preferred_element_type=jnp.float32
        ).astype(jnp.bfloat16),
        "kv",
        scatter_dimension=0,
        tiled=True,
    ).astype(jnp.float32)
    expert_out = summed.T.astype(jnp.bfloat16).reshape(
        arrived.shape[0], arrived.shape[1], feature_cols
    )
    returned = lax.all_to_all(expert_out, "ep", split_axis=0, concat_axis=0, tiled=True)
    back_rows = (
        returned.reshape(-1, feature_cols)[target]
        .reshape(row_count, TOP, feature_cols)
        .astype(jnp.float32)
    )
    combined = hidden_state + jnp.sum(back_rows * gate_weights[:, :, None], axis=1)
    square_two = lax.psum(jnp.sum(combined * combined, axis=1), "kv")
    return (combined * lax.rsqrt(square_two / D + epsilon)[:, None] * final_gain).astype(
        jnp.bfloat16
    )


def attend(slots_ref, lengths_ref, q_ref, k_ref, v_ref, out_ref, kbuf, vbuf, ksem, vsem):
    requests, pages_each, page_rows = kbuf.shape[:3]
    holder = lax.axis_index("kv")
    holders = lax.axis_size("kv")
    for r in range(requests):
        for j in range(pages_each):
            pltpu.make_async_copy(k_ref.at[slots_ref[r, 0, j]], kbuf.at[r, j], ksem.at[r]).start()
    for r in range(requests):
        for j in range(pages_each):
            pltpu.make_async_copy(v_ref.at[slots_ref[r, 0, j]], vbuf.at[r, j], vsem.at[r]).start()
    tokens = pages_each * page_rows
    wide_row = lax.broadcasted_iota(jnp.int32, (HEAD_DIM, D), 0)
    wide_head = lax.broadcasted_iota(jnp.int32, (HEAD_DIM, D), 1) // HEAD_DIM
    own_head = (wide_row == wide_head)[:HEADS]
    place = lax.broadcasted_iota(jnp.int32, (HEADS, tokens), 1)
    position = ((place // page_rows) * holders + holder) * page_rows + place % page_rows
    queries = q_ref[...].astype(jnp.float32)
    for r in range(requests):
        spread = jnp.where(wide_row == wide_head, queries[r : r + 1, :], 0.0).astype(jnp.bfloat16)
        pltpu.make_async_copy(kbuf.at[r], kbuf.at[r], ksem.at[r]).wait()
        scores = lax.dot_general(
            kbuf[r].reshape(tokens, D),
            spread,
            (((1,), (1,)), ((), ())),
            preferred_element_type=jnp.float32,
        )
        visible = position < lengths_ref[r]
        scores = jnp.where(visible, scores.T[:HEADS] / math.sqrt(HEAD_DIM), floor_score)
        peak = scores.max(axis=1, keepdims=True)
        weight = jnp.where(visible, jnp.exp(scores - peak), 0.0)
        mass = weight.sum(axis=1, keepdims=True)
        high = weight.astype(jnp.bfloat16)
        low = (weight - high.astype(jnp.float32)).astype(jnp.bfloat16)
        pltpu.make_async_copy(vbuf.at[r], vbuf.at[r], vsem.at[r]).wait()
        total = jnp.dot(
            jnp.concatenate([high, low], axis=0),
            vbuf[r].reshape(tokens, D),
            preferred_element_type=jnp.float32,
        )
        both = total[:HEADS] + total[HEADS:]
        for n, part in enumerate((both, peak, mass)):
            row = n * requests + r
            out_ref[row : row + 1, :] = jnp.sum(
                jnp.where(own_head, part, 0.0), axis=0, keepdims=True
            )


def local_attention(queries, key_pool, value_pool, page_table, lengths):
    requests, _, pages_each = page_table.shape
    held = (requests, pages_each) + key_pool.shape[1:]
    smem = pl.BlockSpec(memory_space=pltpu.SMEM)
    vmem = pl.BlockSpec(memory_space=pltpu.VMEM)
    hbm = pl.BlockSpec(memory_space=pl.ANY)
    return pl.pallas_call(
        attend,
        out_shape=jax.ShapeDtypeStruct((3 * requests, D), jnp.float32),
        in_specs=[smem, smem, vmem, hbm, hbm],
        out_specs=vmem,
        scratch_shapes=[
            pltpu.VMEM(held, jnp.bfloat16),
            pltpu.VMEM(held, jnp.bfloat16),
            pltpu.SemaphoreType.DMA((requests,)),
            pltpu.SemaphoreType.DMA((requests,)),
        ],
        compiler_params=pltpu.CompilerParams(vmem_limit_bytes=60 * 2**20),
        cost_estimate=pl.CostEstimate(flops=4 * 10**8, bytes_accessed=7 * 2**20, transcendentals=0),
        name="local_attention",
    )(page_table, lengths, queries, key_pool, value_pool)


LABELS = ((0, 0), (0, 1), (1, 0), (1, 1))


def where_held(a, b, path):
    if a == b:
        return a, a
    if a == 1:
        return path, 1 - path
    return 1 - path, path


def expert_kernel(by_slot, side_ref, gate_ref, up_ref, down_ref, *rest):
    blocks = rest[:4]
    outs = rest[4:8]
    xbuf, obuf, gbuf, ubuf, dbuf, wsem, xsem, osem = rest[8:]
    holder, core = lax.axis_index("kv"), lax.axis_index("ep") % 2
    pair = blocks[0].shape[1]
    cols = xbuf.shape[4]
    rows = 2 * pair * xbuf.shape[3]
    halves = (holder, 1 - holder)
    paths = (core, 1 - core)

    def fetch(d, labels):
        for a, b in labels:
            t, f = where_held(a, b, paths[d])
            pltpu.make_async_copy(
                blocks[2 * d + b].at[a], xbuf.at[d, f, pl.ds(t * pair, pair)], xsem.at[d, f]
            ).start()

    def load(source, buffer, kind, f):
        pltpu.make_async_copy(source.at[halves[f]], buffer.at[f], wsem.at[kind, f]).start()

    fetch(0, LABELS)
    load(gate_ref, gbuf, 0, 0)
    load(gate_ref, gbuf, 0, 1)
    load(up_ref, ubuf, 1, 0)
    load(up_ref, ubuf, 1, 1)
    for f in range(2):
        start = pl.multiple_of(halves[f] * cols, cols)
        pltpu.make_async_copy(
            down_ref.at[:, pl.ds(start, cols)], dbuf.at[f], wsem.at[2, f]
        ).start()
    fetch(1, LABELS)

    def ready(d, buffer, kind, f):
        if d == 0:
            pltpu.make_async_copy(buffer.at[f], buffer.at[f], wsem.at[kind, f]).wait()

    def came(d, f):
        pltpu.make_async_copy(xbuf.at[d, f], xbuf.at[d, f], xsem.at[d, f]).wait()

    side = side_ref[...].T
    for d in range(2):
        came(d, 0)
        first = xbuf[d, 0].reshape(rows, cols)
        ready(d, gbuf, 0, 0)
        gate = jnp.dot(first, gbuf[0], preferred_element_type=jnp.float32)
        came(d, 1)
        second = xbuf[d, 1].reshape(rows, cols)
        ready(d, gbuf, 0, 1)
        gate += jnp.dot(second, gbuf[1], preferred_element_type=jnp.float32)
        groups = [4 * i + 2 * t + d for t in range(2) for i in range(pair)]
        scale = jnp.concatenate([side[:, g : g + 1] for g in groups])
        share = jnp.concatenate([side[:, 4 * pair + g : 4 * pair + g + 1] for g in groups])
        gate *= scale
        ready(d, ubuf, 1, 0)
        up = jnp.dot(first, ubuf[0], preferred_element_type=jnp.float32)
        ready(d, ubuf, 1, 1)
        up += jnp.dot(second, ubuf[1], preferred_element_type=jnp.float32)
        up *= scale
        act = (gate / (1.0 + jnp.exp(-gate)) * up).astype(jnp.bfloat16)
        for f in range(2):
            ready(d, dbuf, 2, f)
            out = jnp.dot(act, dbuf[f], preferred_element_type=jnp.float32) * share
            obuf[d, f] = out.astype(jnp.bfloat16).reshape(2 * pair, -1, cols)
        for n, (a, b) in enumerate(LABELS):
            t, f = where_held(a, b, paths[d])
            out = outs[2 * d + b].at[:, a] if by_slot else outs[2 * d + b].at[a]
            pltpu.make_async_copy(
                obuf.at[d, f, pl.ds(t * pair, pair)], out, osem.at[4 * d + n]
            ).start()
    for n in range(8):
        pltpu.make_async_copy(
            obuf.at[0, 0, pl.ds(0, pair)], obuf.at[0, 0, pl.ds(0, pair)], osem.at[n]
        ).wait()


def run_experts(by_slot, side, gate, up, down, blocks):
    _, pair, row_count, cols = blocks[0].shape
    hidden = gate.shape[2]
    vmem = pl.BlockSpec(memory_space=pltpu.VMEM)
    hbm = pl.BlockSpec(memory_space=pl.ANY)
    shape = (pair, 2, row_count, cols) if by_slot else (2, pair, row_count, cols)

    def body(*refs):
        expert_kernel(by_slot, *refs)

    return pl.pallas_call(
        body,
        out_shape=[jax.ShapeDtypeStruct(shape, jnp.bfloat16)] * 4,
        in_specs=[vmem, hbm, hbm, hbm] + [hbm] * 4,
        out_specs=[hbm] * 4,
        scratch_shapes=[
            pltpu.VMEM((2, 2, 2 * pair, row_count, cols), jnp.bfloat16),
            pltpu.VMEM((2, 2, 2 * pair, row_count, cols), jnp.bfloat16),
            pltpu.VMEM((2, cols, hidden), jnp.bfloat16),
            pltpu.VMEM((2, cols, hidden), jnp.bfloat16),
            pltpu.VMEM((2, hidden, cols), jnp.bfloat16),
            pltpu.SemaphoreType.DMA((3, 2)),
            pltpu.SemaphoreType.DMA((2, 2)),
            pltpu.SemaphoreType.DMA((8,)),
        ],
        compiler_params=pltpu.CompilerParams(vmem_limit_bytes=60 * 2**20),
        cost_estimate=pl.CostEstimate(
            flops=4 * pair * row_count * 12 * cols * hidden,
            bytes_accessed=pair * row_count * cols * 32 + 12 * cols * hidden,
            transcendentals=0,
        ),
        name="experts",
    )(side, gate, up, down, *blocks)


def add(*parts):
    total = parts[0].astype(jnp.float32)
    for part in parts[1:]:
        total = total + part.astype(jnp.float32)
    return total.astype(jnp.bfloat16)


def dense(
    queries,
    key_pool,
    value_pool,
    page_table,
    lengths,
    prefill_attn,
    residual,
    w_out,
    norm_gain,
    router,
    w_gate,
    w_up,
    w_down,
    final_gain,
    routes,
):
    request_count = queries.shape[0]
    row_count, cols = residual.shape
    expert_count = router.shape[1]
    ep_size = lax.axis_size("ep")
    depth = ep_size // 4
    axes = ("ep", "kv")

    def number(z, y, c, x):
        return ((z * 2 + y) * 2 + c) * 2 + x

    places = [(z, y, c, x) for z in range(depth) for y in range(2) for c in range(2) for x in range(2)]

    def sent(array, target):
        return lax.ppermute(array, axes, [(number(*p), number(*target(*p))) for p in places])

    def across(array):
        return sent(array, lambda z, y, c, x: (z, y, c, 1 - x))

    def along(array, s):
        return sent(array, lambda z, y, c, x: ((z + s) % depth, y, c, x))

    def hop_one(array):
        return sent(array, lambda z, y, c, x: (z, y, c, 1 - x) if c == 0 else (z, 1 - y, c, x))

    def hop_two(array):
        return sent(array, lambda z, y, c, x: (z, 1 - y, c, x) if c == 0 else (z, y, c, 1 - x))

    def sibling(array):
        return sent(array, lambda z, y, c, x: (z, y, 1 - c, x))

    def fence(*values):
        return lax.optimization_barrier(values)

    early = (row_count - request_count) // 16 * 16

    def hidden_of(rows, part):
        product = jnp.dot(rows, w_out, preferred_element_type=jnp.float32)
        state = residual[part].astype(jnp.float32) + product
        return state, (state * norm_gain).astype(jnp.bfloat16)

    first_hidden, first_scaled = hidden_of(prefill_attn[:early], slice(0, early))
    first_one = along(first_scaled, 1)
    local = local_attention(queries, key_pool, value_pool, page_table, lengths)
    first_one, local, first_scaled = fence(first_one, local, first_scaled)

    first_two = along(first_one, 1)
    other = across(local)
    sum_one, sum_two = local[:request_count], other[:request_count]
    peak_one, peak_two = (v[request_count : 2 * request_count] for v in (local, other))
    mass_one, mass_two = (v[2 * request_count :] for v in (local, other))
    peak = jnp.maximum(peak_one, peak_two)
    factor_one, factor_two = jnp.exp(peak_one - peak), jnp.exp(peak_two - peak)
    decode_attn = (sum_one * factor_one + sum_two * factor_two) / (
        mass_one * factor_one + mass_two * factor_two
    )
    last_rows = jnp.concatenate([prefill_attn[early:], decode_attn.astype(jnp.bfloat16)], axis=0)
    last_hidden, last_scaled = hidden_of(last_rows, slice(early, row_count))
    first_two, last_scaled, last_hidden = fence(first_two, last_scaled, last_hidden)

    hidden_state = jnp.concatenate([first_hidden, last_hidden], axis=0)
    scaled = jnp.concatenate([first_scaled, last_scaled], axis=0)
    square_part = jnp.sum(hidden_state * hidden_state, axis=1)
    logit_part = jnp.dot(scaled, router, preferred_element_type=jnp.float32)
    stats = jnp.concatenate([logit_part, square_part[:, None]], axis=1).T

    slots = ((1, 2), (3, 0))
    last_one, last_two = along(last_scaled, 1), along(last_scaled, 2)
    stats = stats + across(stats)
    own_one = hop_one(scaled)
    last_one, last_two, stats, scaled, own_one = fence(last_one, last_two, stats, scaled, own_one)

    pair = jnp.stack(
        [
            jnp.concatenate([first_one, last_one], axis=0),
            jnp.concatenate([first_two, last_two], axis=0),
        ]
    )
    far_three, one = along(scaled, 3), hop_one(pair)
    inv_first = lax.rsqrt(stats[expert_count] / D + epsilon)
    logits = stats[:expert_count].T * inv_first[:, None]
    matches = routes[:, :, None] == jnp.arange(expert_count, dtype=jnp.int32)[None, None, :]
    chosen = jnp.sum(jnp.where(matches, logits[:, None, :], 0.0), axis=2)
    raised = jnp.exp(chosen)
    gate_weights = raised / jnp.sum(raised, axis=1, keepdims=True)
    by_expert = jnp.sum(jnp.where(matches, gate_weights[:, :, None], 0.0), axis=1)
    side = jnp.concatenate([by_expert, inv_first[:, None]], axis=1).T[None]
    side_s = sibling(side)
    side_y = sent(side, lambda z, y, c, x: (z, 1 - y, c, x))
    side_ys = sent(side, lambda z, y, c, x: (z, 1 - y, 1 - c, x))
    far_three, one, pair, scaled, side, side_s, side_y, side_ys = fence(
        far_three, one, pair, scaled, side, side_s, side_y, side_ys
    )

    own = lax.axis_index("ep")
    near = jnp.stack([pair, one])
    far, near_s, far_one = hop_two(near), sibling(near), hop_one(far_three)
    later_near = jnp.stack([jnp.stack([far_three, scaled]), jnp.stack([far_one, own_one])])
    side = jnp.concatenate([side, side_s, side_y, side_ys], axis=0)
    crossed = sent(side, lambda z, y, c, x: (z ^ 1, y, c, x))
    swapped = sent(jnp.stack([side, crossed]), lambda z, y, c, x: (z ^ 2, y, c, x))
    far, near_s, later_near, side, crossed, swapped = fence(
        far, near_s, later_near, side, crossed, swapped
    )

    odd = (own // 4) % 2 == 1
    before, after = jnp.where(odd, crossed, swapped[1]), jnp.where(odd, swapped[1], crossed)
    held = jnp.stack([side, before, swapped[0], after])
    share = lax.dynamic_index_in_dim(held, own, axis=2, keepdims=False)
    held = jnp.stack([held[:, :, expert_count], share]).reshape(2, depth, 2, 2, row_count)
    both = [jnp.stack([held[:, s] for s in chunk], axis=1).reshape(-1, row_count) for chunk in slots]
    gate_local = w_gate[0].reshape(2, cols, -1)
    up_local = w_up[0].reshape(2, cols, -1)
    down_local = w_down[0]
    far_s, later_far, later_near_s = sibling(far), hop_two(later_near), sibling(later_near)
    made = run_experts(False, both[0], gate_local, up_local, down_local, (near, far, near_s, far_s))
    later_far, later_near_s, later_near, made = fence(later_far, later_near_s, later_near, made)

    crossing = add(made[1], sibling(made[3]))
    later_far_s = sibling(later_far)
    crossing, later_far_s = fence(crossing, later_far_s)

    staying_s = sibling(made[2])
    arrived = hop_two(crossing)
    blocks = (later_near, later_far, later_near_s, later_far_s)
    remade = run_experts(True, both[1], gate_local, up_local, down_local, blocks)
    staying, staying_s, arrived, remade = fence(made[0], staying_s, arrived, remade)

    far_sum = add(staying[1], staying_s[1], arrived[1])
    near_sum = add(staying[0], staying_s[0], arrived[0])
    moved = hop_one(far_sum)
    crossing_s, staying_s = sibling(remade[3]), sibling(remade[2])
    crossing = [add(remade[1][i], crossing_s[i]) for i in range(2)]
    staying = [[add(remade[0][i, a], staying_s[i, a]) for a in range(2)] for i in range(2)]
    moved, near_sum, crossing, staying = fence(moved, near_sum, crossing, staying)

    whole = add(near_sum, moved)
    relayed, three_parts = along(whole[1], depth - 1), hop_two(crossing[0])
    relayed, three_parts = fence(relayed, three_parts)
    passed = along(add(whole[0], relayed), depth - 1)
    moved, zero_parts = hop_one(add(staying[0][1], three_parts[1])), hop_two(crossing[1])
    part_three = along(add(staying[0][0], three_parts[0], moved), depth - 3)
    passed, zero_parts = fence(passed, zero_parts)
    combined = hidden_state + passed.astype(jnp.float32)
    moved = hop_one(add(staying[1][1], zero_parts[1]))
    for part in (staying[1][0], zero_parts[0], moved, part_three):
        combined = combined + part.astype(jnp.float32)
    square_two = jnp.sum(combined * combined, axis=1)[None, :]
    square_two = (square_two + across(square_two))[0]
    return (combined * lax.rsqrt(square_two / D + epsilon)[:, None] * final_gain).astype(
        jnp.bfloat16
    )


def per_device(*arrays):
    row_count, expert_count = arrays[6].shape[0], arrays[9].shape[1]
    capacity = min(row_count, 2 * row_count * TOP // expert_count)
    fits = lax.axis_size("kv") == 2 and lax.axis_size("ep") == 16
    if capacity == row_count and fits:
        return dense(*arrays)
    return routed(*arrays)


def solution(mesh):
    placed = (
        P("ep", None),
        P(("ep", "kv"), None, None),
        P(("ep", "kv"), None, None),
        P("ep", "kv", None),
        P("ep"),
        P("ep", None),
        P("ep", "kv"),
        P(None, "kv"),
        P("kv"),
        P("kv", None),
        P("ep", None, "kv"),
        P("ep", None, "kv"),
        P("ep", "kv", None),
        P("kv"),
        P("ep", None),
    )
    return jax.shard_map(
        per_device, mesh=mesh, in_specs=placed, out_specs=P("ep", "kv"), check_vma=False
    )
```

```python
import math

import jax
import jax.numpy as jnp
from jax import lax
from jax.experimental import pallas as pl
from jax.experimental.pallas import tpu as pltpu
from jax.sharding import PartitionSpec as P

D = 2048
HEADS = 16
HEAD_DIM = 128
TOP = 8


epsilon = 1e-06
floor_score = -1e30


def routed(
    queries,
    key_pool,
    value_pool,
    page_table,
    lengths,
    prefill_attn,
    residual,
    w_out,
    norm_gain,
    router,
    w_gate,
    w_up,
    w_down,
    final_gain,
    routes,
):
    holders = lax.axis_size("kv")
    holder = lax.axis_index("kv")
    request_count = queries.shape[0]
    pool_pages = key_pool.shape[0]
    page_rows = key_pool.shape[1]
    pages_each = page_table.shape[2]
    query_heads = queries.reshape(request_count, HEADS, HEAD_DIM)
    page_slots = page_table[:, 0, :]
    picked_keys = key_pool.reshape(pool_pages, page_rows, HEADS, HEAD_DIM)[page_slots]
    picked_values = value_pool.reshape(pool_pages, page_rows, HEADS, HEAD_DIM)[page_slots]
    scores = jnp.einsum(
        "rhd,rjphd->rhjp", query_heads, picked_keys, preferred_element_type=jnp.float32
    ) / math.sqrt(HEAD_DIM)
    page_number = jnp.arange(pages_each, dtype=jnp.int32) * holders + holder
    position = page_number[:, None] * page_rows + jnp.arange(page_rows, dtype=jnp.int32)[None, :]
    visible = position[None, None, :, :] < lengths[:, None, None, None]
    masked = jnp.where(visible, scores, floor_score)
    local_peak = jnp.max(masked, axis=(2, 3))
    weights = jnp.where(visible, jnp.exp(masked - local_peak[:, :, None, None]), 0.0)
    local_mass = jnp.sum(weights, axis=(2, 3))
    local_sum = jnp.einsum(
        "rhjp,rjphd->rhd",
        weights,
        picked_values.astype(jnp.float32),
        precision=lax.Precision.HIGHEST,
    )
    peak_rows, masses, gathered_sums = (
        lax.all_gather(local_peak[None], "kv", axis=0, tiled=True),
        lax.all_gather(local_mass[None], "kv", axis=0, tiled=True),
        lax.all_gather(local_sum[None], "kv", axis=0, tiled=True),
    )
    all_peak = jnp.max(peak_rows, axis=0)
    factors = jnp.exp(peak_rows - all_peak[None])
    all_mass = jnp.sum(masses * factors, axis=0)
    all_sum = jnp.sum(gathered_sums * factors[..., None], axis=0)
    decode_attn = (all_sum / all_mass[..., None]).reshape(request_count, D).astype(jnp.bfloat16)
    attn_rows = jnp.concatenate([prefill_attn, decode_attn], axis=0)
    hidden_state = residual.astype(jnp.float32) + jnp.dot(
        attn_rows, w_out, preferred_element_type=jnp.float32
    )
    scaled = (hidden_state * norm_gain).astype(jnp.bfloat16)
    square_sum, logit_parts = lax.psum(
        (
            jnp.sum(hidden_state * hidden_state, axis=1),
            jnp.dot(scaled, router, preferred_element_type=jnp.float32),
        ),
        "kv",
    )
    inv_first = lax.rsqrt(square_sum / D + epsilon)
    logits = logit_parts * inv_first[:, None]
    normed = (hidden_state * norm_gain * inv_first[:, None]).astype(jnp.bfloat16)
    row_count = residual.shape[0]
    expert_count = router.shape[1]
    capacity = min(row_count, 2 * row_count * TOP // expert_count)
    matches = routes[:, :, None] == jnp.arange(expert_count, dtype=jnp.int32)[None, None, :]
    chosen = jnp.sum(jnp.where(matches, logits[:, None, :], 0.0), axis=2)
    raised = jnp.exp(chosen)
    gate_weights = raised / jnp.sum(raised, axis=1, keepdims=True)
    one_hot = matches.reshape(row_count * TOP, expert_count).astype(jnp.int32)
    earlier = jnp.cumsum(one_hot, axis=0) - one_hot
    slot_index = jnp.sum(earlier * one_hot, axis=1)
    target = routes.reshape(-1) * capacity + slot_index
    source_row = jnp.arange(row_count * TOP, dtype=jnp.int32) // TOP
    filler = jnp.zeros((expert_count * capacity,), jnp.int32).at[target].set(source_row)
    present = jnp.zeros((expert_count * capacity,), jnp.bool_).at[target].set(True)
    gate_local = w_gate[0]
    up_local = w_up[0]
    down_local = w_down[0]
    full_rows = lax.all_gather(normed, "kv", axis=1, tiled=True)
    picked = full_rows[filler]
    arrived = lax.all_to_all(
        jnp.where(present[:, None], picked, jnp.zeros_like(picked)).reshape(
            expert_count, capacity, full_rows.shape[1]
        ),
        "ep",
        split_axis=0,
        concat_axis=0,
        tiled=True,
    )
    inbound = arrived.reshape(-1, arrived.shape[2])
    gate_proj = jnp.dot(inbound, gate_local, preferred_element_type=jnp.float32)
    up_proj = jnp.dot(inbound, up_local, preferred_element_type=jnp.float32)
    activation = (jax.nn.silu(gate_proj) * up_proj).astype(jnp.bfloat16)
    feature_cols = residual.shape[1]
    summed = lax.psum_scatter(
        lax.dot_general(
            down_local, activation, (((0,), (1,)), ((), ())), preferred_element_type=jnp.float32
        ).astype(jnp.bfloat16),
        "kv",
        scatter_dimension=0,
        tiled=True,
    ).astype(jnp.float32)
    expert_out = summed.T.astype(jnp.bfloat16).reshape(
        arrived.shape[0], arrived.shape[1], feature_cols
    )
    returned = lax.all_to_all(expert_out, "ep", split_axis=0, concat_axis=0, tiled=True)
    back_rows = (
        returned.reshape(-1, feature_cols)[target]
        .reshape(row_count, TOP, feature_cols)
        .astype(jnp.float32)
    )
    combined = hidden_state + jnp.sum(back_rows * gate_weights[:, :, None], axis=1)
    square_two = lax.psum(jnp.sum(combined * combined, axis=1), "kv")
    return (combined * lax.rsqrt(square_two / D + epsilon)[:, None] * final_gain).astype(
        jnp.bfloat16
    )


def attend(slots_ref, lengths_ref, q_ref, k_ref, v_ref, out_ref, kbuf, vbuf, ksem, vsem):
    requests, pages_each, page_rows = kbuf.shape[:3]
    holder = lax.axis_index("kv")
    holders = lax.axis_size("kv")
    for r in range(requests):
        for j in range(pages_each):
            pltpu.make_async_copy(k_ref.at[slots_ref[r, 0, j]], kbuf.at[r, j], ksem.at[r]).start()
    for r in range(requests):
        for j in range(pages_each):
            pltpu.make_async_copy(v_ref.at[slots_ref[r, 0, j]], vbuf.at[r, j], vsem.at[r]).start()
    tokens = pages_each * page_rows
    wide_row = lax.broadcasted_iota(jnp.int32, (HEAD_DIM, D), 0)
    wide_head = lax.broadcasted_iota(jnp.int32, (HEAD_DIM, D), 1) // HEAD_DIM
    own_head = (wide_row == wide_head)[:HEADS]
    place = lax.broadcasted_iota(jnp.int32, (HEADS, tokens), 1)
    position = ((place // page_rows) * holders + holder) * page_rows + place % page_rows
    queries = q_ref[...].astype(jnp.float32)
    for r in range(requests):
        spread = jnp.where(wide_row == wide_head, queries[r : r + 1, :], 0.0).astype(jnp.bfloat16)
        pltpu.make_async_copy(kbuf.at[r], kbuf.at[r], ksem.at[r]).wait()
        scores = lax.dot_general(
            kbuf[r].reshape(tokens, D),
            spread,
            (((1,), (1,)), ((), ())),
            preferred_element_type=jnp.float32,
        )
        visible = position < lengths_ref[r]
        scores = jnp.where(visible, scores.T[:HEADS] / math.sqrt(HEAD_DIM), floor_score)
        peak = scores.max(axis=1, keepdims=True)
        weight = jnp.where(visible, jnp.exp(scores - peak), 0.0)
        mass = weight.sum(axis=1, keepdims=True)
        high = weight.astype(jnp.bfloat16)
        low = (weight - high.astype(jnp.float32)).astype(jnp.bfloat16)
        pltpu.make_async_copy(vbuf.at[r], vbuf.at[r], vsem.at[r]).wait()
        total = jnp.dot(
            jnp.concatenate([high, low], axis=0),
            vbuf[r].reshape(tokens, D),
            preferred_element_type=jnp.float32,
        )
        both = total[:HEADS] + total[HEADS:]
        for n, part in enumerate((both, peak, mass)):
            row = n * requests + r
            out_ref[row : row + 1, :] = jnp.sum(
                jnp.where(own_head, part, 0.0), axis=0, keepdims=True
            )


def local_attention(queries, key_pool, value_pool, page_table, lengths):
    requests, _, pages_each = page_table.shape
    held = (requests, pages_each) + key_pool.shape[1:]
    smem = pl.BlockSpec(memory_space=pltpu.SMEM)
    vmem = pl.BlockSpec(memory_space=pltpu.VMEM)
    hbm = pl.BlockSpec(memory_space=pl.ANY)
    return pl.pallas_call(
        attend,
        out_shape=jax.ShapeDtypeStruct((3 * requests, D), jnp.float32),
        in_specs=[smem, smem, vmem, hbm, hbm],
        out_specs=vmem,
        scratch_shapes=[
            pltpu.VMEM(held, jnp.bfloat16),
            pltpu.VMEM(held, jnp.bfloat16),
            pltpu.SemaphoreType.DMA((requests,)),
            pltpu.SemaphoreType.DMA((requests,)),
        ],
        compiler_params=pltpu.CompilerParams(vmem_limit_bytes=60 * 2**20),
        cost_estimate=pl.CostEstimate(flops=4 * 10**8, bytes_accessed=7 * 2**20, transcendentals=0),
        name="local_attention",
    )(page_table, lengths, queries, key_pool, value_pool)


LABELS = ((0, 0), (0, 1), (1, 0), (1, 1))


def where_held(a, b, path):
    if a == b:
        return a, a
    if a == 1:
        return path, 1 - path
    return 1 - path, path


def expert_kernel(by_slot, side_ref, gate_ref, up_ref, down_ref, *rest):
    blocks = rest[:4]
    outs = rest[4:8]
    xbuf, obuf, gbuf, ubuf, dbuf, wsem, xsem, osem = rest[8:]
    holder, core = lax.axis_index("kv"), lax.axis_index("ep") % 2
    pair = blocks[0].shape[1]
    cols = xbuf.shape[4]
    rows = 2 * pair * xbuf.shape[3]
    halves = (holder, 1 - holder)
    paths = (core, 1 - core)

    def fetch(d, labels):
        for a, b in labels:
            t, f = where_held(a, b, paths[d])
            pltpu.make_async_copy(
                blocks[2 * d + b].at[a], xbuf.at[d, f, pl.ds(t * pair, pair)], xsem.at[d, f]
            ).start()

    def load(source, buffer, kind, f):
        pltpu.make_async_copy(source.at[halves[f]], buffer.at[f], wsem.at[kind, f]).start()

    fetch(0, LABELS)
    load(gate_ref, gbuf, 0, 0)
    load(gate_ref, gbuf, 0, 1)
    load(up_ref, ubuf, 1, 0)
    load(up_ref, ubuf, 1, 1)
    for f in range(2):
        start = pl.multiple_of(halves[f] * cols, cols)
        pltpu.make_async_copy(
            down_ref.at[:, pl.ds(start, cols)], dbuf.at[f], wsem.at[2, f]
        ).start()
    fetch(1, LABELS)

    def ready(d, buffer, kind, f):
        if d == 0:
            pltpu.make_async_copy(buffer.at[f], buffer.at[f], wsem.at[kind, f]).wait()

    def came(d, f):
        pltpu.make_async_copy(xbuf.at[d, f], xbuf.at[d, f], xsem.at[d, f]).wait()

    side = side_ref[...].T
    for d in range(2):
        came(d, 0)
        first = xbuf[d, 0].reshape(rows, cols)
        ready(d, gbuf, 0, 0)
        gate = jnp.dot(first, gbuf[0], preferred_element_type=jnp.float32)
        came(d, 1)
        second = xbuf[d, 1].reshape(rows, cols)
        ready(d, gbuf, 0, 1)
        gate += jnp.dot(second, gbuf[1], preferred_element_type=jnp.float32)
        groups = [4 * i + 2 * t + d for t in range(2) for i in range(pair)]
        scale = jnp.concatenate([side[:, g : g + 1] for g in groups])
        share = jnp.concatenate([side[:, 4 * pair + g : 4 * pair + g + 1] for g in groups])
        gate *= scale
        ready(d, ubuf, 1, 0)
        up = jnp.dot(first, ubuf[0], preferred_element_type=jnp.float32)
        ready(d, ubuf, 1, 1)
        up += jnp.dot(second, ubuf[1], preferred_element_type=jnp.float32)
        up *= scale
        act = (gate / (1.0 + jnp.exp(-gate)) * up).astype(jnp.bfloat16)
        for f in range(2):
            ready(d, dbuf, 2, f)
            out = jnp.dot(act, dbuf[f], preferred_element_type=jnp.float32) * share
            obuf[d, f] = out.astype(jnp.bfloat16).reshape(2 * pair, -1, cols)
        for n, (a, b) in enumerate(LABELS):
            t, f = where_held(a, b, paths[d])
            out = outs[2 * d + b].at[:, a] if by_slot else outs[2 * d + b].at[a]
            pltpu.make_async_copy(
                obuf.at[d, f, pl.ds(t * pair, pair)], out, osem.at[4 * d + n]
            ).start()
    for n in range(8):
        pltpu.make_async_copy(
            obuf.at[0, 0, pl.ds(0, pair)], obuf.at[0, 0, pl.ds(0, pair)], osem.at[n]
        ).wait()


def run_experts(by_slot, side, gate, up, down, blocks):
    _, pair, row_count, cols = blocks[0].shape
    hidden = gate.shape[2]
    vmem = pl.BlockSpec(memory_space=pltpu.VMEM)
    hbm = pl.BlockSpec(memory_space=pl.ANY)
    shape = (pair, 2, row_count, cols) if by_slot else (2, pair, row_count, cols)

    def body(*refs):
        expert_kernel(by_slot, *refs)

    return pl.pallas_call(
        body,
        out_shape=[jax.ShapeDtypeStruct(shape, jnp.bfloat16)] * 4,
        in_specs=[vmem, hbm, hbm, hbm] + [hbm] * 4,
        out_specs=[hbm] * 4,
        scratch_shapes=[
            pltpu.VMEM((2, 2, 2 * pair, row_count, cols), jnp.bfloat16),
            pltpu.VMEM((2, 2, 2 * pair, row_count, cols), jnp.bfloat16),
            pltpu.VMEM((2, cols, hidden), jnp.bfloat16),
            pltpu.VMEM((2, cols, hidden), jnp.bfloat16),
            pltpu.VMEM((2, hidden, cols), jnp.bfloat16),
            pltpu.SemaphoreType.DMA((3, 2)),
            pltpu.SemaphoreType.DMA((2, 2)),
            pltpu.SemaphoreType.DMA((8,)),
        ],
        compiler_params=pltpu.CompilerParams(vmem_limit_bytes=34 * 2**20),
        cost_estimate=pl.CostEstimate(
            flops=4 * pair * row_count * 12 * cols * hidden,
            bytes_accessed=pair * row_count * cols * 32 + 12 * cols * hidden,
            transcendentals=0,
        ),
        name="experts",
    )(side, gate, up, down, *blocks)


def add(*parts):
    total = parts[0].astype(jnp.float32)
    for part in parts[1:]:
        total = total + part.astype(jnp.float32)
    return total.astype(jnp.bfloat16)


def dense(
    queries,
    key_pool,
    value_pool,
    page_table,
    lengths,
    prefill_attn,
    residual,
    w_out,
    norm_gain,
    router,
    w_gate,
    w_up,
    w_down,
    final_gain,
    routes,
):
    request_count = queries.shape[0]
    row_count, cols = residual.shape
    expert_count = router.shape[1]
    ep_size = lax.axis_size("ep")
    depth = ep_size // 4
    axes = ("ep", "kv")

    def number(z, y, c, x):
        return ((z * 2 + y) * 2 + c) * 2 + x

    places = [(z, y, c, x) for z in range(depth) for y in range(2) for c in range(2) for x in range(2)]

    def sent(array, target):
        return lax.ppermute(array, axes, [(number(*p), number(*target(*p))) for p in places])

    def across(array):
        return sent(array, lambda z, y, c, x: (z, y, c, 1 - x))

    def along(array, s):
        return sent(array, lambda z, y, c, x: ((z + s) % depth, y, c, x))

    def hop_one(array):
        return sent(array, lambda z, y, c, x: (z, y, c, 1 - x) if c == 0 else (z, 1 - y, c, x))

    def hop_two(array):
        return sent(array, lambda z, y, c, x: (z, 1 - y, c, x) if c == 0 else (z, y, c, 1 - x))

    def sibling(array):
        return sent(array, lambda z, y, c, x: (z, y, 1 - c, x))

    def fence(*values):
        return lax.optimization_barrier(values)

    early = (row_count - request_count) // 16 * 16

    def hidden_of(rows, part):
        product = jnp.dot(rows, w_out, preferred_element_type=jnp.float32)
        state = residual[part].astype(jnp.float32) + product
        return state, (state * norm_gain).astype(jnp.bfloat16)

    first_hidden, first_scaled = hidden_of(prefill_attn[:early], slice(0, early))
    first_one = along(first_scaled, 1)
    local = local_attention(queries, key_pool, value_pool, page_table, lengths)
    first_one, local, first_scaled = fence(first_one, local, first_scaled)

    first_two = along(first_one, 1)
    other = across(local)
    sum_one, sum_two = local[:request_count], other[:request_count]
    peak_one, peak_two = (v[request_count : 2 * request_count] for v in (local, other))
    mass_one, mass_two = (v[2 * request_count :] for v in (local, other))
    peak = jnp.maximum(peak_one, peak_two)
    factor_one, factor_two = jnp.exp(peak_one - peak), jnp.exp(peak_two - peak)
    decode_attn = (sum_one * factor_one + sum_two * factor_two) / (
        mass_one * factor_one + mass_two * factor_two
    )
    last_rows = jnp.concatenate([prefill_attn[early:], decode_attn.astype(jnp.bfloat16)], axis=0)
    last_hidden, last_scaled = hidden_of(last_rows, slice(early, row_count))
    first_two, last_scaled, last_hidden = fence(first_two, last_scaled, last_hidden)

    hidden_state = jnp.concatenate([first_hidden, last_hidden], axis=0)
    scaled = jnp.concatenate([first_scaled, last_scaled], axis=0)
    square_part = jnp.sum(hidden_state * hidden_state, axis=1)
    logit_part = jnp.dot(scaled, router, preferred_element_type=jnp.float32)
    stats = jnp.concatenate([logit_part, square_part[:, None]], axis=1).T

    slots = ((1, 2), (3, 0))
    last_one, last_two = along(last_scaled, 1), along(last_scaled, 2)
    stats = stats + across(stats)
    own_one = hop_one(scaled)
    last_one, last_two, stats, scaled, own_one = fence(last_one, last_two, stats, scaled, own_one)

    pair = jnp.stack(
        [
            jnp.concatenate([first_one, last_one], axis=0),
            jnp.concatenate([first_two, last_two], axis=0),
        ]
    )
    far_three, one = along(scaled, 3), hop_one(pair)
    inv_first = lax.rsqrt(stats[expert_count] / D + epsilon)
    logits = stats[:expert_count].T * inv_first[:, None]
    matches = routes[:, :, None] == jnp.arange(expert_count, dtype=jnp.int32)[None, None, :]
    chosen = jnp.sum(jnp.where(matches, logits[:, None, :], 0.0), axis=2)
    raised = jnp.exp(chosen)
    gate_weights = raised / jnp.sum(raised, axis=1, keepdims=True)
    by_expert = jnp.sum(jnp.where(matches, gate_weights[:, :, None], 0.0), axis=1)
    side = jnp.concatenate([by_expert, inv_first[:, None]], axis=1).T[None]
    side_s = sibling(side)
    side_y = sent(side, lambda z, y, c, x: (z, 1 - y, c, x))
    side_ys = sent(side, lambda z, y, c, x: (z, 1 - y, 1 - c, x))
    far_three, one, pair, scaled, side, side_s, side_y, side_ys = fence(
        far_three, one, pair, scaled, side, side_s, side_y, side_ys
    )

    own = lax.axis_index("ep")
    near = jnp.stack([pair, one])
    far, near_s, far_one = hop_two(near), sibling(near), hop_one(far_three)
    later_near = jnp.stack([jnp.stack([far_three, scaled]), jnp.stack([far_one, own_one])])
    side = jnp.concatenate([side, side_s, side_y, side_ys], axis=0)
    crossed = sent(side, lambda z, y, c, x: (z ^ 1, y, c, x))
    swapped = sent(jnp.stack([side, crossed]), lambda z, y, c, x: (z ^ 2, y, c, x))
    far, near_s, later_near, side, crossed, swapped = fence(
        far, near_s, later_near, side, crossed, swapped
    )

    odd = (own // 4) % 2 == 1
    before, after = jnp.where(odd, crossed, swapped[1]), jnp.where(odd, swapped[1], crossed)
    held = jnp.stack([side, before, swapped[0], after])
    share = lax.dynamic_index_in_dim(held, own, axis=2, keepdims=False)
    held = jnp.stack([held[:, :, expert_count], share]).reshape(2, depth, 2, 2, row_count)
    both = [jnp.stack([held[:, s] for s in chunk], axis=1).reshape(-1, row_count) for chunk in slots]
    gate_local = w_gate[0].reshape(2, cols, -1)
    up_local = w_up[0].reshape(2, cols, -1)
    down_local = w_down[0]
    far_s, later_far, later_near_s = sibling(far), hop_two(later_near), sibling(later_near)
    made = run_experts(False, both[0], gate_local, up_local, down_local, (near, far, near_s, far_s))
    later_far, later_near_s, later_near, made = fence(later_far, later_near_s, later_near, made)

    crossing = add(made[1], sibling(made[3]))
    later_far_s = sibling(later_far)
    crossing, later_far_s = fence(crossing, later_far_s)

    staying_s = sibling(made[2])
    arrived = hop_two(crossing)
    blocks = (later_near, later_far, later_near_s, later_far_s)
    remade = run_experts(True, both[1], gate_local, up_local, down_local, blocks)
    staying, staying_s, arrived, remade = fence(made[0], staying_s, arrived, remade)

    far_sum = add(staying[1], staying_s[1], arrived[1])
    moved = hop_one(far_sum)
    far_sum, near_parts = fence(far_sum, (staying[0], staying_s[0], arrived[0]))
    near_sum = add(*near_parts)
    crossing_s, staying_s = sibling(remade[3]), sibling(remade[2])
    crossing = [add(remade[1][i], crossing_s[i]) for i in range(2)]
    staying = [[add(remade[0][i, a], staying_s[i, a]) for a in range(2)] for i in range(2)]
    moved, near_sum, crossing, staying = fence(moved, near_sum, crossing, staying)

    whole = add(near_sum, moved)
    relayed, three_parts = along(whole[1], depth - 1), hop_two(crossing[0])
    relayed, three_parts = fence(relayed, three_parts)
    passed = along(add(whole[0], relayed), depth - 1)
    moved, zero_parts = hop_one(add(staying[0][1], three_parts[1])), hop_two(crossing[1])
    part_three = along(add(staying[0][0], three_parts[0], moved), depth - 3)
    passed, zero_parts = fence(passed, zero_parts)
    combined = hidden_state + passed.astype(jnp.float32)
    moved = hop_one(add(staying[1][1], zero_parts[1]))
    for part in (staying[1][0], zero_parts[0], moved, part_three):
        combined = combined + part.astype(jnp.float32)
    square_two = jnp.sum(combined * combined, axis=1)[None, :]
    square_two = (square_two + across(square_two))[0]
    return (combined * lax.rsqrt(square_two / D + epsilon)[:, None] * final_gain).astype(
        jnp.bfloat16
    )


def per_device(*arrays):
    row_count, expert_count = arrays[6].shape[0], arrays[9].shape[1]
    capacity = min(row_count, 2 * row_count * TOP // expert_count)
    fits = lax.axis_size("kv") == 2 and lax.axis_size("ep") == 16
    if capacity == row_count and fits:
        return dense(*arrays)
    return routed(*arrays)


def solution(mesh):
    placed = (
        P("ep", None),
        P(("ep", "kv"), None, None),
        P(("ep", "kv"), None, None),
        P("ep", "kv", None),
        P("ep"),
        P("ep", None),
        P("ep", "kv"),
        P(None, "kv"),
        P("kv"),
        P("kv", None),
        P("ep", None, "kv"),
        P("ep", None, "kv"),
        P("ep", "kv", None),
        P("kv"),
        P("ep", None),
    )
    return jax.shard_map(
        per_device, mesh=mesh, in_specs=placed, out_specs=P("ep", "kv"), check_vma=False
    )
```

```python
import math

import jax
import jax.numpy as jnp
from jax import lax
from jax.experimental import pallas as pl
from jax.experimental.pallas import tpu as pltpu
from jax.sharding import PartitionSpec as P

D = 2048
HEADS = 16
HEAD_DIM = 128
TOP = 8


epsilon = 1e-06
floor_score = -1e30


def routed(
    queries,
    key_pool,
    value_pool,
    page_table,
    lengths,
    prefill_attn,
    residual,
    w_out,
    norm_gain,
    router,
    w_gate,
    w_up,
    w_down,
    final_gain,
    routes,
):
    holders = lax.axis_size("kv")
    holder = lax.axis_index("kv")
    request_count = queries.shape[0]
    pool_pages = key_pool.shape[0]
    page_rows = key_pool.shape[1]
    pages_each = page_table.shape[2]
    query_heads = queries.reshape(request_count, HEADS, HEAD_DIM)
    page_slots = page_table[:, 0, :]
    picked_keys = key_pool.reshape(pool_pages, page_rows, HEADS, HEAD_DIM)[page_slots]
    picked_values = value_pool.reshape(pool_pages, page_rows, HEADS, HEAD_DIM)[page_slots]
    scores = jnp.einsum(
        "rhd,rjphd->rhjp", query_heads, picked_keys, preferred_element_type=jnp.float32
    ) / math.sqrt(HEAD_DIM)
    page_number = jnp.arange(pages_each, dtype=jnp.int32) * holders + holder
    position = page_number[:, None] * page_rows + jnp.arange(page_rows, dtype=jnp.int32)[None, :]
    visible = position[None, None, :, :] < lengths[:, None, None, None]
    masked = jnp.where(visible, scores, floor_score)
    local_peak = jnp.max(masked, axis=(2, 3))
    weights = jnp.where(visible, jnp.exp(masked - local_peak[:, :, None, None]), 0.0)
    local_mass = jnp.sum(weights, axis=(2, 3))
    local_sum = jnp.einsum(
        "rhjp,rjphd->rhd",
        weights,
        picked_values.astype(jnp.float32),
        precision=lax.Precision.HIGHEST,
    )
    peak_rows, masses, gathered_sums = (
        lax.all_gather(local_peak[None], "kv", axis=0, tiled=True),
        lax.all_gather(local_mass[None], "kv", axis=0, tiled=True),
        lax.all_gather(local_sum[None], "kv", axis=0, tiled=True),
    )
    all_peak = jnp.max(peak_rows, axis=0)
    factors = jnp.exp(peak_rows - all_peak[None])
    all_mass = jnp.sum(masses * factors, axis=0)
    all_sum = jnp.sum(gathered_sums * factors[..., None], axis=0)
    decode_attn = (all_sum / all_mass[..., None]).reshape(request_count, D).astype(jnp.bfloat16)
    attn_rows = jnp.concatenate([prefill_attn, decode_attn], axis=0)
    hidden_state = residual.astype(jnp.float32) + jnp.dot(
        attn_rows, w_out, preferred_element_type=jnp.float32
    )
    scaled = (hidden_state * norm_gain).astype(jnp.bfloat16)
    square_sum, logit_parts = lax.psum(
        (
            jnp.sum(hidden_state * hidden_state, axis=1),
            jnp.dot(scaled, router, preferred_element_type=jnp.float32),
        ),
        "kv",
    )
    inv_first = lax.rsqrt(square_sum / D + epsilon)
    logits = logit_parts * inv_first[:, None]
    normed = (hidden_state * norm_gain * inv_first[:, None]).astype(jnp.bfloat16)
    row_count = residual.shape[0]
    expert_count = router.shape[1]
    capacity = min(row_count, 2 * row_count * TOP // expert_count)
    matches = routes[:, :, None] == jnp.arange(expert_count, dtype=jnp.int32)[None, None, :]
    chosen = jnp.sum(jnp.where(matches, logits[:, None, :], 0.0), axis=2)
    raised = jnp.exp(chosen)
    gate_weights = raised / jnp.sum(raised, axis=1, keepdims=True)
    one_hot = matches.reshape(row_count * TOP, expert_count).astype(jnp.int32)
    earlier = jnp.cumsum(one_hot, axis=0) - one_hot
    slot_index = jnp.sum(earlier * one_hot, axis=1)
    target = routes.reshape(-1) * capacity + slot_index
    source_row = jnp.arange(row_count * TOP, dtype=jnp.int32) // TOP
    filler = jnp.zeros((expert_count * capacity,), jnp.int32).at[target].set(source_row)
    present = jnp.zeros((expert_count * capacity,), jnp.bool_).at[target].set(True)
    gate_local = w_gate[0]
    up_local = w_up[0]
    down_local = w_down[0]
    full_rows = lax.all_gather(normed, "kv", axis=1, tiled=True)
    picked = full_rows[filler]
    arrived = lax.all_to_all(
        jnp.where(present[:, None], picked, jnp.zeros_like(picked)).reshape(
            expert_count, capacity, full_rows.shape[1]
        ),
        "ep",
        split_axis=0,
        concat_axis=0,
        tiled=True,
    )
    inbound = arrived.reshape(-1, arrived.shape[2])
    gate_proj = jnp.dot(inbound, gate_local, preferred_element_type=jnp.float32)
    up_proj = jnp.dot(inbound, up_local, preferred_element_type=jnp.float32)
    activation = (jax.nn.silu(gate_proj) * up_proj).astype(jnp.bfloat16)
    feature_cols = residual.shape[1]
    summed = lax.psum_scatter(
        lax.dot_general(
            down_local, activation, (((0,), (1,)), ((), ())), preferred_element_type=jnp.float32
        ).astype(jnp.bfloat16),
        "kv",
        scatter_dimension=0,
        tiled=True,
    ).astype(jnp.float32)
    expert_out = summed.T.astype(jnp.bfloat16).reshape(
        arrived.shape[0], arrived.shape[1], feature_cols
    )
    returned = lax.all_to_all(expert_out, "ep", split_axis=0, concat_axis=0, tiled=True)
    back_rows = (
        returned.reshape(-1, feature_cols)[target]
        .reshape(row_count, TOP, feature_cols)
        .astype(jnp.float32)
    )
    combined = hidden_state + jnp.sum(back_rows * gate_weights[:, :, None], axis=1)
    square_two = lax.psum(jnp.sum(combined * combined, axis=1), "kv")
    return (combined * lax.rsqrt(square_two / D + epsilon)[:, None] * final_gain).astype(
        jnp.bfloat16
    )


def attend(slots_ref, lengths_ref, q_ref, k_ref, v_ref, out_ref, kbuf, vbuf, ksem, vsem):
    requests, pages_each, page_rows = kbuf.shape[:3]
    holder = lax.axis_index("kv")
    holders = lax.axis_size("kv")
    for r in range(requests):
        for j in range(pages_each):
            pltpu.make_async_copy(k_ref.at[slots_ref[r, 0, j]], kbuf.at[r, j], ksem.at[r]).start()
    for r in range(requests):
        for j in range(pages_each):
            pltpu.make_async_copy(v_ref.at[slots_ref[r, 0, j]], vbuf.at[r, j], vsem.at[r]).start()
    tokens = pages_each * page_rows
    wide_row = lax.broadcasted_iota(jnp.int32, (HEAD_DIM, D), 0)
    wide_head = lax.broadcasted_iota(jnp.int32, (HEAD_DIM, D), 1) // HEAD_DIM
    own_head = (wide_row == wide_head)[:HEADS]
    place = lax.broadcasted_iota(jnp.int32, (HEADS, tokens), 1)
    position = ((place // page_rows) * holders + holder) * page_rows + place % page_rows
    queries = q_ref[...].astype(jnp.float32)
    for r in range(requests):
        spread = jnp.where(wide_row == wide_head, queries[r : r + 1, :], 0.0).astype(jnp.bfloat16)
        pltpu.make_async_copy(kbuf.at[r], kbuf.at[r], ksem.at[r]).wait()
        scores = lax.dot_general(
            kbuf[r].reshape(tokens, D),
            spread,
            (((1,), (1,)), ((), ())),
            preferred_element_type=jnp.float32,
        )
        visible = position < lengths_ref[r]
        scores = jnp.where(visible, scores.T[:HEADS] / math.sqrt(HEAD_DIM), floor_score)
        peak = scores.max(axis=1, keepdims=True)
        weight = jnp.where(visible, jnp.exp(scores - peak), 0.0)
        mass = weight.sum(axis=1, keepdims=True)
        high = weight.astype(jnp.bfloat16)
        low = (weight - high.astype(jnp.float32)).astype(jnp.bfloat16)
        pltpu.make_async_copy(vbuf.at[r], vbuf.at[r], vsem.at[r]).wait()
        total = jnp.dot(
            jnp.concatenate([high, low], axis=0),
            vbuf[r].reshape(tokens, D),
            preferred_element_type=jnp.float32,
        )
        both = total[:HEADS] + total[HEADS:]
        for n, part in enumerate((both, peak, mass)):
            row = n * requests + r
            out_ref[row : row + 1, :] = jnp.sum(
                jnp.where(own_head, part, 0.0), axis=0, keepdims=True
            )


def local_attention(queries, key_pool, value_pool, page_table, lengths):
    requests, _, pages_each = page_table.shape
    held = (requests, pages_each) + key_pool.shape[1:]
    smem = pl.BlockSpec(memory_space=pltpu.SMEM)
    vmem = pl.BlockSpec(memory_space=pltpu.VMEM)
    hbm = pl.BlockSpec(memory_space=pl.ANY)
    return pl.pallas_call(
        attend,
        out_shape=jax.ShapeDtypeStruct((3 * requests, D), jnp.float32),
        in_specs=[smem, smem, vmem, hbm, hbm],
        out_specs=vmem,
        scratch_shapes=[
            pltpu.VMEM(held, jnp.bfloat16),
            pltpu.VMEM(held, jnp.bfloat16),
            pltpu.SemaphoreType.DMA((requests,)),
            pltpu.SemaphoreType.DMA((requests,)),
        ],
        compiler_params=pltpu.CompilerParams(vmem_limit_bytes=60 * 2**20),
        cost_estimate=pl.CostEstimate(flops=4 * 10**8, bytes_accessed=7 * 2**20, transcendentals=0),
        name="local_attention",
    )(page_table, lengths, queries, key_pool, value_pool)


LABELS = ((0, 0), (0, 1), (1, 0), (1, 1))


def where_held(a, b, path):
    if a == b:
        return a, a
    if a == 1:
        return path, 1 - path
    return 1 - path, path


def expert_kernel(by_slot, side_ref, gate_ref, up_ref, down_ref, *rest):
    blocks = rest[:4]
    outs = rest[4:8]
    xbuf, obuf, gbuf, ubuf, dbuf, wsem, xsem, osem = rest[8:]
    holder, core = lax.axis_index("kv"), lax.axis_index("ep") % 2
    pair = blocks[0].shape[1]
    cols = xbuf.shape[4]
    rows = 2 * pair * xbuf.shape[3]
    halves = (holder, 1 - holder)
    paths = (core, 1 - core)

    def fetch(d, labels):
        for a, b in labels:
            t, f = where_held(a, b, paths[d])
            pltpu.make_async_copy(
                blocks[2 * d + b].at[a], xbuf.at[d, f, pl.ds(t * pair, pair)], xsem.at[d, f]
            ).start()

    def load(source, buffer, kind, f):
        pltpu.make_async_copy(source.at[halves[f]], buffer.at[f], wsem.at[kind, f]).start()

    fetch(0, LABELS)
    load(gate_ref, gbuf, 0, 0)
    load(gate_ref, gbuf, 0, 1)
    load(up_ref, ubuf, 1, 0)
    load(up_ref, ubuf, 1, 1)
    for f in range(2):
        start = pl.multiple_of(halves[f] * cols, cols)
        pltpu.make_async_copy(
            down_ref.at[:, pl.ds(start, cols)], dbuf.at[f], wsem.at[2, f]
        ).start()
    fetch(1, LABELS)

    def ready(d, buffer, kind, f):
        if d == 0:
            pltpu.make_async_copy(buffer.at[f], buffer.at[f], wsem.at[kind, f]).wait()

    def came(d, f):
        pltpu.make_async_copy(xbuf.at[d, f], xbuf.at[d, f], xsem.at[d, f]).wait()

    side = side_ref[...].T
    for d in range(2):
        came(d, 0)
        first = xbuf[d, 0].reshape(rows, cols)
        ready(d, gbuf, 0, 0)
        gate = jnp.dot(first, gbuf[0], preferred_element_type=jnp.float32)
        came(d, 1)
        second = xbuf[d, 1].reshape(rows, cols)
        ready(d, gbuf, 0, 1)
        gate += jnp.dot(second, gbuf[1], preferred_element_type=jnp.float32)
        groups = [4 * i + 2 * t + d for t in range(2) for i in range(pair)]
        scale = jnp.concatenate([side[:, g : g + 1] for g in groups])
        share = jnp.concatenate([side[:, 4 * pair + g : 4 * pair + g + 1] for g in groups])
        gate *= scale
        ready(d, ubuf, 1, 0)
        up = jnp.dot(first, ubuf[0], preferred_element_type=jnp.float32)
        ready(d, ubuf, 1, 1)
        up += jnp.dot(second, ubuf[1], preferred_element_type=jnp.float32)
        up *= scale
        act = (gate / (1.0 + jnp.exp(-gate)) * up).astype(jnp.bfloat16)
        for f in range(2):
            ready(d, dbuf, 2, f)
            out = jnp.dot(act, dbuf[f], preferred_element_type=jnp.float32) * share
            obuf[d, f] = out.astype(jnp.bfloat16).reshape(2 * pair, -1, cols)
        for n, (a, b) in enumerate(LABELS):
            t, f = where_held(a, b, paths[d])
            out = outs[2 * d + b].at[:, a] if by_slot else outs[2 * d + b].at[a]
            pltpu.make_async_copy(
                obuf.at[d, f, pl.ds(t * pair, pair)], out, osem.at[4 * d + n]
            ).start()
    for n in range(8):
        pltpu.make_async_copy(
            obuf.at[0, 0, pl.ds(0, pair)], obuf.at[0, 0, pl.ds(0, pair)], osem.at[n]
        ).wait()


def run_experts(by_slot, side, gate, up, down, blocks):
    _, pair, row_count, cols = blocks[0].shape
    hidden = gate.shape[2]
    vmem = pl.BlockSpec(memory_space=pltpu.VMEM)
    hbm = pl.BlockSpec(memory_space=pl.ANY)
    shape = (pair, 2, row_count, cols) if by_slot else (2, pair, row_count, cols)

    def body(*refs):
        expert_kernel(by_slot, *refs)

    return pl.pallas_call(
        body,
        out_shape=[jax.ShapeDtypeStruct(shape, jnp.bfloat16)] * 4,
        in_specs=[vmem, hbm, hbm, hbm] + [hbm] * 4,
        out_specs=[hbm] * 4,
        scratch_shapes=[
            pltpu.VMEM((2, 2, 2 * pair, row_count, cols), jnp.bfloat16),
            pltpu.VMEM((2, 2, 2 * pair, row_count, cols), jnp.bfloat16),
            pltpu.VMEM((2, cols, hidden), jnp.bfloat16),
            pltpu.VMEM((2, cols, hidden), jnp.bfloat16),
            pltpu.VMEM((2, hidden, cols), jnp.bfloat16),
            pltpu.SemaphoreType.DMA((3, 2)),
            pltpu.SemaphoreType.DMA((2, 2)),
            pltpu.SemaphoreType.DMA((8,)),
        ],
        compiler_params=pltpu.CompilerParams(vmem_limit_bytes=44 * 2**20),
        cost_estimate=pl.CostEstimate(
            flops=4 * pair * row_count * 12 * cols * hidden,
            bytes_accessed=pair * row_count * cols * 32 + 12 * cols * hidden,
            transcendentals=0,
        ),
        name="experts",
    )(side, gate, up, down, *blocks)


def add(*parts):
    total = parts[0].astype(jnp.float32)
    for part in parts[1:]:
        total = total + part.astype(jnp.float32)
    return total.astype(jnp.bfloat16)


def dense(
    queries,
    key_pool,
    value_pool,
    page_table,
    lengths,
    prefill_attn,
    residual,
    w_out,
    norm_gain,
    router,
    w_gate,
    w_up,
    w_down,
    final_gain,
    routes,
):
    request_count = queries.shape[0]
    row_count, cols = residual.shape
    expert_count = router.shape[1]
    ep_size = lax.axis_size("ep")
    depth = ep_size // 4
    axes = ("ep", "kv")

    def number(z, y, c, x):
        return ((z * 2 + y) * 2 + c) * 2 + x

    places = [(z, y, c, x) for z in range(depth) for y in range(2) for c in range(2) for x in range(2)]

    def sent(array, target):
        return lax.ppermute(array, axes, [(number(*p), number(*target(*p))) for p in places])

    def across(array):
        return sent(array, lambda z, y, c, x: (z, y, c, 1 - x))

    def along(array, s):
        return sent(array, lambda z, y, c, x: ((z + s) % depth, y, c, x))

    def hop_one(array):
        return sent(array, lambda z, y, c, x: (z, y, c, 1 - x) if c == 0 else (z, 1 - y, c, x))

    def hop_two(array):
        return sent(array, lambda z, y, c, x: (z, 1 - y, c, x) if c == 0 else (z, y, c, 1 - x))

    def sibling(array):
        return sent(array, lambda z, y, c, x: (z, y, 1 - c, x))

    def fence(*values):
        return lax.optimization_barrier(values)

    early = (row_count - request_count) // 16 * 16

    def hidden_of(rows, part):
        product = jnp.dot(rows, w_out, preferred_element_type=jnp.float32)
        state = residual[part].astype(jnp.float32) + product
        return state, (state * norm_gain).astype(jnp.bfloat16)

    first_hidden, first_scaled = hidden_of(prefill_attn[:early], slice(0, early))
    first_one = along(first_scaled, 1)
    local = local_attention(queries, key_pool, value_pool, page_table, lengths)
    first_one, local, first_scaled = fence(first_one, local, first_scaled)

    first_two = along(first_one, 1)
    other = across(local)
    sum_one, sum_two = local[:request_count], other[:request_count]
    peak_one, peak_two = (v[request_count : 2 * request_count] for v in (local, other))
    mass_one, mass_two = (v[2 * request_count :] for v in (local, other))
    peak = jnp.maximum(peak_one, peak_two)
    factor_one, factor_two = jnp.exp(peak_one - peak), jnp.exp(peak_two - peak)
    decode_attn = (sum_one * factor_one + sum_two * factor_two) / (
        mass_one * factor_one + mass_two * factor_two
    )
    last_rows = jnp.concatenate([prefill_attn[early:], decode_attn.astype(jnp.bfloat16)], axis=0)
    last_hidden, last_scaled = hidden_of(last_rows, slice(early, row_count))
    first_two, last_scaled, last_hidden = fence(first_two, last_scaled, last_hidden)

    hidden_state = jnp.concatenate([first_hidden, last_hidden], axis=0)
    scaled = jnp.concatenate([first_scaled, last_scaled], axis=0)
    square_part = jnp.sum(hidden_state * hidden_state, axis=1)
    logit_part = jnp.dot(scaled, router, preferred_element_type=jnp.float32)
    stats = jnp.concatenate([logit_part, square_part[:, None]], axis=1).T

    slots = ((1, 2), (3, 0))
    last_one, last_two = along(last_scaled, 1), along(last_scaled, 2)
    stats = stats + across(stats)
    own_one = hop_one(scaled)
    last_one, last_two, stats, scaled, own_one = fence(last_one, last_two, stats, scaled, own_one)

    pair = jnp.stack(
        [
            jnp.concatenate([first_one, last_one], axis=0),
            jnp.concatenate([first_two, last_two], axis=0),
        ]
    )
    far_three, one = along(scaled, 3), hop_one(pair)
    inv_first = lax.rsqrt(stats[expert_count] / D + epsilon)
    logits = stats[:expert_count].T * inv_first[:, None]
    matches = routes[:, :, None] == jnp.arange(expert_count, dtype=jnp.int32)[None, None, :]
    chosen = jnp.sum(jnp.where(matches, logits[:, None, :], 0.0), axis=2)
    raised = jnp.exp(chosen)
    gate_weights = raised / jnp.sum(raised, axis=1, keepdims=True)
    by_expert = jnp.sum(jnp.where(matches, gate_weights[:, :, None], 0.0), axis=1)
    side = jnp.concatenate([by_expert, inv_first[:, None]], axis=1).T[None]
    side_s = sibling(side)
    side_y = sent(side, lambda z, y, c, x: (z, 1 - y, c, x))
    side_ys = sent(side, lambda z, y, c, x: (z, 1 - y, 1 - c, x))
    far_three, one, pair, scaled, side, side_s, side_y, side_ys = fence(
        far_three, one, pair, scaled, side, side_s, side_y, side_ys
    )

    own = lax.axis_index("ep")
    near = jnp.stack([pair, one])
    far, near_s, far_one = hop_two(near), sibling(near), hop_one(far_three)
    later_near = jnp.stack([jnp.stack([far_three, scaled]), jnp.stack([far_one, own_one])])
    side = jnp.concatenate([side, side_s, side_y, side_ys], axis=0)
    crossed = sent(side, lambda z, y, c, x: (z ^ 1, y, c, x))
    swapped = sent(jnp.stack([side, crossed]), lambda z, y, c, x: (z ^ 2, y, c, x))
    far, near_s, later_near, side, crossed, swapped = fence(
        far, near_s, later_near, side, crossed, swapped
    )

    odd = (own // 4) % 2 == 1
    before, after = jnp.where(odd, crossed, swapped[1]), jnp.where(odd, swapped[1], crossed)
    held = jnp.stack([side, before, swapped[0], after])
    share = lax.dynamic_index_in_dim(held, own, axis=2, keepdims=False)
    held = jnp.stack([held[:, :, expert_count], share]).reshape(2, depth, 2, 2, row_count)
    both = [jnp.stack([held[:, s] for s in chunk], axis=1).reshape(-1, row_count) for chunk in slots]
    gate_local = w_gate[0].reshape(2, cols, -1)
    up_local = w_up[0].reshape(2, cols, -1)
    down_local = w_down[0]
    far_s, later_far, later_near_s = sibling(far), hop_two(later_near), sibling(later_near)
    made = run_experts(False, both[0], gate_local, up_local, down_local, (near, far, near_s, far_s))
    later_far, later_near_s, later_near, made = fence(later_far, later_near_s, later_near, made)

    crossing = add(made[1], sibling(made[3]))
    later_far_s = sibling(later_far)
    crossing, later_far_s = fence(crossing, later_far_s)

    staying_s = sibling(made[2])
    arrived = hop_two(crossing)
    blocks = (later_near, later_far, later_near_s, later_far_s)
    remade = run_experts(True, both[1], gate_local, up_local, down_local, blocks)
    staying, staying_s, arrived, remade = fence(made[0], staying_s, arrived, remade)

    far_sum = add(staying[1], staying_s[1], arrived[1])
    moved = hop_one(far_sum)
    far_sum, near_parts = fence(far_sum, (staying[0], staying_s[0], arrived[0]))
    near_sum = add(*near_parts)
    crossing_s, staying_s = sibling(remade[3]), sibling(remade[2])
    crossing = [add(remade[1][i], crossing_s[i]) for i in range(2)]
    staying = [[add(remade[0][i, a], staying_s[i, a]) for a in range(2)] for i in range(2)]
    moved, near_sum, crossing, staying = fence(moved, near_sum, crossing, staying)

    whole = add(near_sum, moved)
    relayed, three_parts = along(whole[1], depth - 1), hop_two(crossing[0])
    relayed, three_parts = fence(relayed, three_parts)
    passed = along(add(whole[0], relayed), depth - 1)
    moved, zero_parts = hop_one(add(staying[0][1], three_parts[1])), hop_two(crossing[1])
    part_three = along(add(staying[0][0], three_parts[0], moved), depth - 3)
    passed, zero_parts = fence(passed, zero_parts)
    combined = hidden_state + passed.astype(jnp.float32)
    moved = hop_one(add(staying[1][1], zero_parts[1]))
    for part in (staying[1][0], zero_parts[0], moved, part_three):
        combined = combined + part.astype(jnp.float32)
    square_two = jnp.sum(combined * combined, axis=1)[None, :]
    square_two = (square_two + across(square_two))[0]
    return (combined * lax.rsqrt(square_two / D + epsilon)[:, None] * final_gain).astype(
        jnp.bfloat16
    )


def per_device(*arrays):
    row_count, expert_count = arrays[6].shape[0], arrays[9].shape[1]
    capacity = min(row_count, 2 * row_count * TOP // expert_count)
    fits = lax.axis_size("kv") == 2 and lax.axis_size("ep") == 16
    if capacity == row_count and fits:
        return dense(*arrays)
    return routed(*arrays)


def solution(mesh):
    placed = (
        P("ep", None),
        P(("ep", "kv"), None, None),
        P(("ep", "kv"), None, None),
        P("ep", "kv", None),
        P("ep"),
        P("ep", None),
        P("ep", "kv"),
        P(None, "kv"),
        P("kv"),
        P("kv", None),
        P("ep", None, "kv"),
        P("ep", None, "kv"),
        P("ep", "kv", None),
        P("kv"),
        P("ep", None),
    )
    return jax.shard_map(
        per_device, mesh=mesh, in_specs=placed, out_specs=P("ep", "kv"), check_vma=False
    )
```

```python
import math

import jax
import jax.numpy as jnp
from jax import lax
from jax.experimental import pallas as pl
from jax.experimental.pallas import tpu as pltpu
from jax.sharding import PartitionSpec as P

D = 2048
HEADS = 16
HEAD_DIM = 128
TOP = 8


epsilon = 1e-06
floor_score = -1e30


def routed(
    queries,
    key_pool,
    value_pool,
    page_table,
    lengths,
    prefill_attn,
    residual,
    w_out,
    norm_gain,
    router,
    w_gate,
    w_up,
    w_down,
    final_gain,
    routes,
):
    holders = lax.axis_size("kv")
    holder = lax.axis_index("kv")
    request_count = queries.shape[0]
    pool_pages = key_pool.shape[0]
    page_rows = key_pool.shape[1]
    pages_each = page_table.shape[2]
    query_heads = queries.reshape(request_count, HEADS, HEAD_DIM)
    page_slots = page_table[:, 0, :]
    picked_keys = key_pool.reshape(pool_pages, page_rows, HEADS, HEAD_DIM)[page_slots]
    picked_values = value_pool.reshape(pool_pages, page_rows, HEADS, HEAD_DIM)[page_slots]
    scores = jnp.einsum(
        "rhd,rjphd->rhjp", query_heads, picked_keys, preferred_element_type=jnp.float32
    ) / math.sqrt(HEAD_DIM)
    page_number = jnp.arange(pages_each, dtype=jnp.int32) * holders + holder
    position = page_number[:, None] * page_rows + jnp.arange(page_rows, dtype=jnp.int32)[None, :]
    visible = position[None, None, :, :] < lengths[:, None, None, None]
    masked = jnp.where(visible, scores, floor_score)
    local_peak = jnp.max(masked, axis=(2, 3))
    weights = jnp.where(visible, jnp.exp(masked - local_peak[:, :, None, None]), 0.0)
    local_mass = jnp.sum(weights, axis=(2, 3))
    local_sum = jnp.einsum(
        "rhjp,rjphd->rhd",
        weights,
        picked_values.astype(jnp.float32),
        precision=lax.Precision.HIGHEST,
    )
    peak_rows, masses, gathered_sums = (
        lax.all_gather(local_peak[None], "kv", axis=0, tiled=True),
        lax.all_gather(local_mass[None], "kv", axis=0, tiled=True),
        lax.all_gather(local_sum[None], "kv", axis=0, tiled=True),
    )
    all_peak = jnp.max(peak_rows, axis=0)
    factors = jnp.exp(peak_rows - all_peak[None])
    all_mass = jnp.sum(masses * factors, axis=0)
    all_sum = jnp.sum(gathered_sums * factors[..., None], axis=0)
    decode_attn = (all_sum / all_mass[..., None]).reshape(request_count, D).astype(jnp.bfloat16)
    attn_rows = jnp.concatenate([prefill_attn, decode_attn], axis=0)
    hidden_state = residual.astype(jnp.float32) + jnp.dot(
        attn_rows, w_out, preferred_element_type=jnp.float32
    )
    scaled = (hidden_state * norm_gain).astype(jnp.bfloat16)
    square_sum, logit_parts = lax.psum(
        (
            jnp.sum(hidden_state * hidden_state, axis=1),
            jnp.dot(scaled, router, preferred_element_type=jnp.float32),
        ),
        "kv",
    )
    inv_first = lax.rsqrt(square_sum / D + epsilon)
    logits = logit_parts * inv_first[:, None]
    normed = (hidden_state * norm_gain * inv_first[:, None]).astype(jnp.bfloat16)
    row_count = residual.shape[0]
    expert_count = router.shape[1]
    capacity = min(row_count, 2 * row_count * TOP // expert_count)
    matches = routes[:, :, None] == jnp.arange(expert_count, dtype=jnp.int32)[None, None, :]
    chosen = jnp.sum(jnp.where(matches, logits[:, None, :], 0.0), axis=2)
    raised = jnp.exp(chosen)
    gate_weights = raised / jnp.sum(raised, axis=1, keepdims=True)
    one_hot = matches.reshape(row_count * TOP, expert_count).astype(jnp.int32)
    earlier = jnp.cumsum(one_hot, axis=0) - one_hot
    slot_index = jnp.sum(earlier * one_hot, axis=1)
    target = routes.reshape(-1) * capacity + slot_index
    source_row = jnp.arange(row_count * TOP, dtype=jnp.int32) // TOP
    filler = jnp.zeros((expert_count * capacity,), jnp.int32).at[target].set(source_row)
    present = jnp.zeros((expert_count * capacity,), jnp.bool_).at[target].set(True)
    gate_local = w_gate[0]
    up_local = w_up[0]
    down_local = w_down[0]
    full_rows = lax.all_gather(normed, "kv", axis=1, tiled=True)
    picked = full_rows[filler]
    arrived = lax.all_to_all(
        jnp.where(present[:, None], picked, jnp.zeros_like(picked)).reshape(
            expert_count, capacity, full_rows.shape[1]
        ),
        "ep",
        split_axis=0,
        concat_axis=0,
        tiled=True,
    )
    inbound = arrived.reshape(-1, arrived.shape[2])
    gate_proj = jnp.dot(inbound, gate_local, preferred_element_type=jnp.float32)
    up_proj = jnp.dot(inbound, up_local, preferred_element_type=jnp.float32)
    activation = (jax.nn.silu(gate_proj) * up_proj).astype(jnp.bfloat16)
    feature_cols = residual.shape[1]
    summed = lax.psum_scatter(
        lax.dot_general(
            down_local, activation, (((0,), (1,)), ((), ())), preferred_element_type=jnp.float32
        ).astype(jnp.bfloat16),
        "kv",
        scatter_dimension=0,
        tiled=True,
    ).astype(jnp.float32)
    expert_out = summed.T.astype(jnp.bfloat16).reshape(
        arrived.shape[0], arrived.shape[1], feature_cols
    )
    returned = lax.all_to_all(expert_out, "ep", split_axis=0, concat_axis=0, tiled=True)
    back_rows = (
        returned.reshape(-1, feature_cols)[target]
        .reshape(row_count, TOP, feature_cols)
        .astype(jnp.float32)
    )
    combined = hidden_state + jnp.sum(back_rows * gate_weights[:, :, None], axis=1)
    square_two = lax.psum(jnp.sum(combined * combined, axis=1), "kv")
    return (combined * lax.rsqrt(square_two / D + epsilon)[:, None] * final_gain).astype(
        jnp.bfloat16
    )


def attend(slots_ref, lengths_ref, q_ref, k_ref, v_ref, out_ref, kbuf, vbuf, ksem, vsem):
    requests, pages_each, page_rows = kbuf.shape[:3]
    holder = lax.axis_index("kv")
    holders = lax.axis_size("kv")
    for r in range(requests):
        for j in range(pages_each):
            pltpu.make_async_copy(k_ref.at[slots_ref[r, 0, j]], kbuf.at[r, j], ksem.at[r]).start()
    for r in range(requests):
        for j in range(pages_each):
            pltpu.make_async_copy(v_ref.at[slots_ref[r, 0, j]], vbuf.at[r, j], vsem.at[r]).start()
    tokens = pages_each * page_rows
    wide_row = lax.broadcasted_iota(jnp.int32, (HEAD_DIM, D), 0)
    wide_head = lax.broadcasted_iota(jnp.int32, (HEAD_DIM, D), 1) // HEAD_DIM
    own_head = (wide_row == wide_head)[:HEADS]
    place = lax.broadcasted_iota(jnp.int32, (HEADS, tokens), 1)
    position = ((place // page_rows) * holders + holder) * page_rows + place % page_rows
    queries = q_ref[...].astype(jnp.float32)
    for r in range(requests):
        spread = jnp.where(wide_row == wide_head, queries[r : r + 1, :], 0.0).astype(jnp.bfloat16)
        pltpu.make_async_copy(kbuf.at[r], kbuf.at[r], ksem.at[r]).wait()
        scores = lax.dot_general(
            kbuf[r].reshape(tokens, D),
            spread,
            (((1,), (1,)), ((), ())),
            preferred_element_type=jnp.float32,
        )
        visible = position < lengths_ref[r]
        scores = jnp.where(visible, scores.T[:HEADS] / math.sqrt(HEAD_DIM), floor_score)
        peak = scores.max(axis=1, keepdims=True)
        weight = jnp.where(visible, jnp.exp(scores - peak), 0.0)
        mass = weight.sum(axis=1, keepdims=True)
        high = weight.astype(jnp.bfloat16)
        low = (weight - high.astype(jnp.float32)).astype(jnp.bfloat16)
        pltpu.make_async_copy(vbuf.at[r], vbuf.at[r], vsem.at[r]).wait()
        total = jnp.dot(
            jnp.concatenate([high, low], axis=0),
            vbuf[r].reshape(tokens, D),
            preferred_element_type=jnp.float32,
        )
        both = total[:HEADS] + total[HEADS:]
        for n, part in enumerate((both, peak, mass)):
            row = n * requests + r
            out_ref[row : row + 1, :] = jnp.sum(
                jnp.where(own_head, part, 0.0), axis=0, keepdims=True
            )


def local_attention(queries, key_pool, value_pool, page_table, lengths):
    requests, _, pages_each = page_table.shape
    held = (requests, pages_each) + key_pool.shape[1:]
    smem = pl.BlockSpec(memory_space=pltpu.SMEM)
    vmem = pl.BlockSpec(memory_space=pltpu.VMEM)
    hbm = pl.BlockSpec(memory_space=pl.ANY)
    return pl.pallas_call(
        attend,
        out_shape=jax.ShapeDtypeStruct((3 * requests, D), jnp.float32),
        in_specs=[smem, smem, vmem, hbm, hbm],
        out_specs=vmem,
        scratch_shapes=[
            pltpu.VMEM(held, jnp.bfloat16),
            pltpu.VMEM(held, jnp.bfloat16),
            pltpu.SemaphoreType.DMA((requests,)),
            pltpu.SemaphoreType.DMA((requests,)),
        ],
        compiler_params=pltpu.CompilerParams(vmem_limit_bytes=60 * 2**20),
        cost_estimate=pl.CostEstimate(flops=4 * 10**8, bytes_accessed=7 * 2**20, transcendentals=0),
        name="local_attention",
    )(page_table, lengths, queries, key_pool, value_pool)


LABELS = ((0, 0), (0, 1), (1, 0), (1, 1))


def where_held(a, b, path):
    if a == b:
        return a, a
    if a == 1:
        return path, 1 - path
    return 1 - path, path


def expert_kernel(by_slot, side_ref, gate_ref, up_ref, down_ref, *rest):
    blocks = rest[:4]
    outs = rest[4:8]
    xbuf, obuf, gbuf, ubuf, dbuf, wsem, xsem, osem = rest[8:]
    holder, core = lax.axis_index("kv"), lax.axis_index("ep") % 2
    pair = blocks[0].shape[1]
    cols = xbuf.shape[4]
    rows = 2 * pair * xbuf.shape[3]
    halves = (holder, 1 - holder)
    paths = (core, 1 - core)

    def fetch(d, labels):
        for a, b in labels:
            t, f = where_held(a, b, paths[d])
            pltpu.make_async_copy(
                blocks[2 * d + b].at[a], xbuf.at[d, f, pl.ds(t * pair, pair)], xsem.at[d, f]
            ).start()

    def load(source, buffer, kind, f):
        pltpu.make_async_copy(source.at[halves[f]], buffer.at[f], wsem.at[kind, f]).start()

    fetch(0, LABELS)
    load(gate_ref, gbuf, 0, 0)
    load(gate_ref, gbuf, 0, 1)
    load(up_ref, ubuf, 1, 0)
    load(up_ref, ubuf, 1, 1)
    for f in range(2):
        start = pl.multiple_of(halves[f] * cols, cols)
        pltpu.make_async_copy(
            down_ref.at[:, pl.ds(start, cols)], dbuf.at[f], wsem.at[2, f]
        ).start()
    fetch(1, LABELS)

    def ready(d, buffer, kind, f):
        if d == 0:
            pltpu.make_async_copy(buffer.at[f], buffer.at[f], wsem.at[kind, f]).wait()

    def came(d, f):
        pltpu.make_async_copy(xbuf.at[d, f], xbuf.at[d, f], xsem.at[d, f]).wait()

    side = side_ref[...].T
    for d in range(2):
        came(d, 0)
        first = xbuf[d, 0].reshape(rows, cols)
        ready(d, gbuf, 0, 0)
        gate = jnp.dot(first, gbuf[0], preferred_element_type=jnp.float32)
        came(d, 1)
        second = xbuf[d, 1].reshape(rows, cols)
        ready(d, gbuf, 0, 1)
        gate += jnp.dot(second, gbuf[1], preferred_element_type=jnp.float32)
        groups = [4 * i + 2 * t + d for t in range(2) for i in range(pair)]
        scale = jnp.concatenate([side[:, g : g + 1] for g in groups])
        share = jnp.concatenate([side[:, 4 * pair + g : 4 * pair + g + 1] for g in groups])
        gate *= scale
        ready(d, ubuf, 1, 0)
        up = jnp.dot(first, ubuf[0], preferred_element_type=jnp.float32)
        ready(d, ubuf, 1, 1)
        up += jnp.dot(second, ubuf[1], preferred_element_type=jnp.float32)
        up *= scale
        act = (gate / (1.0 + jnp.exp(-gate)) * up).astype(jnp.bfloat16)
        for f in range(2):
            ready(d, dbuf, 2, f)
            out = jnp.dot(act, dbuf[f], preferred_element_type=jnp.float32) * share
            obuf[d, f] = out.astype(jnp.bfloat16).reshape(2 * pair, -1, cols)
        for n, (a, b) in enumerate(LABELS):
            t, f = where_held(a, b, paths[d])
            out = outs[2 * d + b].at[:, a] if by_slot else outs[2 * d + b].at[a]
            pltpu.make_async_copy(
                obuf.at[d, f, pl.ds(t * pair, pair)], out, osem.at[4 * d + n]
            ).start()
    for n in range(8):
        pltpu.make_async_copy(
            obuf.at[0, 0, pl.ds(0, pair)], obuf.at[0, 0, pl.ds(0, pair)], osem.at[n]
        ).wait()


def run_experts(by_slot, side, gate, up, down, blocks):
    _, pair, row_count, cols = blocks[0].shape
    hidden = gate.shape[2]
    vmem = pl.BlockSpec(memory_space=pltpu.VMEM)
    hbm = pl.BlockSpec(memory_space=pl.ANY)
    shape = (pair, 2, row_count, cols) if by_slot else (2, pair, row_count, cols)

    def body(*refs):
        expert_kernel(by_slot, *refs)

    return pl.pallas_call(
        body,
        out_shape=[jax.ShapeDtypeStruct(shape, jnp.bfloat16)] * 4,
        in_specs=[vmem, hbm, hbm, hbm] + [hbm] * 4,
        out_specs=[hbm] * 4,
        scratch_shapes=[
            pltpu.VMEM((2, 2, 2 * pair, row_count, cols), jnp.bfloat16),
            pltpu.VMEM((2, 2, 2 * pair, row_count, cols), jnp.bfloat16),
            pltpu.VMEM((2, cols, hidden), jnp.bfloat16),
            pltpu.VMEM((2, cols, hidden), jnp.bfloat16),
            pltpu.VMEM((2, hidden, cols), jnp.bfloat16),
            pltpu.SemaphoreType.DMA((3, 2)),
            pltpu.SemaphoreType.DMA((2, 2)),
            pltpu.SemaphoreType.DMA((8,)),
        ],
        compiler_params=pltpu.CompilerParams(vmem_limit_bytes=44 * 2**20),
        cost_estimate=pl.CostEstimate(
            flops=4 * pair * row_count * 12 * cols * hidden,
            bytes_accessed=pair * row_count * cols * 32 + 12 * cols * hidden,
            transcendentals=0,
        ),
        name="experts",
    )(side, gate, up, down, *blocks)


def add(*parts):
    total = parts[0].astype(jnp.float32)
    for part in parts[1:]:
        total = total + part.astype(jnp.float32)
    return total.astype(jnp.bfloat16)


def dense(
    queries,
    key_pool,
    value_pool,
    page_table,
    lengths,
    prefill_attn,
    residual,
    w_out,
    norm_gain,
    router,
    w_gate,
    w_up,
    w_down,
    final_gain,
    routes,
):
    request_count = queries.shape[0]
    row_count, cols = residual.shape
    expert_count = router.shape[1]
    ep_size = lax.axis_size("ep")
    depth = ep_size // 4
    axes = ("ep", "kv")

    def number(z, y, c, x):
        return ((z * 2 + y) * 2 + c) * 2 + x

    places = [(z, y, c, x) for z in range(depth) for y in range(2) for c in range(2) for x in range(2)]

    def sent(array, target):
        return lax.ppermute(array, axes, [(number(*p), number(*target(*p))) for p in places])

    def across(array):
        return sent(array, lambda z, y, c, x: (z, y, c, 1 - x))

    def along(array, s):
        return sent(array, lambda z, y, c, x: ((z + s) % depth, y, c, x))

    def hop_one(array):
        return sent(array, lambda z, y, c, x: (z, y, c, 1 - x) if c == 0 else (z, 1 - y, c, x))

    def hop_two(array):
        return sent(array, lambda z, y, c, x: (z, 1 - y, c, x) if c == 0 else (z, y, c, 1 - x))

    def sibling(array):
        return sent(array, lambda z, y, c, x: (z, y, 1 - c, x))

    def fence(*values):
        return lax.optimization_barrier(values)

    early = (row_count - request_count) // 16 * 16

    def hidden_of(rows, part):
        product = jnp.dot(rows, w_out, preferred_element_type=jnp.float32)
        state = residual[part].astype(jnp.float32) + product
        return state, (state * norm_gain).astype(jnp.bfloat16)

    first_hidden, first_scaled = hidden_of(prefill_attn[:early], slice(0, early))
    first_one = along(first_scaled, 1)
    local = local_attention(queries, key_pool, value_pool, page_table, lengths)
    first_one, local, first_scaled = fence(first_one, local, first_scaled)

    first_two = along(first_one, 1)
    other = across(local)
    sum_one, sum_two = local[:request_count], other[:request_count]
    peak_one, peak_two = (v[request_count : 2 * request_count] for v in (local, other))
    mass_one, mass_two = (v[2 * request_count :] for v in (local, other))
    peak = jnp.maximum(peak_one, peak_two)
    factor_one, factor_two = jnp.exp(peak_one - peak), jnp.exp(peak_two - peak)
    decode_attn = (sum_one * factor_one + sum_two * factor_two) / (
        mass_one * factor_one + mass_two * factor_two
    )
    last_rows = jnp.concatenate([prefill_attn[early:], decode_attn.astype(jnp.bfloat16)], axis=0)
    last_hidden, last_scaled = hidden_of(last_rows, slice(early, row_count))
    first_two, last_scaled, last_hidden = fence(first_two, last_scaled, last_hidden)

    hidden_state = jnp.concatenate([first_hidden, last_hidden], axis=0)
    scaled = jnp.concatenate([first_scaled, last_scaled], axis=0)
    square_part = jnp.sum(hidden_state * hidden_state, axis=1)
    logit_part = jnp.dot(scaled, router, preferred_element_type=jnp.float32)
    stats = jnp.concatenate([logit_part, square_part[:, None]], axis=1).T

    slots = ((1, 2), (3, 0))
    last_one, last_two = along(last_scaled, 1), along(last_scaled, 2)
    stats = stats + across(stats)
    own_one = hop_one(scaled)
    last_one, last_two, stats, scaled, own_one = fence(last_one, last_two, stats, scaled, own_one)

    pair = jnp.stack(
        [
            jnp.concatenate([first_one, last_one], axis=0),
            jnp.concatenate([first_two, last_two], axis=0),
        ]
    )
    far_three, one = along(scaled, 3), hop_one(pair)
    inv_first = lax.rsqrt(stats[expert_count] / D + epsilon)
    logits = stats[:expert_count].T * inv_first[:, None]
    matches = routes[:, :, None] == jnp.arange(expert_count, dtype=jnp.int32)[None, None, :]
    chosen = jnp.sum(jnp.where(matches, logits[:, None, :], 0.0), axis=2)
    raised = jnp.exp(chosen)
    gate_weights = raised / jnp.sum(raised, axis=1, keepdims=True)
    by_expert = jnp.sum(jnp.where(matches, gate_weights[:, :, None], 0.0), axis=1)
    side = jnp.concatenate([by_expert, inv_first[:, None]], axis=1).T[None]
    side_s = sibling(side)
    side_y = sent(side, lambda z, y, c, x: (z, 1 - y, c, x))
    side_ys = sent(side, lambda z, y, c, x: (z, 1 - y, 1 - c, x))
    far_three, one, pair, scaled, side, side_s, side_y, side_ys = fence(
        far_three, one, pair, scaled, side, side_s, side_y, side_ys
    )

    own = lax.axis_index("ep")
    near = jnp.stack([pair, one])
    far, near_s, far_one = hop_two(near), sibling(near), hop_one(far_three)
    later_near = jnp.stack([jnp.stack([far_three, scaled]), jnp.stack([far_one, own_one])])
    side = jnp.concatenate([side, side_s, side_y, side_ys], axis=0)
    crossed = sent(side, lambda z, y, c, x: (z ^ 1, y, c, x))
    swapped = sent(jnp.stack([side, crossed]), lambda z, y, c, x: (z ^ 2, y, c, x))
    far, near_s, later_near, side, crossed, swapped = fence(
        far, near_s, later_near, side, crossed, swapped
    )

    odd = (own // 4) % 2 == 1
    before, after = jnp.where(odd, crossed, swapped[1]), jnp.where(odd, swapped[1], crossed)
    held = jnp.stack([side, before, swapped[0], after])
    share = lax.dynamic_index_in_dim(held, own, axis=2, keepdims=False)
    held = jnp.stack([held[:, :, expert_count], share]).reshape(2, depth, 2, 2, row_count)
    both = [jnp.stack([held[:, s] for s in chunk], axis=1).reshape(-1, row_count) for chunk in slots]
    gate_local = w_gate[0].reshape(2, cols, -1)
    up_local = w_up[0].reshape(2, cols, -1)
    down_local = w_down[0]
    far_s, later_far, later_near_s = sibling(far), hop_two(later_near), sibling(later_near)
    made = run_experts(False, both[0], gate_local, up_local, down_local, (near, far, near_s, far_s))
    later_far, later_near_s, later_near, made = fence(later_far, later_near_s, later_near, made)

    crossing = sibling(made[3])
    crossing = [add(made[1][a], crossing[a]) for a in range(2)]
    later_far_s = sibling(later_far)
    crossing, later_far_s = fence(crossing, later_far_s)

    staying_s = sibling(made[2])
    far_arrived, near_arrived = hop_two(crossing[1]), hop_two(crossing[0])
    blocks = (later_near, later_far, later_near_s, later_far_s)
    remade = run_experts(True, both[1], gate_local, up_local, down_local, blocks)
    staying, staying_s, far_arrived, remade = fence(made[0], staying_s, far_arrived, remade)

    far_sum = add(staying[1], staying_s[1], far_arrived)
    moved = hop_one(far_sum)
    far_sum, near_parts = fence(far_sum, (staying[0], staying_s[0]))
    near_sum = add(*near_parts, near_arrived)
    crossing_s, staying_s = sibling(remade[3]), sibling(remade[2])
    crossing = [add(remade[1][i], crossing_s[i]) for i in range(2)]
    staying = [[add(remade[0][i, a], staying_s[i, a]) for a in range(2)] for i in range(2)]
    moved, near_sum, crossing, staying = fence(moved, near_sum, crossing, staying)

    whole = add(near_sum, moved)
    relayed, three_parts = along(whole[1], depth - 1), hop_two(crossing[0])
    relayed, three_parts = fence(relayed, three_parts)
    passed = along(add(whole[0], relayed), depth - 1)
    moved, zero_parts = hop_one(add(staying[0][1], three_parts[1])), hop_two(crossing[1])
    part_three = along(add(staying[0][0], three_parts[0], moved), depth - 3)
    passed, zero_parts = fence(passed, zero_parts)
    combined = hidden_state + passed.astype(jnp.float32)
    moved = hop_one(add(staying[1][1], zero_parts[1]))
    for part in (staying[1][0], zero_parts[0], moved, part_three):
        combined = combined + part.astype(jnp.float32)
    square_two = jnp.sum(combined * combined, axis=1)[None, :]
    square_two = (square_two + across(square_two))[0]
    return (combined * lax.rsqrt(square_two / D + epsilon)[:, None] * final_gain).astype(
        jnp.bfloat16
    )


def per_device(*arrays):
    row_count, expert_count = arrays[6].shape[0], arrays[9].shape[1]
    capacity = min(row_count, 2 * row_count * TOP // expert_count)
    fits = lax.axis_size("kv") == 2 and lax.axis_size("ep") == 16
    if capacity == row_count and fits:
        return dense(*arrays)
    return routed(*arrays)


def solution(mesh):
    placed = (
        P("ep", None),
        P(("ep", "kv"), None, None),
        P(("ep", "kv"), None, None),
        P("ep", "kv", None),
        P("ep"),
        P("ep", None),
        P("ep", "kv"),
        P(None, "kv"),
        P("kv"),
        P("kv", None),
        P("ep", None, "kv"),
        P("ep", None, "kv"),
        P("ep", "kv", None),
        P("kv"),
        P("ep", None),
    )
    return jax.shard_map(
        per_device, mesh=mesh, in_specs=placed, out_specs=P("ep", "kv"), check_vma=False
    )
```

```python
import math

import jax
import jax.numpy as jnp
from jax import lax
from jax.experimental import pallas as pl
from jax.experimental.pallas import tpu as pltpu
from jax.sharding import PartitionSpec as P

D = 2048
HEADS = 16
HEAD_DIM = 128
TOP = 8


epsilon = 1e-06
floor_score = -1e30


def routed(
    queries,
    key_pool,
    value_pool,
    page_table,
    lengths,
    prefill_attn,
    residual,
    w_out,
    norm_gain,
    router,
    w_gate,
    w_up,
    w_down,
    final_gain,
    routes,
):
    holders = lax.axis_size("kv")
    holder = lax.axis_index("kv")
    request_count = queries.shape[0]
    pool_pages = key_pool.shape[0]
    page_rows = key_pool.shape[1]
    pages_each = page_table.shape[2]
    query_heads = queries.reshape(request_count, HEADS, HEAD_DIM)
    page_slots = page_table[:, 0, :]
    picked_keys = key_pool.reshape(pool_pages, page_rows, HEADS, HEAD_DIM)[page_slots]
    picked_values = value_pool.reshape(pool_pages, page_rows, HEADS, HEAD_DIM)[page_slots]
    scores = jnp.einsum(
        "rhd,rjphd->rhjp", query_heads, picked_keys, preferred_element_type=jnp.float32
    ) / math.sqrt(HEAD_DIM)
    page_number = jnp.arange(pages_each, dtype=jnp.int32) * holders + holder
    position = page_number[:, None] * page_rows + jnp.arange(page_rows, dtype=jnp.int32)[None, :]
    visible = position[None, None, :, :] < lengths[:, None, None, None]
    masked = jnp.where(visible, scores, floor_score)
    local_peak = jnp.max(masked, axis=(2, 3))
    weights = jnp.where(visible, jnp.exp(masked - local_peak[:, :, None, None]), 0.0)
    local_mass = jnp.sum(weights, axis=(2, 3))
    local_sum = jnp.einsum(
        "rhjp,rjphd->rhd",
        weights,
        picked_values.astype(jnp.float32),
        precision=lax.Precision.HIGHEST,
    )
    peak_rows, masses, gathered_sums = (
        lax.all_gather(local_peak[None], "kv", axis=0, tiled=True),
        lax.all_gather(local_mass[None], "kv", axis=0, tiled=True),
        lax.all_gather(local_sum[None], "kv", axis=0, tiled=True),
    )
    all_peak = jnp.max(peak_rows, axis=0)
    factors = jnp.exp(peak_rows - all_peak[None])
    all_mass = jnp.sum(masses * factors, axis=0)
    all_sum = jnp.sum(gathered_sums * factors[..., None], axis=0)
    decode_attn = (all_sum / all_mass[..., None]).reshape(request_count, D).astype(jnp.bfloat16)
    attn_rows = jnp.concatenate([prefill_attn, decode_attn], axis=0)
    hidden_state = residual.astype(jnp.float32) + jnp.dot(
        attn_rows, w_out, preferred_element_type=jnp.float32
    )
    scaled = (hidden_state * norm_gain).astype(jnp.bfloat16)
    square_sum, logit_parts = lax.psum(
        (
            jnp.sum(hidden_state * hidden_state, axis=1),
            jnp.dot(scaled, router, preferred_element_type=jnp.float32),
        ),
        "kv",
    )
    inv_first = lax.rsqrt(square_sum / D + epsilon)
    logits = logit_parts * inv_first[:, None]
    normed = (hidden_state * norm_gain * inv_first[:, None]).astype(jnp.bfloat16)
    row_count = residual.shape[0]
    expert_count = router.shape[1]
    capacity = min(row_count, 2 * row_count * TOP // expert_count)
    matches = routes[:, :, None] == jnp.arange(expert_count, dtype=jnp.int32)[None, None, :]
    chosen = jnp.sum(jnp.where(matches, logits[:, None, :], 0.0), axis=2)
    raised = jnp.exp(chosen)
    gate_weights = raised / jnp.sum(raised, axis=1, keepdims=True)
    one_hot = matches.reshape(row_count * TOP, expert_count).astype(jnp.int32)
    earlier = jnp.cumsum(one_hot, axis=0) - one_hot
    slot_index = jnp.sum(earlier * one_hot, axis=1)
    target = routes.reshape(-1) * capacity + slot_index
    source_row = jnp.arange(row_count * TOP, dtype=jnp.int32) // TOP
    filler = jnp.zeros((expert_count * capacity,), jnp.int32).at[target].set(source_row)
    present = jnp.zeros((expert_count * capacity,), jnp.bool_).at[target].set(True)
    gate_local = w_gate[0]
    up_local = w_up[0]
    down_local = w_down[0]
    full_rows = lax.all_gather(normed, "kv", axis=1, tiled=True)
    picked = full_rows[filler]
    arrived = lax.all_to_all(
        jnp.where(present[:, None], picked, jnp.zeros_like(picked)).reshape(
            expert_count, capacity, full_rows.shape[1]
        ),
        "ep",
        split_axis=0,
        concat_axis=0,
        tiled=True,
    )
    inbound = arrived.reshape(-1, arrived.shape[2])
    gate_proj = jnp.dot(inbound, gate_local, preferred_element_type=jnp.float32)
    up_proj = jnp.dot(inbound, up_local, preferred_element_type=jnp.float32)
    activation = (jax.nn.silu(gate_proj) * up_proj).astype(jnp.bfloat16)
    feature_cols = residual.shape[1]
    summed = lax.psum_scatter(
        lax.dot_general(
            down_local, activation, (((0,), (1,)), ((), ())), preferred_element_type=jnp.float32
        ).astype(jnp.bfloat16),
        "kv",
        scatter_dimension=0,
        tiled=True,
    ).astype(jnp.float32)
    expert_out = summed.T.astype(jnp.bfloat16).reshape(
        arrived.shape[0], arrived.shape[1], feature_cols
    )
    returned = lax.all_to_all(expert_out, "ep", split_axis=0, concat_axis=0, tiled=True)
    back_rows = (
        returned.reshape(-1, feature_cols)[target]
        .reshape(row_count, TOP, feature_cols)
        .astype(jnp.float32)
    )
    combined = hidden_state + jnp.sum(back_rows * gate_weights[:, :, None], axis=1)
    square_two = lax.psum(jnp.sum(combined * combined, axis=1), "kv")
    return (combined * lax.rsqrt(square_two / D + epsilon)[:, None] * final_gain).astype(
        jnp.bfloat16
    )


def attend(slots_ref, lengths_ref, q_ref, k_ref, v_ref, out_ref, kbuf, vbuf, ksem, vsem):
    requests, pages_each, page_rows = kbuf.shape[:3]
    holder = lax.axis_index("kv")
    holders = lax.axis_size("kv")
    for r in range(requests):
        for j in range(pages_each):
            pltpu.make_async_copy(k_ref.at[slots_ref[r, 0, j]], kbuf.at[r, j], ksem.at[r]).start()
    for r in range(requests):
        for j in range(pages_each):
            pltpu.make_async_copy(v_ref.at[slots_ref[r, 0, j]], vbuf.at[r, j], vsem.at[r]).start()
    tokens = pages_each * page_rows
    wide_row = lax.broadcasted_iota(jnp.int32, (HEAD_DIM, D), 0)
    wide_head = lax.broadcasted_iota(jnp.int32, (HEAD_DIM, D), 1) // HEAD_DIM
    own_head = (wide_row == wide_head)[:HEADS]
    place = lax.broadcasted_iota(jnp.int32, (HEADS, tokens), 1)
    position = ((place // page_rows) * holders + holder) * page_rows + place % page_rows
    queries = q_ref[...].astype(jnp.float32)
    for r in range(requests):
        spread = jnp.where(wide_row == wide_head, queries[r : r + 1, :], 0.0).astype(jnp.bfloat16)
        pltpu.make_async_copy(kbuf.at[r], kbuf.at[r], ksem.at[r]).wait()
        scores = lax.dot_general(
            kbuf[r].reshape(tokens, D),
            spread,
            (((1,), (1,)), ((), ())),
            preferred_element_type=jnp.float32,
        )
        visible = position < lengths_ref[r]
        scores = jnp.where(visible, scores.T[:HEADS] / math.sqrt(HEAD_DIM), floor_score)
        peak = scores.max(axis=1, keepdims=True)
        weight = jnp.where(visible, jnp.exp(scores - peak), 0.0)
        mass = weight.sum(axis=1, keepdims=True)
        high = weight.astype(jnp.bfloat16)
        low = (weight - high.astype(jnp.float32)).astype(jnp.bfloat16)
        pltpu.make_async_copy(vbuf.at[r], vbuf.at[r], vsem.at[r]).wait()
        total = jnp.dot(
            jnp.concatenate([high, low], axis=0),
            vbuf[r].reshape(tokens, D),
            preferred_element_type=jnp.float32,
        )
        both = total[:HEADS] + total[HEADS:]
        for n, part in enumerate((both, peak, mass)):
            row = n * requests + r
            out_ref[row : row + 1, :] = jnp.sum(
                jnp.where(own_head, part, 0.0), axis=0, keepdims=True
            )


def local_attention(queries, key_pool, value_pool, page_table, lengths):
    requests, _, pages_each = page_table.shape
    held = (requests, pages_each) + key_pool.shape[1:]
    smem = pl.BlockSpec(memory_space=pltpu.SMEM)
    vmem = pl.BlockSpec(memory_space=pltpu.VMEM)
    hbm = pl.BlockSpec(memory_space=pl.ANY)
    return pl.pallas_call(
        attend,
        out_shape=jax.ShapeDtypeStruct((3 * requests, D), jnp.float32),
        in_specs=[smem, smem, vmem, hbm, hbm],
        out_specs=vmem,
        scratch_shapes=[
            pltpu.VMEM(held, jnp.bfloat16),
            pltpu.VMEM(held, jnp.bfloat16),
            pltpu.SemaphoreType.DMA((requests,)),
            pltpu.SemaphoreType.DMA((requests,)),
        ],
        compiler_params=pltpu.CompilerParams(vmem_limit_bytes=60 * 2**20),
        cost_estimate=pl.CostEstimate(flops=4 * 10**8, bytes_accessed=7 * 2**20, transcendentals=0),
        name="local_attention",
    )(page_table, lengths, queries, key_pool, value_pool)


LABELS = ((0, 0), (0, 1), (1, 0), (1, 1))


def where_held(a, b, path):
    if a == b:
        return a, a
    if a == 1:
        return path, 1 - path
    return 1 - path, path


def expert_kernel(by_slot, side_ref, gate_ref, up_ref, down_ref, *rest):
    blocks = rest[:4]
    outs = rest[4:8]
    xbuf, obuf, gbuf, ubuf, dbuf, wsem, xsem, osem = rest[8:]
    holder, core = lax.axis_index("kv"), lax.axis_index("ep") % 2
    pair = blocks[0].shape[1]
    cols = xbuf.shape[4]
    rows = 2 * pair * xbuf.shape[3]
    halves = (holder, 1 - holder)
    paths = (core, 1 - core)

    def fetch(d, labels):
        for a, b in labels:
            t, f = where_held(a, b, paths[d])
            pltpu.make_async_copy(
                blocks[2 * d + b].at[a], xbuf.at[d, f, pl.ds(t * pair, pair)], xsem.at[d, f]
            ).start()

    def load(source, buffer, kind, f):
        pltpu.make_async_copy(source.at[halves[f]], buffer.at[f], wsem.at[kind, f]).start()

    fetch(0, LABELS)
    load(gate_ref, gbuf, 0, 0)
    load(gate_ref, gbuf, 0, 1)
    load(up_ref, ubuf, 1, 0)
    load(up_ref, ubuf, 1, 1)
    for f in range(2):
        start = pl.multiple_of(halves[f] * cols, cols)
        pltpu.make_async_copy(
            down_ref.at[:, pl.ds(start, cols)], dbuf.at[f], wsem.at[2, f]
        ).start()
    fetch(1, LABELS)

    def ready(d, buffer, kind, f):
        if d == 0:
            pltpu.make_async_copy(buffer.at[f], buffer.at[f], wsem.at[kind, f]).wait()

    def came(d, f):
        pltpu.make_async_copy(xbuf.at[d, f], xbuf.at[d, f], xsem.at[d, f]).wait()

    side = side_ref[...].T
    for d in range(2):
        came(d, 0)
        first = xbuf[d, 0].reshape(rows, cols)
        ready(d, gbuf, 0, 0)
        gate = jnp.dot(first, gbuf[0], preferred_element_type=jnp.float32)
        came(d, 1)
        second = xbuf[d, 1].reshape(rows, cols)
        ready(d, gbuf, 0, 1)
        gate += jnp.dot(second, gbuf[1], preferred_element_type=jnp.float32)
        groups = [4 * i + 2 * t + d for t in range(2) for i in range(pair)]
        scale = jnp.concatenate([side[:, g : g + 1] for g in groups])
        share = jnp.concatenate([side[:, 4 * pair + g : 4 * pair + g + 1] for g in groups])
        gate *= scale
        ready(d, ubuf, 1, 0)
        up = jnp.dot(first, ubuf[0], preferred_element_type=jnp.float32)
        ready(d, ubuf, 1, 1)
        up += jnp.dot(second, ubuf[1], preferred_element_type=jnp.float32)
        up *= scale
        act = (gate / (1.0 + jnp.exp(-gate)) * up).astype(jnp.bfloat16)
        for f in range(2):
            ready(d, dbuf, 2, f)
            out = jnp.dot(act, dbuf[f], preferred_element_type=jnp.float32) * share
            obuf[d, f] = out.astype(jnp.bfloat16).reshape(2 * pair, -1, cols)
        for n, (a, b) in enumerate(LABELS):
            t, f = where_held(a, b, paths[d])
            out = outs[2 * d + b].at[:, a] if by_slot else outs[2 * d + b].at[a]
            pltpu.make_async_copy(
                obuf.at[d, f, pl.ds(t * pair, pair)], out, osem.at[4 * d + n]
            ).start()
    for n in range(8):
        pltpu.make_async_copy(
            obuf.at[0, 0, pl.ds(0, pair)], obuf.at[0, 0, pl.ds(0, pair)], osem.at[n]
        ).wait()


def run_experts(by_slot, side, gate, up, down, blocks):
    _, pair, row_count, cols = blocks[0].shape
    hidden = gate.shape[2]
    vmem = pl.BlockSpec(memory_space=pltpu.VMEM)
    hbm = pl.BlockSpec(memory_space=pl.ANY)
    shape = (pair, 2, row_count, cols) if by_slot else (2, pair, row_count, cols)

    def body(*refs):
        expert_kernel(by_slot, *refs)

    return pl.pallas_call(
        body,
        out_shape=[jax.ShapeDtypeStruct(shape, jnp.bfloat16)] * 4,
        in_specs=[vmem, hbm, hbm, hbm] + [hbm] * 4,
        out_specs=[hbm] * 4,
        scratch_shapes=[
            pltpu.VMEM((2, 2, 2 * pair, row_count, cols), jnp.bfloat16),
            pltpu.VMEM((2, 2, 2 * pair, row_count, cols), jnp.bfloat16),
            pltpu.VMEM((2, cols, hidden), jnp.bfloat16),
            pltpu.VMEM((2, cols, hidden), jnp.bfloat16),
            pltpu.VMEM((2, hidden, cols), jnp.bfloat16),
            pltpu.SemaphoreType.DMA((3, 2)),
            pltpu.SemaphoreType.DMA((2, 2)),
            pltpu.SemaphoreType.DMA((8,)),
        ],
        compiler_params=pltpu.CompilerParams(vmem_limit_bytes=44 * 2**20),
        cost_estimate=pl.CostEstimate(
            flops=4 * pair * row_count * 12 * cols * hidden,
            bytes_accessed=pair * row_count * cols * 32 + 12 * cols * hidden,
            transcendentals=0,
        ),
        name="experts",
    )(side, gate, up, down, *blocks)


def add(*parts):
    total = parts[0].astype(jnp.float32)
    for part in parts[1:]:
        total = total + part.astype(jnp.float32)
    return total.astype(jnp.bfloat16)


def dense(
    queries,
    key_pool,
    value_pool,
    page_table,
    lengths,
    prefill_attn,
    residual,
    w_out,
    norm_gain,
    router,
    w_gate,
    w_up,
    w_down,
    final_gain,
    routes,
):
    request_count = queries.shape[0]
    row_count, cols = residual.shape
    expert_count = router.shape[1]
    ep_size = lax.axis_size("ep")
    depth = ep_size // 4
    axes = ("ep", "kv")

    def number(z, y, c, x):
        return ((z * 2 + y) * 2 + c) * 2 + x

    places = [(z, y, c, x) for z in range(depth) for y in range(2) for c in range(2) for x in range(2)]

    def sent(array, target):
        return lax.ppermute(array, axes, [(number(*p), number(*target(*p))) for p in places])

    def across(array):
        return sent(array, lambda z, y, c, x: (z, y, c, 1 - x))

    def along(array, s):
        return sent(array, lambda z, y, c, x: ((z + s) % depth, y, c, x))

    def hop_one(array):
        return sent(array, lambda z, y, c, x: (z, y, c, 1 - x) if c == 0 else (z, 1 - y, c, x))

    def hop_two(array):
        return sent(array, lambda z, y, c, x: (z, 1 - y, c, x) if c == 0 else (z, y, c, 1 - x))

    def sibling(array):
        return sent(array, lambda z, y, c, x: (z, y, 1 - c, x))

    def fence(*values):
        return lax.optimization_barrier(values)

    early = (row_count - request_count) // 16 * 16

    def hidden_of(rows, part):
        product = jnp.dot(rows, w_out, preferred_element_type=jnp.float32)
        state = residual[part].astype(jnp.float32) + product
        return state, (state * norm_gain).astype(jnp.bfloat16)

    first_hidden, first_scaled = hidden_of(prefill_attn[:early], slice(0, early))
    first_one = along(first_scaled, 1)
    local = local_attention(queries, key_pool, value_pool, page_table, lengths)
    first_one, local, first_scaled = fence(first_one, local, first_scaled)

    first_two = along(first_one, 1)
    other = across(local)
    sum_one, sum_two = local[:request_count], other[:request_count]
    peak_one, peak_two = (v[request_count : 2 * request_count] for v in (local, other))
    mass_one, mass_two = (v[2 * request_count :] for v in (local, other))
    peak = jnp.maximum(peak_one, peak_two)
    factor_one, factor_two = jnp.exp(peak_one - peak), jnp.exp(peak_two - peak)
    decode_attn = (sum_one * factor_one + sum_two * factor_two) / (
        mass_one * factor_one + mass_two * factor_two
    )
    last_rows = jnp.concatenate([prefill_attn[early:], decode_attn.astype(jnp.bfloat16)], axis=0)
    last_hidden, last_scaled = hidden_of(last_rows, slice(early, row_count))
    first_two, last_scaled, last_hidden = fence(first_two, last_scaled, last_hidden)

    hidden_state = jnp.concatenate([first_hidden, last_hidden], axis=0)
    scaled = jnp.concatenate([first_scaled, last_scaled], axis=0)
    square_part = jnp.sum(hidden_state * hidden_state, axis=1)
    logit_part = jnp.dot(scaled, router, preferred_element_type=jnp.float32)
    stats = jnp.concatenate([logit_part, square_part[:, None]], axis=1).T

    slots = ((1, 2), (3, 0))
    last_one, last_two = along(last_scaled, 1), along(last_scaled, 2)
    stats = stats + across(stats)
    own_one = hop_one(scaled)
    last_one, last_two, stats, scaled, own_one = fence(last_one, last_two, stats, scaled, own_one)

    pair = jnp.stack(
        [
            jnp.concatenate([first_one, last_one], axis=0),
            jnp.concatenate([first_two, last_two], axis=0),
        ]
    )
    far_three, one = along(scaled, 3), hop_one(pair)
    inv_first = lax.rsqrt(stats[expert_count] / D + epsilon)
    logits = stats[:expert_count].T * inv_first[:, None]
    matches = routes[:, :, None] == jnp.arange(expert_count, dtype=jnp.int32)[None, None, :]
    chosen = jnp.sum(jnp.where(matches, logits[:, None, :], 0.0), axis=2)
    raised = jnp.exp(chosen)
    gate_weights = raised / jnp.sum(raised, axis=1, keepdims=True)
    by_expert = jnp.sum(jnp.where(matches, gate_weights[:, :, None], 0.0), axis=1)
    side = jnp.concatenate([by_expert, inv_first[:, None]], axis=1).T[None]
    side_s = sibling(side)
    side_y = sent(side, lambda z, y, c, x: (z, 1 - y, c, x))
    side_ys = sent(side, lambda z, y, c, x: (z, 1 - y, 1 - c, x))
    far_three, one, pair, scaled, side, side_s, side_y, side_ys = fence(
        far_three, one, pair, scaled, side, side_s, side_y, side_ys
    )

    own = lax.axis_index("ep")
    near = jnp.stack([pair, one])
    far, near_s, far_one = hop_two(near), sibling(near), hop_one(far_three)
    later_near = jnp.stack([jnp.stack([far_three, scaled]), jnp.stack([far_one, own_one])])
    side = jnp.concatenate([side, side_s, side_y, side_ys], axis=0)
    crossed = sent(side, lambda z, y, c, x: (z ^ 1, y, c, x))
    swapped = sent(jnp.stack([side, crossed]), lambda z, y, c, x: (z ^ 2, y, c, x))
    far, near_s, later_near, side, crossed, swapped = fence(
        far, near_s, later_near, side, crossed, swapped
    )

    odd = (own // 4) % 2 == 1
    before, after = jnp.where(odd, crossed, swapped[1]), jnp.where(odd, swapped[1], crossed)
    held = jnp.stack([side, before, swapped[0], after])
    share = lax.dynamic_index_in_dim(held, own, axis=2, keepdims=False)
    held = jnp.stack([held[:, :, expert_count], share]).reshape(2, depth, 2, 2, row_count)
    both = [jnp.stack([held[:, s] for s in chunk], axis=1).reshape(-1, row_count) for chunk in slots]
    gate_local = w_gate[0].reshape(2, cols, -1)
    up_local = w_up[0].reshape(2, cols, -1)
    down_local = w_down[0]
    far_s, later_far, later_near_s = sibling(far), hop_two(later_near), sibling(later_near)
    made = run_experts(False, both[0], gate_local, up_local, down_local, (near, far, near_s, far_s))
    later_far, later_near_s, later_near, made = fence(later_far, later_near_s, later_near, made)

    crossing = sibling(made[3])
    crossing = [add(made[1][a], crossing[a]) for a in range(2)]
    later_far_s = sibling(later_far)
    crossing, later_far_s = fence(crossing, later_far_s)

    staying_s = sibling(made[2])
    far_arrived, near_arrived = hop_two(crossing[1]), hop_two(crossing[0])
    blocks = (later_near, later_far, later_near_s, later_far_s)
    remade = run_experts(True, both[1], gate_local, up_local, down_local, blocks)
    staying, staying_s, far_arrived, remade = fence(made[0], staying_s, far_arrived, remade)

    far_sum = add(staying[1], staying_s[1], far_arrived)
    moved = hop_one(far_sum)
    far_sum, near_parts = fence(far_sum, (staying[0], staying_s[0]))
    near_sum = add(*near_parts, near_arrived)
    crossing_s, staying_s = sibling(remade[3]), sibling(remade[2])
    crossing = [add(remade[1][1], crossing_s[1])]
    crossing += [add(remade[1][0, a], crossing_s[0, a]) for a in range(2)]
    staying = [[add(remade[0][i, a], staying_s[i, a]) for a in range(2)] for i in range(2)]
    moved, near_sum, crossing, staying = fence(moved, near_sum, crossing, staying)

    whole = add(near_sum, moved)
    three_far, three_near = hop_two(crossing[2]), hop_two(crossing[1])
    relayed = along(whole[1], depth - 1)
    passed = along(add(whole[0], relayed), depth - 1)
    moved, zero_parts = hop_one(add(staying[0][1], three_far)), hop_two(crossing[0])
    part_three = along(add(staying[0][0], three_near, moved), depth - 3)
    passed, zero_parts = fence(passed, zero_parts)
    combined = hidden_state + passed.astype(jnp.float32)
    moved = hop_one(add(staying[1][1], zero_parts[1]))
    for part in (staying[1][0], zero_parts[0], moved, part_three):
        combined = combined + part.astype(jnp.float32)
    square_two = jnp.sum(combined * combined, axis=1)[None, :]
    square_two = (square_two + across(square_two))[0]
    return (combined * lax.rsqrt(square_two / D + epsilon)[:, None] * final_gain).astype(
        jnp.bfloat16
    )


def per_device(*arrays):
    row_count, expert_count = arrays[6].shape[0], arrays[9].shape[1]
    capacity = min(row_count, 2 * row_count * TOP // expert_count)
    fits = lax.axis_size("kv") == 2 and lax.axis_size("ep") == 16
    if capacity == row_count and fits:
        return dense(*arrays)
    return routed(*arrays)


def solution(mesh):
    placed = (
        P("ep", None),
        P(("ep", "kv"), None, None),
        P(("ep", "kv"), None, None),
        P("ep", "kv", None),
        P("ep"),
        P("ep", None),
        P("ep", "kv"),
        P(None, "kv"),
        P("kv"),
        P("kv", None),
        P("ep", None, "kv"),
        P("ep", None, "kv"),
        P("ep", "kv", None),
        P("kv"),
        P("ep", None),
    )
    return jax.shard_map(
        per_device, mesh=mesh, in_specs=placed, out_specs=P("ep", "kv"), check_vma=False
    )
```

```python
import math

import jax
import jax.numpy as jnp
from jax import lax
from jax.experimental import pallas as pl
from jax.experimental.pallas import tpu as pltpu
from jax.sharding import PartitionSpec as P

D = 2048
HEADS = 16
HEAD_DIM = 128
TOP = 8


epsilon = 1e-06
floor_score = -1e30


def routed(
    queries,
    key_pool,
    value_pool,
    page_table,
    lengths,
    prefill_attn,
    residual,
    w_out,
    norm_gain,
    router,
    w_gate,
    w_up,
    w_down,
    final_gain,
    routes,
):
    holders = lax.axis_size("kv")
    holder = lax.axis_index("kv")
    request_count = queries.shape[0]
    pool_pages = key_pool.shape[0]
    page_rows = key_pool.shape[1]
    pages_each = page_table.shape[2]
    query_heads = queries.reshape(request_count, HEADS, HEAD_DIM)
    page_slots = page_table[:, 0, :]
    picked_keys = key_pool.reshape(pool_pages, page_rows, HEADS, HEAD_DIM)[page_slots]
    picked_values = value_pool.reshape(pool_pages, page_rows, HEADS, HEAD_DIM)[page_slots]
    scores = jnp.einsum(
        "rhd,rjphd->rhjp", query_heads, picked_keys, preferred_element_type=jnp.float32
    ) / math.sqrt(HEAD_DIM)
    page_number = jnp.arange(pages_each, dtype=jnp.int32) * holders + holder
    position = page_number[:, None] * page_rows + jnp.arange(page_rows, dtype=jnp.int32)[None, :]
    visible = position[None, None, :, :] < lengths[:, None, None, None]
    masked = jnp.where(visible, scores, floor_score)
    local_peak = jnp.max(masked, axis=(2, 3))
    weights = jnp.where(visible, jnp.exp(masked - local_peak[:, :, None, None]), 0.0)
    local_mass = jnp.sum(weights, axis=(2, 3))
    local_sum = jnp.einsum(
        "rhjp,rjphd->rhd",
        weights,
        picked_values.astype(jnp.float32),
        precision=lax.Precision.HIGHEST,
    )
    peak_rows, masses, gathered_sums = (
        lax.all_gather(local_peak[None], "kv", axis=0, tiled=True),
        lax.all_gather(local_mass[None], "kv", axis=0, tiled=True),
        lax.all_gather(local_sum[None], "kv", axis=0, tiled=True),
    )
    all_peak = jnp.max(peak_rows, axis=0)
    factors = jnp.exp(peak_rows - all_peak[None])
    all_mass = jnp.sum(masses * factors, axis=0)
    all_sum = jnp.sum(gathered_sums * factors[..., None], axis=0)
    decode_attn = (all_sum / all_mass[..., None]).reshape(request_count, D).astype(jnp.bfloat16)
    attn_rows = jnp.concatenate([prefill_attn, decode_attn], axis=0)
    hidden_state = residual.astype(jnp.float32) + jnp.dot(
        attn_rows, w_out, preferred_element_type=jnp.float32
    )
    scaled = (hidden_state * norm_gain).astype(jnp.bfloat16)
    square_sum, logit_parts = lax.psum(
        (
            jnp.sum(hidden_state * hidden_state, axis=1),
            jnp.dot(scaled, router, preferred_element_type=jnp.float32),
        ),
        "kv",
    )
    inv_first = lax.rsqrt(square_sum / D + epsilon)
    logits = logit_parts * inv_first[:, None]
    normed = (hidden_state * norm_gain * inv_first[:, None]).astype(jnp.bfloat16)
    row_count = residual.shape[0]
    expert_count = router.shape[1]
    capacity = min(row_count, 2 * row_count * TOP // expert_count)
    matches = routes[:, :, None] == jnp.arange(expert_count, dtype=jnp.int32)[None, None, :]
    chosen = jnp.sum(jnp.where(matches, logits[:, None, :], 0.0), axis=2)
    raised = jnp.exp(chosen)
    gate_weights = raised / jnp.sum(raised, axis=1, keepdims=True)
    one_hot = matches.reshape(row_count * TOP, expert_count).astype(jnp.int32)
    earlier = jnp.cumsum(one_hot, axis=0) - one_hot
    slot_index = jnp.sum(earlier * one_hot, axis=1)
    target = routes.reshape(-1) * capacity + slot_index
    source_row = jnp.arange(row_count * TOP, dtype=jnp.int32) // TOP
    filler = jnp.zeros((expert_count * capacity,), jnp.int32).at[target].set(source_row)
    present = jnp.zeros((expert_count * capacity,), jnp.bool_).at[target].set(True)
    gate_local = w_gate[0]
    up_local = w_up[0]
    down_local = w_down[0]
    full_rows = lax.all_gather(normed, "kv", axis=1, tiled=True)
    picked = full_rows[filler]
    arrived = lax.all_to_all(
        jnp.where(present[:, None], picked, jnp.zeros_like(picked)).reshape(
            expert_count, capacity, full_rows.shape[1]
        ),
        "ep",
        split_axis=0,
        concat_axis=0,
        tiled=True,
    )
    inbound = arrived.reshape(-1, arrived.shape[2])
    gate_proj = jnp.dot(inbound, gate_local, preferred_element_type=jnp.float32)
    up_proj = jnp.dot(inbound, up_local, preferred_element_type=jnp.float32)
    activation = (jax.nn.silu(gate_proj) * up_proj).astype(jnp.bfloat16)
    feature_cols = residual.shape[1]
    summed = lax.psum_scatter(
        lax.dot_general(
            down_local, activation, (((0,), (1,)), ((), ())), preferred_element_type=jnp.float32
        ).astype(jnp.bfloat16),
        "kv",
        scatter_dimension=0,
        tiled=True,
    ).astype(jnp.float32)
    expert_out = summed.T.astype(jnp.bfloat16).reshape(
        arrived.shape[0], arrived.shape[1], feature_cols
    )
    returned = lax.all_to_all(expert_out, "ep", split_axis=0, concat_axis=0, tiled=True)
    back_rows = (
        returned.reshape(-1, feature_cols)[target]
        .reshape(row_count, TOP, feature_cols)
        .astype(jnp.float32)
    )
    combined = hidden_state + jnp.sum(back_rows * gate_weights[:, :, None], axis=1)
    square_two = lax.psum(jnp.sum(combined * combined, axis=1), "kv")
    return (combined * lax.rsqrt(square_two / D + epsilon)[:, None] * final_gain).astype(
        jnp.bfloat16
    )


def attend(slots_ref, lengths_ref, q_ref, k_ref, v_ref, out_ref, kbuf, vbuf, ksem, vsem):
    requests, pages_each, page_rows = kbuf.shape[:3]
    holder = lax.axis_index("kv")
    holders = lax.axis_size("kv")
    for r in range(requests):
        for j in range(pages_each):
            pltpu.make_async_copy(k_ref.at[slots_ref[r, 0, j]], kbuf.at[r, j], ksem.at[r]).start()
    for r in range(requests):
        for j in range(pages_each):
            pltpu.make_async_copy(v_ref.at[slots_ref[r, 0, j]], vbuf.at[r, j], vsem.at[r]).start()
    tokens = pages_each * page_rows
    wide_row = lax.broadcasted_iota(jnp.int32, (HEAD_DIM, D), 0)
    wide_head = lax.broadcasted_iota(jnp.int32, (HEAD_DIM, D), 1) // HEAD_DIM
    own_head = (wide_row == wide_head)[:HEADS]
    place = lax.broadcasted_iota(jnp.int32, (HEADS, tokens), 1)
    position = ((place // page_rows) * holders + holder) * page_rows + place % page_rows
    queries = q_ref[...].astype(jnp.float32)
    for r in range(requests):
        spread = jnp.where(wide_row == wide_head, queries[r : r + 1, :], 0.0).astype(jnp.bfloat16)
        pltpu.make_async_copy(kbuf.at[r], kbuf.at[r], ksem.at[r]).wait()
        scores = lax.dot_general(
            kbuf[r].reshape(tokens, D),
            spread,
            (((1,), (1,)), ((), ())),
            preferred_element_type=jnp.float32,
        )
        visible = position < lengths_ref[r]
        scores = jnp.where(visible, scores.T[:HEADS] / math.sqrt(HEAD_DIM), floor_score)
        peak = scores.max(axis=1, keepdims=True)
        weight = jnp.where(visible, jnp.exp(scores - peak), 0.0)
        mass = weight.sum(axis=1, keepdims=True)
        high = weight.astype(jnp.bfloat16)
        low = (weight - high.astype(jnp.float32)).astype(jnp.bfloat16)
        pltpu.make_async_copy(vbuf.at[r], vbuf.at[r], vsem.at[r]).wait()
        total = jnp.dot(
            jnp.concatenate([high, low], axis=0),
            vbuf[r].reshape(tokens, D),
            preferred_element_type=jnp.float32,
        )
        both = total[:HEADS] + total[HEADS:]
        for n, part in enumerate((both, peak, mass)):
            row = n * requests + r
            out_ref[row : row + 1, :] = jnp.sum(
                jnp.where(own_head, part, 0.0), axis=0, keepdims=True
            )


def local_attention(queries, key_pool, value_pool, page_table, lengths):
    requests, _, pages_each = page_table.shape
    held = (requests, pages_each) + key_pool.shape[1:]
    smem = pl.BlockSpec(memory_space=pltpu.SMEM)
    vmem = pl.BlockSpec(memory_space=pltpu.VMEM)
    hbm = pl.BlockSpec(memory_space=pl.ANY)
    return pl.pallas_call(
        attend,
        out_shape=jax.ShapeDtypeStruct((3 * requests, D), jnp.float32),
        in_specs=[smem, smem, vmem, hbm, hbm],
        out_specs=vmem,
        scratch_shapes=[
            pltpu.VMEM(held, jnp.bfloat16),
            pltpu.VMEM(held, jnp.bfloat16),
            pltpu.SemaphoreType.DMA((requests,)),
            pltpu.SemaphoreType.DMA((requests,)),
        ],
        compiler_params=pltpu.CompilerParams(vmem_limit_bytes=60 * 2**20),
        cost_estimate=pl.CostEstimate(flops=4 * 10**8, bytes_accessed=7 * 2**20, transcendentals=0),
        name="local_attention",
    )(page_table, lengths, queries, key_pool, value_pool)


LABELS = ((0, 0), (0, 1), (1, 0), (1, 1))


def where_held(a, b, path):
    if a == b:
        return a, a
    if a == 1:
        return path, 1 - path
    return 1 - path, path


def expert_kernel(by_slot, side_ref, gate_ref, up_ref, down_ref, *rest):
    blocks = rest[:4]
    outs = rest[4:8]
    xbuf, obuf, gbuf, ubuf, dbuf, wsem, xsem, osem = rest[8:]
    holder, core = lax.axis_index("kv"), lax.axis_index("ep") % 2
    pair = blocks[0].shape[1]
    cols = xbuf.shape[4]
    rows = 2 * pair * xbuf.shape[3]
    halves = (holder, 1 - holder)
    paths = (core, 1 - core)

    def fetch(d, labels):
        for a, b in labels:
            t, f = where_held(a, b, paths[d])
            pltpu.make_async_copy(
                blocks[2 * d + b].at[a], xbuf.at[d, f, pl.ds(t * pair, pair)], xsem.at[d, f]
            ).start()

    def load(source, buffer, kind, f):
        pltpu.make_async_copy(source.at[halves[f]], buffer.at[f], wsem.at[kind, f]).start()

    fetch(0, LABELS)
    load(gate_ref, gbuf, 0, 0)
    load(gate_ref, gbuf, 0, 1)
    load(up_ref, ubuf, 1, 0)
    load(up_ref, ubuf, 1, 1)
    for f in range(2):
        start = pl.multiple_of(halves[f] * cols, cols)
        pltpu.make_async_copy(
            down_ref.at[:, pl.ds(start, cols)], dbuf.at[f], wsem.at[2, f]
        ).start()
    fetch(1, LABELS)

    def ready(d, buffer, kind, f):
        if d == 0:
            pltpu.make_async_copy(buffer.at[f], buffer.at[f], wsem.at[kind, f]).wait()

    def came(d, f):
        pltpu.make_async_copy(xbuf.at[d, f], xbuf.at[d, f], xsem.at[d, f]).wait()

    side = side_ref[...].T
    for d in range(2):
        came(d, 0)
        first = xbuf[d, 0].reshape(rows, cols)
        ready(d, gbuf, 0, 0)
        gate = jnp.dot(first, gbuf[0], preferred_element_type=jnp.float32)
        came(d, 1)
        second = xbuf[d, 1].reshape(rows, cols)
        ready(d, gbuf, 0, 1)
        gate += jnp.dot(second, gbuf[1], preferred_element_type=jnp.float32)
        groups = [4 * i + 2 * t + d for t in range(2) for i in range(pair)]
        scale = jnp.concatenate([side[:, g : g + 1] for g in groups])
        share = jnp.concatenate([side[:, 4 * pair + g : 4 * pair + g + 1] for g in groups])
        gate *= scale
        ready(d, ubuf, 1, 0)
        up = jnp.dot(first, ubuf[0], preferred_element_type=jnp.float32)
        ready(d, ubuf, 1, 1)
        up += jnp.dot(second, ubuf[1], preferred_element_type=jnp.float32)
        up *= scale
        act = (gate / (1.0 + jnp.exp(-gate)) * up).astype(jnp.bfloat16)
        for f in range(2):
            ready(d, dbuf, 2, f)
            out = jnp.dot(act, dbuf[f], preferred_element_type=jnp.float32) * share
            obuf[d, f] = out.astype(jnp.bfloat16).reshape(2 * pair, -1, cols)
        for n, (a, b) in enumerate(LABELS):
            t, f = where_held(a, b, paths[d])
            out = outs[2 * d + b].at[:, a] if by_slot else outs[2 * d + b].at[a]
            pltpu.make_async_copy(
                obuf.at[d, f, pl.ds(t * pair, pair)], out, osem.at[4 * d + n]
            ).start()
    for n in range(8):
        pltpu.make_async_copy(
            obuf.at[0, 0, pl.ds(0, pair)], obuf.at[0, 0, pl.ds(0, pair)], osem.at[n]
        ).wait()


def run_experts(by_slot, side, gate, up, down, blocks):
    _, pair, row_count, cols = blocks[0].shape
    hidden = gate.shape[2]
    vmem = pl.BlockSpec(memory_space=pltpu.VMEM)
    hbm = pl.BlockSpec(memory_space=pl.ANY)
    shape = (pair, 2, row_count, cols) if by_slot else (2, pair, row_count, cols)

    def body(*refs):
        expert_kernel(by_slot, *refs)

    return pl.pallas_call(
        body,
        out_shape=[jax.ShapeDtypeStruct(shape, jnp.bfloat16)] * 4,
        in_specs=[vmem, hbm, hbm, hbm] + [hbm] * 4,
        out_specs=[hbm] * 4,
        scratch_shapes=[
            pltpu.VMEM((2, 2, 2 * pair, row_count, cols), jnp.bfloat16),
            pltpu.VMEM((2, 2, 2 * pair, row_count, cols), jnp.bfloat16),
            pltpu.VMEM((2, cols, hidden), jnp.bfloat16),
            pltpu.VMEM((2, cols, hidden), jnp.bfloat16),
            pltpu.VMEM((2, hidden, cols), jnp.bfloat16),
            pltpu.SemaphoreType.DMA((3, 2)),
            pltpu.SemaphoreType.DMA((2, 2)),
            pltpu.SemaphoreType.DMA((8,)),
        ],
        compiler_params=pltpu.CompilerParams(vmem_limit_bytes=44 * 2**20),
        cost_estimate=pl.CostEstimate(
            flops=4 * pair * row_count * 12 * cols * hidden,
            bytes_accessed=pair * row_count * cols * 32 + 12 * cols * hidden,
            transcendentals=0,
        ),
        name="experts",
    )(side, gate, up, down, *blocks)


def add(*parts):
    total = parts[0].astype(jnp.float32)
    for part in parts[1:]:
        total = total + part.astype(jnp.float32)
    return total.astype(jnp.bfloat16)


def dense(
    queries,
    key_pool,
    value_pool,
    page_table,
    lengths,
    prefill_attn,
    residual,
    w_out,
    norm_gain,
    router,
    w_gate,
    w_up,
    w_down,
    final_gain,
    routes,
):
    request_count = queries.shape[0]
    row_count, cols = residual.shape
    expert_count = router.shape[1]
    ep_size = lax.axis_size("ep")
    depth = ep_size // 4
    axes = ("ep", "kv")

    def number(z, y, c, x):
        return ((z * 2 + y) * 2 + c) * 2 + x

    places = [(z, y, c, x) for z in range(depth) for y in range(2) for c in range(2) for x in range(2)]

    def sent(array, target):
        return lax.ppermute(array, axes, [(number(*p), number(*target(*p))) for p in places])

    def across(array):
        return sent(array, lambda z, y, c, x: (z, y, c, 1 - x))

    def along(array, s):
        return sent(array, lambda z, y, c, x: ((z + s) % depth, y, c, x))

    def hop_one(array):
        return sent(array, lambda z, y, c, x: (z, y, c, 1 - x) if c == 0 else (z, 1 - y, c, x))

    def hop_two(array):
        return sent(array, lambda z, y, c, x: (z, 1 - y, c, x) if c == 0 else (z, y, c, 1 - x))

    def sibling(array):
        return sent(array, lambda z, y, c, x: (z, y, 1 - c, x))

    def fence(*values):
        return lax.optimization_barrier(values)

    early = (row_count - request_count) // 16 * 16

    def hidden_of(rows, part):
        product = jnp.dot(rows, w_out, preferred_element_type=jnp.float32)
        state = residual[part].astype(jnp.float32) + product
        return state, (state * norm_gain).astype(jnp.bfloat16)

    first_hidden, first_scaled = hidden_of(prefill_attn[:early], slice(0, early))
    first_one = along(first_scaled, 1)
    local = local_attention(queries, key_pool, value_pool, page_table, lengths)
    first_one, local, first_scaled = fence(first_one, local, first_scaled)

    first_two = along(first_one, 1)
    other = across(local)
    sum_one, sum_two = local[:request_count], other[:request_count]
    peak_one, peak_two = (v[request_count : 2 * request_count] for v in (local, other))
    mass_one, mass_two = (v[2 * request_count :] for v in (local, other))
    peak = jnp.maximum(peak_one, peak_two)
    factor_one, factor_two = jnp.exp(peak_one - peak), jnp.exp(peak_two - peak)
    decode_attn = (sum_one * factor_one + sum_two * factor_two) / (
        mass_one * factor_one + mass_two * factor_two
    )
    last_rows = jnp.concatenate([prefill_attn[early:], decode_attn.astype(jnp.bfloat16)], axis=0)
    last_hidden, last_scaled = hidden_of(last_rows, slice(early, row_count))
    first_two, last_scaled, last_hidden = fence(first_two, last_scaled, last_hidden)

    hidden_state = jnp.concatenate([first_hidden, last_hidden], axis=0)
    scaled = jnp.concatenate([first_scaled, last_scaled], axis=0)
    square_part = jnp.sum(hidden_state * hidden_state, axis=1)
    logit_part = jnp.dot(scaled, router, preferred_element_type=jnp.float32)
    stats = jnp.concatenate([logit_part, square_part[:, None]], axis=1).T

    slots = ((1, 2), (3, 0))
    last_one, last_two = along(last_scaled, 1), along(last_scaled, 2)
    stats = stats + across(stats)
    own_one = hop_one(scaled)
    last_one, last_two, stats, scaled, own_one = fence(last_one, last_two, stats, scaled, own_one)

    pair = jnp.stack(
        [
            jnp.concatenate([first_one, last_one], axis=0),
            jnp.concatenate([first_two, last_two], axis=0),
        ]
    )
    far_three, one = along(scaled, 3), hop_one(pair)
    inv_first = lax.rsqrt(stats[expert_count] / D + epsilon)
    logits = stats[:expert_count].T * inv_first[:, None]
    matches = routes[:, :, None] == jnp.arange(expert_count, dtype=jnp.int32)[None, None, :]
    chosen = jnp.sum(jnp.where(matches, logits[:, None, :], 0.0), axis=2)
    raised = jnp.exp(chosen)
    gate_weights = raised / jnp.sum(raised, axis=1, keepdims=True)
    by_expert = jnp.sum(jnp.where(matches, gate_weights[:, :, None], 0.0), axis=1)
    side = jnp.concatenate([by_expert, inv_first[:, None]], axis=1).T[None]
    side_s = sibling(side)
    side_y = sent(side, lambda z, y, c, x: (z, 1 - y, c, x))
    side_ys = sent(side, lambda z, y, c, x: (z, 1 - y, 1 - c, x))
    far_three, one, pair, scaled, side, side_s, side_y, side_ys = fence(
        far_three, one, pair, scaled, side, side_s, side_y, side_ys
    )

    own = lax.axis_index("ep")
    near = jnp.stack([pair, one])
    far, near_s, far_one = hop_two(near), sibling(near), hop_one(far_three)
    later_near = jnp.stack([jnp.stack([far_three, scaled]), jnp.stack([far_one, own_one])])
    side = jnp.concatenate([side, side_s, side_y, side_ys], axis=0)
    crossed = sent(side, lambda z, y, c, x: (z ^ 1, y, c, x))
    swapped = sent(jnp.stack([side, crossed]), lambda z, y, c, x: (z ^ 2, y, c, x))
    far, near_s, later_near, side, crossed, swapped = fence(
        far, near_s, later_near, side, crossed, swapped
    )

    odd = (own // 4) % 2 == 1
    before, after = jnp.where(odd, crossed, swapped[1]), jnp.where(odd, swapped[1], crossed)
    held = jnp.stack([side, before, swapped[0], after])
    share = lax.dynamic_index_in_dim(held, own, axis=2, keepdims=False)
    held = jnp.stack([held[:, :, expert_count], share]).reshape(2, depth, 2, 2, row_count)
    both = [jnp.stack([held[:, s] for s in chunk], axis=1).reshape(-1, row_count) for chunk in slots]
    gate_local = w_gate[0].reshape(2, cols, -1)
    up_local = w_up[0].reshape(2, cols, -1)
    down_local = w_down[0]
    far_s, later_far, later_near_s = sibling(far), hop_two(later_near), sibling(later_near)
    made = run_experts(False, both[0], gate_local, up_local, down_local, (near, far, near_s, far_s))
    later_far, later_near_s, later_near, made = fence(later_far, later_near_s, later_near, made)

    crossing = sibling(made[3])
    crossing = [add(made[1][a], crossing[a]) for a in range(2)]
    later_far_s = sibling(later_far)

    staying_s = sibling(made[2])
    far_arrived, near_arrived = hop_two(crossing[1]), hop_two(crossing[0])
    blocks = (later_near, later_far, later_near_s, later_far_s)
    remade = run_experts(True, both[1], gate_local, up_local, down_local, blocks)
    staying, staying_s, far_arrived, remade = fence(made[0], staying_s, far_arrived, remade)

    far_sum = add(staying[1], staying_s[1], far_arrived)
    moved = hop_one(far_sum)
    far_sum, near_parts = fence(far_sum, (staying[0], staying_s[0]))
    near_sum = add(*near_parts, near_arrived)
    crossing_s, staying_s = sibling(remade[3]), sibling(remade[2])
    crossing = [add(remade[1][1], crossing_s[1])]
    crossing += [add(remade[1][0, a], crossing_s[0, a]) for a in range(2)]
    staying = [[add(remade[0][i, a], staying_s[i, a]) for a in range(2)] for i in range(2)]
    moved, near_sum, crossing, staying = fence(moved, near_sum, crossing, staying)

    whole = add(near_sum, moved)
    three_far, three_near = hop_two(crossing[2]), hop_two(crossing[1])
    relayed = along(whole[1], depth - 1)
    passed = along(add(whole[0], relayed), depth - 1)
    moved, zero_parts = hop_one(add(staying[0][1], three_far)), hop_two(crossing[0])
    part_three = along(add(staying[0][0], three_near, moved), depth - 3)
    passed, zero_parts = fence(passed, zero_parts)
    combined = hidden_state + passed.astype(jnp.float32)
    moved = hop_one(add(staying[1][1], zero_parts[1]))
    for part in (staying[1][0], zero_parts[0], moved, part_three):
        combined = combined + part.astype(jnp.float32)
    square_two = jnp.sum(combined * combined, axis=1)[None, :]
    square_two = (square_two + across(square_two))[0]
    return (combined * lax.rsqrt(square_two / D + epsilon)[:, None] * final_gain).astype(
        jnp.bfloat16
    )


def per_device(*arrays):
    row_count, expert_count = arrays[6].shape[0], arrays[9].shape[1]
    capacity = min(row_count, 2 * row_count * TOP // expert_count)
    fits = lax.axis_size("kv") == 2 and lax.axis_size("ep") == 16
    if capacity == row_count and fits:
        return dense(*arrays)
    return routed(*arrays)


def solution(mesh):
    placed = (
        P("ep", None),
        P(("ep", "kv"), None, None),
        P(("ep", "kv"), None, None),
        P("ep", "kv", None),
        P("ep"),
        P("ep", None),
        P("ep", "kv"),
        P(None, "kv"),
        P("kv"),
        P("kv", None),
        P("ep", None, "kv"),
        P("ep", None, "kv"),
        P("ep", "kv", None),
        P("kv"),
        P("ep", None),
    )
    return jax.shard_map(
        per_device, mesh=mesh, in_specs=placed, out_specs=P("ep", "kv"), check_vma=False
    )
```

```python
import math

import jax
import jax.numpy as jnp
from jax import lax
from jax.experimental import pallas as pl
from jax.experimental.pallas import tpu as pltpu
from jax.sharding import PartitionSpec as P

D = 2048
HEADS = 16
HEAD_DIM = 128
TOP = 8


epsilon = 1e-06
floor_score = -1e30


def routed(
    queries,
    key_pool,
    value_pool,
    page_table,
    lengths,
    prefill_attn,
    residual,
    w_out,
    norm_gain,
    router,
    w_gate,
    w_up,
    w_down,
    final_gain,
    routes,
):
    holders = lax.axis_size("kv")
    holder = lax.axis_index("kv")
    request_count = queries.shape[0]
    pool_pages = key_pool.shape[0]
    page_rows = key_pool.shape[1]
    pages_each = page_table.shape[2]
    query_heads = queries.reshape(request_count, HEADS, HEAD_DIM)
    page_slots = page_table[:, 0, :]
    picked_keys = key_pool.reshape(pool_pages, page_rows, HEADS, HEAD_DIM)[page_slots]
    picked_values = value_pool.reshape(pool_pages, page_rows, HEADS, HEAD_DIM)[page_slots]
    scores = jnp.einsum(
        "rhd,rjphd->rhjp", query_heads, picked_keys, preferred_element_type=jnp.float32
    ) / math.sqrt(HEAD_DIM)
    page_number = jnp.arange(pages_each, dtype=jnp.int32) * holders + holder
    position = page_number[:, None] * page_rows + jnp.arange(page_rows, dtype=jnp.int32)[None, :]
    visible = position[None, None, :, :] < lengths[:, None, None, None]
    masked = jnp.where(visible, scores, floor_score)
    local_peak = jnp.max(masked, axis=(2, 3))
    weights = jnp.where(visible, jnp.exp(masked - local_peak[:, :, None, None]), 0.0)
    local_mass = jnp.sum(weights, axis=(2, 3))
    local_sum = jnp.einsum(
        "rhjp,rjphd->rhd",
        weights,
        picked_values.astype(jnp.float32),
        precision=lax.Precision.HIGHEST,
    )
    peak_rows, masses, gathered_sums = (
        lax.all_gather(local_peak[None], "kv", axis=0, tiled=True),
        lax.all_gather(local_mass[None], "kv", axis=0, tiled=True),
        lax.all_gather(local_sum[None], "kv", axis=0, tiled=True),
    )
    all_peak = jnp.max(peak_rows, axis=0)
    factors = jnp.exp(peak_rows - all_peak[None])
    all_mass = jnp.sum(masses * factors, axis=0)
    all_sum = jnp.sum(gathered_sums * factors[..., None], axis=0)
    decode_attn = (all_sum / all_mass[..., None]).reshape(request_count, D).astype(jnp.bfloat16)
    attn_rows = jnp.concatenate([prefill_attn, decode_attn], axis=0)
    hidden_state = residual.astype(jnp.float32) + jnp.dot(
        attn_rows, w_out, preferred_element_type=jnp.float32
    )
    scaled = (hidden_state * norm_gain).astype(jnp.bfloat16)
    square_sum, logit_parts = lax.psum(
        (
            jnp.sum(hidden_state * hidden_state, axis=1),
            jnp.dot(scaled, router, preferred_element_type=jnp.float32),
        ),
        "kv",
    )
    inv_first = lax.rsqrt(square_sum / D + epsilon)
    logits = logit_parts * inv_first[:, None]
    normed = (hidden_state * norm_gain * inv_first[:, None]).astype(jnp.bfloat16)
    row_count = residual.shape[0]
    expert_count = router.shape[1]
    capacity = min(row_count, 2 * row_count * TOP // expert_count)
    matches = routes[:, :, None] == jnp.arange(expert_count, dtype=jnp.int32)[None, None, :]
    chosen = jnp.sum(jnp.where(matches, logits[:, None, :], 0.0), axis=2)
    raised = jnp.exp(chosen)
    gate_weights = raised / jnp.sum(raised, axis=1, keepdims=True)
    one_hot = matches.reshape(row_count * TOP, expert_count).astype(jnp.int32)
    earlier = jnp.cumsum(one_hot, axis=0) - one_hot
    slot_index = jnp.sum(earlier * one_hot, axis=1)
    target = routes.reshape(-1) * capacity + slot_index
    source_row = jnp.arange(row_count * TOP, dtype=jnp.int32) // TOP
    filler = jnp.zeros((expert_count * capacity,), jnp.int32).at[target].set(source_row)
    present = jnp.zeros((expert_count * capacity,), jnp.bool_).at[target].set(True)
    gate_local = w_gate[0]
    up_local = w_up[0]
    down_local = w_down[0]
    full_rows = lax.all_gather(normed, "kv", axis=1, tiled=True)
    picked = full_rows[filler]
    arrived = lax.all_to_all(
        jnp.where(present[:, None], picked, jnp.zeros_like(picked)).reshape(
            expert_count, capacity, full_rows.shape[1]
        ),
        "ep",
        split_axis=0,
        concat_axis=0,
        tiled=True,
    )
    inbound = arrived.reshape(-1, arrived.shape[2])
    gate_proj = jnp.dot(inbound, gate_local, preferred_element_type=jnp.float32)
    up_proj = jnp.dot(inbound, up_local, preferred_element_type=jnp.float32)
    activation = (jax.nn.silu(gate_proj) * up_proj).astype(jnp.bfloat16)
    feature_cols = residual.shape[1]
    summed = lax.psum_scatter(
        lax.dot_general(
            down_local, activation, (((0,), (1,)), ((), ())), preferred_element_type=jnp.float32
        ).astype(jnp.bfloat16),
        "kv",
        scatter_dimension=0,
        tiled=True,
    ).astype(jnp.float32)
    expert_out = summed.T.astype(jnp.bfloat16).reshape(
        arrived.shape[0], arrived.shape[1], feature_cols
    )
    returned = lax.all_to_all(expert_out, "ep", split_axis=0, concat_axis=0, tiled=True)
    back_rows = (
        returned.reshape(-1, feature_cols)[target]
        .reshape(row_count, TOP, feature_cols)
        .astype(jnp.float32)
    )
    combined = hidden_state + jnp.sum(back_rows * gate_weights[:, :, None], axis=1)
    square_two = lax.psum(jnp.sum(combined * combined, axis=1), "kv")
    return (combined * lax.rsqrt(square_two / D + epsilon)[:, None] * final_gain).astype(
        jnp.bfloat16
    )


def attend(slots_ref, lengths_ref, q_ref, k_ref, v_ref, out_ref, kbuf, vbuf, ksem, vsem):
    requests, pages_each, page_rows = kbuf.shape[:3]
    holder = lax.axis_index("kv")
    holders = lax.axis_size("kv")
    for r in range(requests):
        for j in range(pages_each):
            pltpu.make_async_copy(k_ref.at[slots_ref[r, 0, j]], kbuf.at[r, j], ksem.at[r]).start()
    for r in range(requests):
        for j in range(pages_each):
            pltpu.make_async_copy(v_ref.at[slots_ref[r, 0, j]], vbuf.at[r, j], vsem.at[r]).start()
    tokens = pages_each * page_rows
    wide_row = lax.broadcasted_iota(jnp.int32, (HEAD_DIM, D), 0)
    wide_head = lax.broadcasted_iota(jnp.int32, (HEAD_DIM, D), 1) // HEAD_DIM
    own_head = (wide_row == wide_head)[:HEADS]
    place = lax.broadcasted_iota(jnp.int32, (HEADS, tokens), 1)
    position = ((place // page_rows) * holders + holder) * page_rows + place % page_rows
    queries = q_ref[...].astype(jnp.float32)
    for r in range(requests):
        spread = jnp.where(wide_row == wide_head, queries[r : r + 1, :], 0.0).astype(jnp.bfloat16)
        pltpu.make_async_copy(kbuf.at[r], kbuf.at[r], ksem.at[r]).wait()
        scores = lax.dot_general(
            kbuf[r].reshape(tokens, D),
            spread,
            (((1,), (1,)), ((), ())),
            preferred_element_type=jnp.float32,
        )
        visible = position < lengths_ref[r]
        scores = jnp.where(visible, scores.T[:HEADS] / math.sqrt(HEAD_DIM), floor_score)
        peak = scores.max(axis=1, keepdims=True)
        weight = jnp.where(visible, jnp.exp(scores - peak), 0.0)
        mass = weight.sum(axis=1, keepdims=True)
        high = weight.astype(jnp.bfloat16)
        low = (weight - high.astype(jnp.float32)).astype(jnp.bfloat16)
        pltpu.make_async_copy(vbuf.at[r], vbuf.at[r], vsem.at[r]).wait()
        total = jnp.dot(
            jnp.concatenate([high, low], axis=0),
            vbuf[r].reshape(tokens, D),
            preferred_element_type=jnp.float32,
        )
        both = total[:HEADS] + total[HEADS:]
        for n, part in enumerate((both, peak, mass)):
            row = n * requests + r
            out_ref[row : row + 1, :] = jnp.sum(
                jnp.where(own_head, part, 0.0), axis=0, keepdims=True
            )


def local_attention(queries, key_pool, value_pool, page_table, lengths):
    requests, _, pages_each = page_table.shape
    held = (requests, pages_each) + key_pool.shape[1:]
    smem = pl.BlockSpec(memory_space=pltpu.SMEM)
    vmem = pl.BlockSpec(memory_space=pltpu.VMEM)
    hbm = pl.BlockSpec(memory_space=pl.ANY)
    return pl.pallas_call(
        attend,
        out_shape=jax.ShapeDtypeStruct((3 * requests, D), jnp.float32),
        in_specs=[smem, smem, vmem, hbm, hbm],
        out_specs=vmem,
        scratch_shapes=[
            pltpu.VMEM(held, jnp.bfloat16),
            pltpu.VMEM(held, jnp.bfloat16),
            pltpu.SemaphoreType.DMA((requests,)),
            pltpu.SemaphoreType.DMA((requests,)),
        ],
        compiler_params=pltpu.CompilerParams(vmem_limit_bytes=60 * 2**20),
        cost_estimate=pl.CostEstimate(flops=4 * 10**8, bytes_accessed=7 * 2**20, transcendentals=0),
        name="local_attention",
    )(page_table, lengths, queries, key_pool, value_pool)


LABELS = ((0, 0), (0, 1), (1, 0), (1, 1))


def where_held(a, b, path):
    if a == b:
        return a, a
    if a == 1:
        return path, 1 - path
    return 1 - path, path


def expert_kernel(by_slot, side_ref, gate_ref, up_ref, down_ref, *rest):
    blocks = rest[:4]
    outs = rest[4:8]
    xbuf, obuf, gbuf, ubuf, dbuf, wsem, xsem, osem = rest[8:]
    holder, core = lax.axis_index("kv"), lax.axis_index("ep") % 2
    pair = blocks[0].shape[1]
    cols = xbuf.shape[4]
    rows = 2 * pair * xbuf.shape[3]
    halves = (holder, 1 - holder)
    paths = (core, 1 - core)

    def fetch(d, labels):
        for a, b in labels:
            t, f = where_held(a, b, paths[d])
            pltpu.make_async_copy(
                blocks[2 * d + b].at[a], xbuf.at[d, f, pl.ds(t * pair, pair)], xsem.at[d, f]
            ).start()

    def load(source, buffer, kind, f):
        pltpu.make_async_copy(source.at[halves[f]], buffer.at[f], wsem.at[kind, f]).start()

    fetch(0, LABELS)
    load(gate_ref, gbuf, 0, 0)
    load(gate_ref, gbuf, 0, 1)
    load(up_ref, ubuf, 1, 0)
    load(up_ref, ubuf, 1, 1)
    for f in range(2):
        start = pl.multiple_of(halves[f] * cols, cols)
        pltpu.make_async_copy(
            down_ref.at[:, pl.ds(start, cols)], dbuf.at[f], wsem.at[2, f]
        ).start()
    fetch(1, LABELS)

    def ready(d, buffer, kind, f):
        if d == 0:
            pltpu.make_async_copy(buffer.at[f], buffer.at[f], wsem.at[kind, f]).wait()

    def came(d, f):
        pltpu.make_async_copy(xbuf.at[d, f], xbuf.at[d, f], xsem.at[d, f]).wait()

    side = side_ref[...].T
    for d in range(2):
        came(d, 0)
        first = xbuf[d, 0].reshape(rows, cols)
        ready(d, gbuf, 0, 0)
        gate = jnp.dot(first, gbuf[0], preferred_element_type=jnp.float32)
        came(d, 1)
        second = xbuf[d, 1].reshape(rows, cols)
        ready(d, gbuf, 0, 1)
        gate += jnp.dot(second, gbuf[1], preferred_element_type=jnp.float32)
        groups = [4 * i + 2 * t + d for t in range(2) for i in range(pair)]
        scale = jnp.concatenate([side[:, g : g + 1] for g in groups])
        share = jnp.concatenate([side[:, 4 * pair + g : 4 * pair + g + 1] for g in groups])
        gate *= scale
        ready(d, ubuf, 1, 0)
        up = jnp.dot(first, ubuf[0], preferred_element_type=jnp.float32)
        ready(d, ubuf, 1, 1)
        up += jnp.dot(second, ubuf[1], preferred_element_type=jnp.float32)
        up *= scale
        act = (gate / (1.0 + jnp.exp(-gate)) * up).astype(jnp.bfloat16)
        for f in range(2):
            ready(d, dbuf, 2, f)
            out = jnp.dot(act, dbuf[f], preferred_element_type=jnp.float32) * share
            obuf[d, f] = out.astype(jnp.bfloat16).reshape(2 * pair, -1, cols)
        for n, (a, b) in enumerate(LABELS):
            t, f = where_held(a, b, paths[d])
            out = outs[2 * d + b].at[:, a] if by_slot else outs[2 * d + b].at[a]
            pltpu.make_async_copy(
                obuf.at[d, f, pl.ds(t * pair, pair)], out, osem.at[4 * d + n]
            ).start()
    for n in range(8):
        pltpu.make_async_copy(
            obuf.at[0, 0, pl.ds(0, pair)], obuf.at[0, 0, pl.ds(0, pair)], osem.at[n]
        ).wait()


def run_experts(by_slot, side, gate, up, down, blocks):
    _, pair, row_count, cols = blocks[0].shape
    hidden = gate.shape[2]
    vmem = pl.BlockSpec(memory_space=pltpu.VMEM)
    hbm = pl.BlockSpec(memory_space=pl.ANY)
    shape = (pair, 2, row_count, cols) if by_slot else (2, pair, row_count, cols)

    def body(*refs):
        expert_kernel(by_slot, *refs)

    return pl.pallas_call(
        body,
        out_shape=[jax.ShapeDtypeStruct(shape, jnp.bfloat16)] * 4,
        in_specs=[vmem, hbm, hbm, hbm] + [hbm] * 4,
        out_specs=[hbm] * 4,
        scratch_shapes=[
            pltpu.VMEM((2, 2, 2 * pair, row_count, cols), jnp.bfloat16),
            pltpu.VMEM((2, 2, 2 * pair, row_count, cols), jnp.bfloat16),
            pltpu.VMEM((2, cols, hidden), jnp.bfloat16),
            pltpu.VMEM((2, cols, hidden), jnp.bfloat16),
            pltpu.VMEM((2, hidden, cols), jnp.bfloat16),
            pltpu.SemaphoreType.DMA((3, 2)),
            pltpu.SemaphoreType.DMA((2, 2)),
            pltpu.SemaphoreType.DMA((8,)),
        ],
        compiler_params=pltpu.CompilerParams(vmem_limit_bytes=44 * 2**20),
        cost_estimate=pl.CostEstimate(
            flops=4 * pair * row_count * 12 * cols * hidden,
            bytes_accessed=pair * row_count * cols * 32 + 12 * cols * hidden,
            transcendentals=0,
        ),
        name="experts",
    )(side, gate, up, down, *blocks)


def add(*parts):
    total = parts[0].astype(jnp.float32)
    for part in parts[1:]:
        total = total + part.astype(jnp.float32)
    return total.astype(jnp.bfloat16)


def dense(
    queries,
    key_pool,
    value_pool,
    page_table,
    lengths,
    prefill_attn,
    residual,
    w_out,
    norm_gain,
    router,
    w_gate,
    w_up,
    w_down,
    final_gain,
    routes,
):
    request_count = queries.shape[0]
    row_count, cols = residual.shape
    expert_count = router.shape[1]
    ep_size = lax.axis_size("ep")
    depth = ep_size // 4
    axes = ("ep", "kv")

    def number(z, y, c, x):
        return ((z * 2 + y) * 2 + c) * 2 + x

    places = [(z, y, c, x) for z in range(depth) for y in range(2) for c in range(2) for x in range(2)]

    def sent(array, target):
        return lax.ppermute(array, axes, [(number(*p), number(*target(*p))) for p in places])

    def across(array):
        return sent(array, lambda z, y, c, x: (z, y, c, 1 - x))

    def along(array, s):
        return sent(array, lambda z, y, c, x: ((z + s) % depth, y, c, x))

    def hop_one(array):
        return sent(array, lambda z, y, c, x: (z, y, c, 1 - x) if c == 0 else (z, 1 - y, c, x))

    def hop_two(array):
        return sent(array, lambda z, y, c, x: (z, 1 - y, c, x) if c == 0 else (z, y, c, 1 - x))

    def sibling(array):
        return sent(array, lambda z, y, c, x: (z, y, 1 - c, x))

    def fence(*values):
        return lax.optimization_barrier(values)

    early = (row_count - request_count) // 16 * 16

    def hidden_of(rows, part):
        product = jnp.dot(rows, w_out, preferred_element_type=jnp.float32)
        state = residual[part].astype(jnp.float32) + product
        return state, (state * norm_gain).astype(jnp.bfloat16)

    first_hidden, first_scaled = hidden_of(prefill_attn[:early], slice(0, early))
    first_one = along(first_scaled, 1)
    local = local_attention(queries, key_pool, value_pool, page_table, lengths)
    first_one, local, first_scaled = fence(first_one, local, first_scaled)

    first_two = along(first_one, 1)
    other = across(local)
    sum_one, sum_two = local[:request_count], other[:request_count]
    peak_one, peak_two = (v[request_count : 2 * request_count] for v in (local, other))
    mass_one, mass_two = (v[2 * request_count :] for v in (local, other))
    peak = jnp.maximum(peak_one, peak_two)
    factor_one, factor_two = jnp.exp(peak_one - peak), jnp.exp(peak_two - peak)
    decode_attn = (sum_one * factor_one + sum_two * factor_two) / (
        mass_one * factor_one + mass_two * factor_two
    )
    last_rows = jnp.concatenate([prefill_attn[early:], decode_attn.astype(jnp.bfloat16)], axis=0)
    last_hidden, last_scaled = hidden_of(last_rows, slice(early, row_count))
    first_two, last_scaled, last_hidden = fence(first_two, last_scaled, last_hidden)

    hidden_state = jnp.concatenate([first_hidden, last_hidden], axis=0)
    scaled = jnp.concatenate([first_scaled, last_scaled], axis=0)
    square_part = jnp.sum(hidden_state * hidden_state, axis=1)
    logit_part = jnp.dot(scaled, router, preferred_element_type=jnp.float32)
    stats = jnp.concatenate([logit_part, square_part[:, None]], axis=1).T

    slots = ((1, 2), (3, 0))
    last_one, last_two = along(last_scaled, 1), along(last_scaled, 2)
    stats = stats + across(stats)
    own_one = hop_one(scaled)
    last_one, last_two, stats, scaled, own_one = fence(last_one, last_two, stats, scaled, own_one)

    pair = jnp.stack(
        [
            jnp.concatenate([first_one, last_one], axis=0),
            jnp.concatenate([first_two, last_two], axis=0),
        ]
    )
    far_three, one, far_first = along(scaled, 3), hop_one(pair), hop_two(pair)
    inv_first = lax.rsqrt(stats[expert_count] / D + epsilon)
    logits = stats[:expert_count].T * inv_first[:, None]
    matches = routes[:, :, None] == jnp.arange(expert_count, dtype=jnp.int32)[None, None, :]
    chosen = jnp.sum(jnp.where(matches, logits[:, None, :], 0.0), axis=2)
    raised = jnp.exp(chosen)
    gate_weights = raised / jnp.sum(raised, axis=1, keepdims=True)
    by_expert = jnp.sum(jnp.where(matches, gate_weights[:, :, None], 0.0), axis=1)
    side = jnp.concatenate([by_expert, inv_first[:, None]], axis=1).T[None]
    side_s = sibling(side)
    side_y = sent(side, lambda z, y, c, x: (z, 1 - y, c, x))
    side_ys = sent(side, lambda z, y, c, x: (z, 1 - y, 1 - c, x))
    far_three, one, pair, scaled, side, side_s, side_y, side_ys = fence(
        far_three, one, pair, scaled, side, side_s, side_y, side_ys
    )

    own = lax.axis_index("ep")
    near = jnp.stack([pair, one])
    far_last, near_s, far_one = hop_two(one), sibling(near), hop_one(far_three)
    far_first_s = sibling(far_first)
    later_near = jnp.stack([jnp.stack([far_three, scaled]), jnp.stack([far_one, own_one])])
    side = jnp.concatenate([side, side_s, side_y, side_ys], axis=0)
    crossed = sent(side, lambda z, y, c, x: (z ^ 1, y, c, x))
    swapped = sent(jnp.stack([side, crossed]), lambda z, y, c, x: (z ^ 2, y, c, x))
    far_first, far_first_s, far_last, near_s, later_near, side, crossed, swapped = fence(
        far_first, far_first_s, far_last, near_s, later_near, side, crossed, swapped
    )
    far = jnp.stack([far_first, far_last])

    odd = (own // 4) % 2 == 1
    before, after = jnp.where(odd, crossed, swapped[1]), jnp.where(odd, swapped[1], crossed)
    held = jnp.stack([side, before, swapped[0], after])
    share = lax.dynamic_index_in_dim(held, own, axis=2, keepdims=False)
    held = jnp.stack([held[:, :, expert_count], share]).reshape(2, depth, 2, 2, row_count)
    both = [jnp.stack([held[:, s] for s in chunk], axis=1).reshape(-1, row_count) for chunk in slots]
    gate_local = w_gate[0].reshape(2, cols, -1)
    up_local = w_up[0].reshape(2, cols, -1)
    down_local = w_down[0]
    far_last_s, later_far, later_near_s = sibling(far_last), hop_two(later_near), sibling(later_near)
    far_s = jnp.stack([far_first_s, far_last_s])
    made = run_experts(False, both[0], gate_local, up_local, down_local, (near, far, near_s, far_s))
    later_far, later_near_s, later_near, made = fence(later_far, later_near_s, later_near, made)

    crossing = sibling(made[3])
    crossing = [add(made[1][a], crossing[a]) for a in range(2)]
    later_far_s = sibling(later_far)
    crossing, later_far_s = fence(crossing, later_far_s)

    staying_s = sibling(made[2])
    far_arrived, near_arrived = hop_two(crossing[1]), hop_two(crossing[0])
    blocks = (later_near, later_far, later_near_s, later_far_s)
    remade = run_experts(True, both[1], gate_local, up_local, down_local, blocks)
    staying, staying_s, far_arrived, remade = fence(made[0], staying_s, far_arrived, remade)

    far_sum = add(staying[1], staying_s[1], far_arrived)
    moved = hop_one(far_sum)
    far_sum, near_parts = fence(far_sum, (staying[0], staying_s[0]))
    near_sum = add(*near_parts, near_arrived)
    crossing_s, staying_s = sibling(remade[3]), sibling(remade[2])
    crossing = [add(remade[1][1], crossing_s[1])]
    crossing += [add(remade[1][0, a], crossing_s[0, a]) for a in range(2)]
    staying = [[add(remade[0][i, a], staying_s[i, a]) for a in range(2)] for i in range(2)]
    moved, near_sum, crossing, staying = fence(moved, near_sum, crossing, staying)

    whole = add(near_sum, moved)
    three_far, three_near = hop_two(crossing[2]), hop_two(crossing[1])
    relayed = along(whole[1], depth - 1)
    passed = along(add(whole[0], relayed), depth - 1)
    moved, zero_parts = hop_one(add(staying[0][1], three_far)), hop_two(crossing[0])
    part_three = along(add(staying[0][0], three_near, moved), depth - 3)
    passed, zero_parts = fence(passed, zero_parts)
    combined = hidden_state + passed.astype(jnp.float32)
    moved = hop_one(add(staying[1][1], zero_parts[1]))
    for part in (staying[1][0], zero_parts[0], moved, part_three):
        combined = combined + part.astype(jnp.float32)
    square_two = jnp.sum(combined * combined, axis=1)[None, :]
    square_two = (square_two + across(square_two))[0]
    return (combined * lax.rsqrt(square_two / D + epsilon)[:, None] * final_gain).astype(
        jnp.bfloat16
    )


def per_device(*arrays):
    row_count, expert_count = arrays[6].shape[0], arrays[9].shape[1]
    capacity = min(row_count, 2 * row_count * TOP // expert_count)
    fits = lax.axis_size("kv") == 2 and lax.axis_size("ep") == 16
    if capacity == row_count and fits:
        return dense(*arrays)
    return routed(*arrays)


def solution(mesh):
    placed = (
        P("ep", None),
        P(("ep", "kv"), None, None),
        P(("ep", "kv"), None, None),
        P("ep", "kv", None),
        P("ep"),
        P("ep", None),
        P("ep", "kv"),
        P(None, "kv"),
        P("kv"),
        P("kv", None),
        P("ep", None, "kv"),
        P("ep", None, "kv"),
        P("ep", "kv", None),
        P("kv"),
        P("ep", None),
    )
    return jax.shard_map(
        per_device, mesh=mesh, in_specs=placed, out_specs=P("ep", "kv"), check_vma=False
    )
```
